32 devices in a mesh: seq: 8 (over y, x, core), shard: 4 (over z).
Axes of the slice: x: 2, y: 2, z: 4, core: 2. Of those that a mesh axis runs over, the one named last changes fastest.
Arguments:
- hidden_in: bfloat16 [8192, 2048], P('seq'), may hold values from -6 to 6
- out_grad: bfloat16 [8192, 2048], P('seq'), may hold values from -6 to 6
- deal: int32 [8192], P('seq'), may hold values from 0 to 8191, as said below
- lengths: int32 [4], replicated, may hold values from 1024 to 4096, as said below
- qkv_weight: float32 [2048, 3, 2048], P('seq', None, 'shard'), may hold values from -0.125 to 0.125
- qkv_first: float32 [2048, 3, 2048], P('seq', None, 'shard'), may hold values from -32 to 32
- qkv_second: float32 [2048, 3, 2048], P('seq', None, 'shard'), may hold values from 54.0672 to 860.16
- beta_weight: float32 [2048, 16], P('seq', 'shard'), may hold values from -0.125 to 0.125
- beta_first: float32 [2048, 16], P('seq', 'shard'), may hold values from -16 to 16
- beta_second: float32 [2048, 16], P('seq', 'shard'), may hold values from 19.6608 to 311.296
- out_weight: float32 [2048, 2048], P('shard', 'seq'), may hold values from -0.125 to 0.125
- out_first: float32 [2048, 2048], P('shard', 'seq'), may hold values from -64 to 64
- out_second: float32 [2048, 2048], P('shard', 'seq'), may hold values from 212.992 to 3440.64
- gate_up_weight: float32 [2048, 2, 5632], P('seq', None, 'shard'), may hold values from -0.125 to 0.125
- gate_up_first: float32 [2048, 2, 5632], P('seq', None, 'shard'), may hold values from -32 to 32
- gate_up_second: float32 [2048, 2, 5632], P('seq', None, 'shard'), may hold values from 54.0672 to 860.16
- down_weight: float32 [5632, 2048], P('shard', 'seq'), may hold values from -0.078125 to 0.078125
- down_first: float32 [5632, 2048], P('shard', 'seq'), may hold values from -24 to 24
- down_second: float32 [5632, 2048], P('shard', 'seq'), may hold values from 34.4064 to 548.864
- conv_weight: float32 [4, 3, 2048], P(None, None, 'shard'), may hold values from -2 to 2
- conv_first: float32 [4, 3, 2048], P(None, None, 'shard'), may hold values from -32 to 32
- conv_second: float32 [4, 3, 2048], P(None, None, 'shard'), may hold values from 54.0672 to 860.16
- gains: float32 [4224], replicated, may hold values from 0.5 to 1.5
- gains_first: float32 [4224], replicated, may hold values from -64 to 64
- gains_second: float32 [4224], replicated, may hold values from 212.992 to 3440.64
Outputs:
- hidden_out: bfloat16 [8192, 2048], P('seq')
- input_grad: bfloat16 [8192, 2048], P('seq')
- new_qkv_weight: float32 [2048, 3, 2048], P('seq', None, 'shard')
- new_qkv_first: float32 [2048, 3, 2048], P('seq', None, 'shard')
- new_qkv_second: float32 [2048, 3, 2048], P('seq', None, 'shard')
- new_beta_weight: float32 [2048, 16], P('seq', 'shard')
- new_beta_first: float32 [2048, 16], P('seq', 'shard')
- new_beta_second: float32 [2048, 16], P('seq', 'shard')
- new_out_weight: float32 [2048, 2048], P('shard', 'seq')
- new_out_first: float32 [2048, 2048], P('shard', 'seq')
- new_out_second: float32 [2048, 2048], P('shard', 'seq')
- new_gate_up_weight: float32 [2048, 2, 5632], P('seq', None, 'shard')
- new_gate_up_first: float32 [2048, 2, 5632], P('seq', None, 'shard')
- new_gate_up_second: float32 [2048, 2, 5632], P('seq', None, 'shard')
- new_down_weight: float32 [5632, 2048], P('shard', 'seq')
- new_down_first: float32 [5632, 2048], P('shard', 'seq')
- new_down_second: float32 [5632, 2048], P('shard', 'seq')
- new_conv_weight: float32 [4, 3, 2048], P(None, None, 'shard')
- new_conv_first: float32 [4, 3, 2048], P(None, None, 'shard')
- new_conv_second: float32 [4, 3, 2048], P(None, None, 'shard')
- new_gains: float32 [4224], replicated
- new_gains_first: float32 [4224], replicated
- new_gains_second: float32 [4224], replicated
The draws below stay inside these ranges and needn't reach their ends.
Inputs may be any that keep to these rules, and one draw needn't show every extreme that they name: Row r of the input stands at place deal[r] of the concatenated sequences; every place is named once, and of the rows that one device holds, the same number land in every device's block of 1024 places. `lengths`: each length is a multiple of 64; they sum to 8192; the largest is exactly 4096.
All inputs are finite; a program needn't handle non-finite values.
Results may differ from the reference program's by a relative error of at most 0.019.
The reference program's roundings to bfloat16 on the way count: a program that leaves them out, or rounds other values in their place, can miss the bound.
Values may be sent and summed in bfloat16 or wider, within the bound.
A program may use at most 320 MiB of HBM per device.

```python
import math
import jax
import jax.numpy as jnp
from jax import lax

D = 2048
HEADS = 16
HEAD = 128
FF = 5632
TAPS = 4
GROUP = 64
TOK_DEV = 1024
MINLEN = 1024
STEP = 10
TOKENS = 8192
LONGEST = 4096
GAINS = 4224


def draw_deal(key, part):
    key = jax.random.fold_in(key, 11)
    device_count = TOKENS // TOK_DEV
    share = TOK_DEV // device_count
    send_key, land_key = jax.random.split(key)

    def shuffled(sub_key):
        return jax.random.permutation(sub_key, TOK_DEV)
    sending = jax.vmap(shuffled)(jax.random.split(send_key, device_count))
    landing = jax.vmap(shuffled)(jax.random.split(land_key, device_count))
    target = sending // share
    within = sending % share
    source = jnp.arange(device_count, dtype=jnp.int32)[:, None]
    landed = landing[target, source * share + within]
    return (target * TOK_DEV + landed).reshape(TOKENS).astype(jnp.int32)


def draw_lengths(key, part):
    key = jax.random.fold_in(key, 7)
    seq_count = TOKENS // (2 * MINLEN)
    total_blocks = TOKENS // GROUP
    longest_blocks = LONGEST // GROUP
    fewest_block_count = MINLEN // GROUP
    remaining_items = seq_count - 1
    spare = total_blocks - longest_blocks - remaining_items * fewest_block_count
    division_quotient = spare // remaining_items
    division_leftover = spare % remaining_items
    extra_random_key, shift_random_key, permute_random_key = jax.random.split(key, 3)
    extra_flags = (jax.random.permutation(extra_random_key, remaining_items) < division_leftover).astype(jnp.int32)
    floor_block_count = fewest_block_count + division_quotient + extra_flags
    pair_count = remaining_items // 2
    first_half = floor_block_count[:pair_count]
    second_half = floor_block_count[pair_count:2 * pair_count]
    room = jnp.minimum(second_half - fewest_block_count, longest_blocks - first_half)
    moved = jax.random.randint(shift_random_key, (pair_count,), 0, room + 1).astype(jnp.int32)
    gathered = jnp.concatenate([jnp.full((1,), longest_blocks, jnp.int32), first_half + moved, second_half - moved, floor_block_count[2 * pair_count:]])
    shuffle_order = jax.random.permutation(permute_random_key, seq_count)
    return (gathered[shuffle_order] * GROUP).astype(jnp.int32)


def steps_of(rng, dims, cuts, least, largest):
    level, own = 1.0, jax.random.fold_in(rng, 6)
    for dim, blocks in cuts:
        draws = jnp.exp(jax.random.uniform(jax.random.fold_in(own, dim), (blocks,), jnp.float32, least / len(cuts), largest / len(cuts)))
        level = level * jnp.repeat(draws, dims[dim] // blocks).reshape([-1 if axis == dim else 1 for axis in range(len(dims))])
    return level


def normal_values(stream_key, shape, deviation, bound, cuts=(), held_as=jnp.bfloat16):
    factor_of = steps_of(stream_key, shape, cuts, -0.22, 0.18) if cuts else 1.0
    values = jax.random.normal(stream_key, shape, jnp.float32) * deviation * factor_of
    return jnp.minimum(jnp.maximum(values, -bound), bound).astype(held_as)


def setup_inputs(seed: int = 0) -> dict:
    seeds = jax.random.split(jax.random.key(seed), 26)
    return {
        "hidden_in": normal_values(seeds[0], (TOKENS, D), 1.0, 6.0, ((0, 8),)),
        "out_grad": normal_values(seeds[1], (TOKENS, D), 1.0, 6.0, ((0, 8),)),
        "deal": draw_deal(jax.random.fold_in(seeds[25], 71), 0),
        "lengths": draw_lengths(jax.random.fold_in(seeds[25], 71), 0),
        "qkv_weight": normal_values(seeds[4], (D, 3, D), D ** -0.5, 0.125, ((0, 8), (2, 4)), jnp.float32),
        "qkv_first": normal_values(seeds[5], (D, 3, D), (0.056 * TOKENS ** 0.5), 32.0, ((0, 8), (2, 4)), jnp.float32),
        "qkv_second": jnp.clip(jnp.exp(math.log(860.16) - 2.7668907 * jax.random.uniform(seeds[6], (D, 3, D), jnp.float32) ** steps_of(seeds[6], (D, 3, D), ((0, 8), (2, 4)), -0.2, 0.2)), 54.0672, 860.16),
        "beta_weight": normal_values(seeds[7], (D, HEADS), D ** -0.5, 0.125, ((0, 8), (1, 4)), jnp.float32),
        "beta_first": normal_values(seeds[8], (D, HEADS), (0.033 * TOKENS ** 0.5), 16.0, ((0, 8), (1, 4)), jnp.float32),
        "beta_second": jnp.clip(jnp.exp(math.log(311.296) - 2.7621173 * jax.random.uniform(seeds[9], (D, HEADS), jnp.float32) ** steps_of(seeds[9], (D, HEADS), ((0, 8), (1, 4)), -0.2, 0.2)), 19.6608, 311.296),
        "out_weight": normal_values(seeds[10], (D, D), D ** -0.5, 0.125, ((0, 4), (1, 8)), jnp.float32),
        "out_first": normal_values(seeds[11], (D, D), (0.111 * TOKENS ** 0.5), 64.0, ((0, 4), (1, 8)), jnp.float32),
        "out_second": jnp.clip(jnp.exp(math.log(3440.64) - 2.7821581 * jax.random.uniform(seeds[12], (D, D), jnp.float32) ** steps_of(seeds[12], (D, D), ((0, 4), (1, 8)), -0.2, 0.2)), 212.992, 3440.64),
        "gate_up_weight": normal_values(seeds[13], (D, 2, FF), D ** -0.5, 0.125, ((0, 8), (2, 4)), jnp.float32),
        "gate_up_first": normal_values(seeds[14], (D, 2, FF), (0.056 * TOKENS ** 0.5), 32.0, ((0, 8), (2, 4)), jnp.float32),
        "gate_up_second": jnp.clip(jnp.exp(math.log(860.16) - 2.7668907 * jax.random.uniform(seeds[15], (D, 2, FF), jnp.float32) ** steps_of(seeds[15], (D, 2, FF), ((0, 8), (2, 4)), -0.2, 0.2)), 54.0672, 860.16),
        "down_weight": normal_values(seeds[16], (FF, D), FF ** -0.5, 0.078125, ((0, 4), (1, 8)), jnp.float32),
        "down_first": normal_values(seeds[17], (FF, D), (0.044 * TOKENS ** 0.5), 24.0, ((0, 4), (1, 8)), jnp.float32),
        "down_second": jnp.clip(jnp.exp(math.log(548.864) - 2.7696082 * jax.random.uniform(seeds[18], (FF, D), jnp.float32) ** steps_of(seeds[18], (FF, D), ((0, 4), (1, 8)), -0.2, 0.2)), 34.4064, 548.864),
        "conv_weight": normal_values(seeds[19], (TAPS, 3, D), 0.5, 2.0, ((2, 4),), jnp.float32),
        "conv_first": normal_values(seeds[20], (TAPS, 3, D), (0.056 * TOKENS ** 0.5), 32.0, ((2, 4),), jnp.float32),
        "conv_second": jnp.clip(jnp.exp(math.log(860.16) - 2.7668907 * jax.random.uniform(seeds[21], (TAPS, 3, D), jnp.float32) ** steps_of(seeds[21], (TAPS, 3, D), ((2, 4),), -0.2, 0.2)), 54.0672, 860.16),
        "gains": jnp.clip(1.0 + 0.1 * jax.random.normal(seeds[22], (GAINS,), jnp.float32), 0.5, 1.5),
        "gains_first": normal_values(seeds[23], (GAINS,), (0.111 * TOKENS ** 0.5), 64.0, (), jnp.float32),
        "gains_second": jnp.clip(jnp.exp(jax.random.uniform(seeds[24], (GAINS,), jnp.float32, math.log(212.992), math.log(3440.64))), 212.992, 3440.64),
    }


EPSILON = 1e-06
PRECISE = lax.Precision.HIGHEST
FIRST_DECAY = 0.9
SECOND_DECAY = 0.95
ADAM_EPSILON = 1e-08
RATE_WIDE = 0.044
RATE_DOWN = 0.027
RATE_CONV = 0.8
RATE_GAIN = 0.3
SHRINK = 0.1

@jax.custom_vjp
def low(v):
    return lax.optimization_barrier(v.astype(jnp.bfloat16)).astype(jnp.float32)

@jax.custom_vjp
def low_back(v):
    return v

def low_keep(v):
    return (low(v), None)

def low_pass(kept, grad):
    return (grad,)

def back_keep(v):
    return (v, None)

def back_low(kept, grad):
    return (low(grad),)
low.defvjp(low_keep, low_pass)
low_back.defvjp(back_keep, back_low)

def matmul(left_side, right_side):
    return jnp.dot(left_side.astype(jnp.float32), right_side.astype(jnp.float32), precision=PRECISE, preferred_element_type=jnp.float32)

def rms_scale(values, gain_vec):
    return values * lax.rsqrt(lax.optimization_barrier(jnp.mean(values * values, axis=-1, keepdims=True)) + EPSILON) * gain_vec

def unit_rows(values):
    return values * lax.rsqrt(lax.optimization_barrier(jnp.sum(values * values, axis=-1, keepdims=True)) + EPSILON)

def conv_taps(extended, weights, offset):
    row_count = offset.shape[0]
    tap_count = weights.shape[0]
    running = jnp.zeros((row_count, weights.shape[1]), jnp.float32)
    for tap_index in range(tap_count):
        valid_rows = (offset >= tap_count - 1 - tap_index).astype(jnp.float32)[:, None]
        running = running + weights[tap_index] * extended[tap_index:tap_index + row_count] * valid_rows
    return running

def mixer_inputs(extended, logits, weights, offset, head_count):
    activated = jax.nn.silu(conv_taps(extended, weights, offset))
    row_count = activated.shape[0]
    inner_width = activated.shape[1] // 3
    queries = unit_rows(activated[:, :inner_width].reshape(row_count, head_count, -1))
    key_rows = unit_rows(activated[:, inner_width:2 * inner_width].reshape(row_count, head_count, -1))
    values = activated[:, 2 * inner_width:].reshape(row_count, head_count, -1)
    return (queries, key_rows, values, jax.nn.sigmoid(logits))

def group_step(state_now, inputs):
    queries, key_rows, values, strength, keep_flag = inputs
    block_len = key_rows.shape[0]
    key_width = key_rows.shape[-1]
    state_start = state_now * keep_flag
    queries = jnp.swapaxes(queries, 0, 1)
    key_rows = jnp.swapaxes(key_rows, 0, 1)
    values = jnp.swapaxes(values, 0, 1)
    strength = jnp.swapaxes(strength, 0, 1)[:, :, None]
    positions = jnp.arange(block_len)
    strict = (positions[:, None] > positions[None, :]).astype(jnp.float32)
    inclusive = (positions[:, None] >= positions[None, :]).astype(jnp.float32)
    intersection = jnp.einsum('hcd,hed->hce', key_rows, key_rows, precision=PRECISE)
    system = jnp.eye(block_len, dtype=jnp.float32) + strict * strength * intersection
    right_side = jnp.concatenate([strength * key_rows, strength * values], axis=-1)
    solved = jax.scipy.linalg.solve_triangular(system, right_side, lower=True, unit_diagonal=True)
    write_rows = solved[..., :key_width]
    fresh_values = solved[..., key_width:] - jnp.einsum('hcd,hde->hce', write_rows, state_start, precision=PRECISE)
    scores = inclusive * jnp.einsum('hcd,hed->hce', queries, key_rows, precision=PRECISE)
    outputs = jnp.einsum('hcd,hde->hce', queries, state_start, precision=PRECISE) + jnp.einsum('hce,hef->hcf', scores, fresh_values, precision=PRECISE)
    outputs = outputs * key_width ** (-0.5)
    state_end = state_start + jnp.einsum('hcd,hce->hde', key_rows, fresh_values, precision=PRECISE)
    return (state_end, jnp.swapaxes(outputs, 0, 1))

def delta_rule(queries, key_rows, values, strength, keep):
    group_count = queries.shape[0] // GROUP

    def to_groups(array):
        return array.reshape((group_count, GROUP) + array.shape[1:])
    state_zero = jnp.zeros((HEADS, HEAD, HEAD), jnp.float32)
    _, outputs = lax.scan(jax.checkpoint(group_step), state_zero, (to_groups(queries), to_groups(key_rows), to_groups(values), to_groups(strength), keep))
    return outputs.reshape(queries.shape)

def layer(hidden, qkv_mat, beta_mat, out_mat, gate_up_mat, down_mat, conv_mat, gain_vec, offset, keep):
    row_count = hidden.shape[0]
    normed_in = low(rms_scale(hidden, gain_vec[:D]))
    projected = low_back(low(matmul(normed_in, low(qkv_mat.reshape(D, 3 * D)))))
    logits = low_back(matmul(normed_in, low(beta_mat)))
    extended = jnp.concatenate([jnp.zeros((TAPS - 1, 3 * D), jnp.float32), projected], axis=0)
    queries, key_rows, values, strength = mixer_inputs(extended, logits, conv_mat.reshape(TAPS, 3 * D), offset, HEADS)
    mixer_out = delta_rule(queries, key_rows, values, strength, keep)
    normed = low(rms_scale(mixer_out, gain_vec[2 * D:]).reshape(row_count, D))
    residual = hidden + low_back(matmul(normed, low(out_mat)))
    normed_ff = low(rms_scale(residual, gain_vec[D:2 * D]))
    gate_up_out = low_back(matmul(normed_ff, low(gate_up_mat.reshape(D, 2 * FF))))
    hidden_units = low(jax.nn.silu(gate_up_out[:, :FF]) * gate_up_out[:, FF:])
    return residual + matmul(hidden_units, low(down_mat))

def adamw(weight, first, second, grad, rate, decay):
    first = FIRST_DECAY * first + (1.0 - FIRST_DECAY) * grad
    second = SECOND_DECAY * second + (1.0 - SECOND_DECAY) * grad * grad
    stepped = first / (1.0 - FIRST_DECAY ** STEP) / (jnp.sqrt(second / (1.0 - SECOND_DECAY ** STEP)) + ADAM_EPSILON)
    return (weight - rate * (stepped + decay * weight), first, second)

def reference(hidden_in, out_grad, deal, lengths, qkv_weight, qkv_first, qkv_second, beta_weight, beta_first, beta_second, out_weight, out_first, out_second, gate_up_weight, gate_up_first, gate_up_second, down_weight, down_first, down_second, conv_weight, conv_first, conv_second, gains, gains_first, gains_second):
    arrival = jnp.argsort(deal).astype(jnp.int32)
    chain_x = hidden_in.astype(jnp.float32)[arrival]
    chain_dy = out_grad.astype(jnp.float32)[arrival]
    places = jnp.arange(TOKENS, dtype=jnp.int32)
    starts = (jnp.cumsum(lengths) - lengths).astype(jnp.int32)
    latest = lax.optimization_barrier(jnp.max(jnp.where(starts[None, :] <= places[:, None], starts[None, :], 0), axis=1)).astype(jnp.int32)
    offset = places - latest
    keep = (offset[::GROUP] > 0).astype(jnp.float32)

    def forward(hidden, qkv_mat, beta_mat, out_mat, gate_up_mat, down_mat, conv_mat, gain_vec):
        return layer(hidden, qkv_mat, beta_mat, out_mat, gate_up_mat, down_mat, conv_mat, gain_vec, offset, keep)
    result, pullback = jax.vjp(forward, chain_x, qkv_weight, beta_weight, out_weight, gate_up_weight, down_weight, conv_weight, gains)
    grads = pullback(chain_dy)
    qkv_new = adamw(qkv_weight, qkv_first, qkv_second, grads[1], RATE_WIDE, SHRINK)
    beta_new = adamw(beta_weight, beta_first, beta_second, grads[2], RATE_WIDE, SHRINK)
    out_new = adamw(out_weight, out_first, out_second, grads[3], RATE_WIDE, SHRINK)
    gate_up_new = adamw(gate_up_weight, gate_up_first, gate_up_second, grads[4], RATE_WIDE, SHRINK)
    down_new = adamw(down_weight, down_first, down_second, grads[5], RATE_DOWN, SHRINK)
    conv_new = adamw(conv_weight, conv_first, conv_second, grads[6], RATE_CONV, 0.0)
    gains_new = adamw(gains, gains_first, gains_second, grads[7], RATE_GAIN, 0.0)
    hidden_out = result[deal].astype(jnp.bfloat16)
    input_grad = grads[0][deal].astype(jnp.bfloat16)
    return (hidden_out, input_grad, qkv_new[0], qkv_new[1], qkv_new[2], beta_new[0], beta_new[1], beta_new[2], out_new[0], out_new[1], out_new[2], gate_up_new[0], gate_up_new[1], gate_up_new[2], down_new[0], down_new[1], down_new[2], conv_new[0], conv_new[1], conv_new[2], gains_new[0], gains_new[1], gains_new[2])
```

```python
import functools

import jax
import jax.numpy as jnp
from jax import lax
from jax.experimental import pallas as pl
from jax.experimental.pallas import tpu as pltpu
from jax.sharding import PartitionSpec as P

HEAD = 128
TAPS = 4
GROUP = 64
STEP = 10


EPSILON = 1e-06
PRECISE = lax.Precision.HIGHEST
FIRST_DECAY = 0.9
SECOND_DECAY = 0.95
ADAM_EPSILON = 1e-08
RATE_WIDE = 0.044
RATE_DOWN = 0.027
RATE_CONV = 0.8
RATE_GAIN = 0.3
SHRINK = 0.1


def halves(value):
    high = value.astype(jnp.bfloat16)
    return high, (value - high.astype(jnp.float32)).astype(jnp.bfloat16)


def mul(left, right, dims=((1,), (0,))):
    def one(a, b):
        return lax.dot_general(a, b, (dims, ((), ())), preferred_element_type=jnp.float32)

    left_high, left_low = halves(left)
    right_high, right_low = halves(right)
    return one(left_high, right_high) + (one(left_high, right_low) + one(left_low, right_high))


def mul_nt(left, right):
    return mul(left, right, ((1,), (1,)))


def grid_indices(size):
    return (
        lax.broadcasted_iota(jnp.int32, (size, size), 0),
        lax.broadcasted_iota(jnp.int32, (size, size), 1),
    )


def unit_lower_inverse(strict_part):
    size = strict_part.shape[0]
    rows, cols = grid_indices(size)
    inverse = (rows == cols).astype(jnp.float32)
    level = 0
    while (1 << level) < size:
        corner = (
            ((rows >> (level + 1)) == (cols >> (level + 1)))
            & (((rows >> level) & 1) == 1)
            & (((cols >> level) & 1) == 0)
        )
        part = jnp.where(corner, strict_part, 0.0)
        if level == 0:
            inverse = inverse - part
        else:
            inverse = inverse - mul(inverse, mul(part, inverse))
        level += 1
    return inverse


def sigmoid(value):
    return 1.0 / (1.0 + jnp.exp(-value))


def unit_scale(act):
    return lax.rsqrt(jnp.sum(act * act, axis=-1, keepdims=True) + EPSILON)


def maps_kernel(
    heads,
    keep_ref,
    pre_ref,
    edge_ref,
    logit_ref,
    taps_ref,
    conv_ref,
    solved_ref,
    square_ref,
    step_ref,
    fresh_ref,
    reach_ref,
    zero_out_ref,
    total_ref,
    history,
    running,
):
    block = pl.program_id(0)
    keep = keep_ref[block]
    scale = HEAD**-0.5

    @pl.when(block == 0)
    def _():
        history[0:8, :] = edge_ref[...] * keep
        rows, cols = grid_indices(HEAD)
        start = jnp.where(rows == cols, 1.0, 0.0)
        for head in range(heads):
            running[head, :, 0:HEAD] = start
            running[head, :, HEAD : 2 * HEAD] = jnp.zeros((HEAD, HEAD), jnp.float32)

    @pl.when(block > 0)
    def _():
        history[0:8, :] = history[GROUP : GROUP + 8, :] * keep

    history[8 : GROUP + 8, :] = pre_ref[...].astype(jnp.float32)

    def conv_of(column):
        cols = slice(column * HEAD, (column + 1) * HEAD)
        total = taps_ref[0:1, cols] * history[5 : 5 + GROUP, cols]
        for tap in range(1, TAPS):
            total = total + taps_ref[tap : tap + 1, cols] * history[5 + tap : 5 + tap + GROUP, cols]
        conv_ref[:, cols] = total
        return total * sigmoid(total)

    rows, cols = grid_indices(GROUP)
    for head in range(heads):
        lanes = slice(head * HEAD, (head + 1) * HEAD)
        query = conv_of(head)
        query = query * unit_scale(query)
        key = conv_of(heads + head)
        key = key * unit_scale(key)
        value = conv_of(2 * heads + head)
        strength = sigmoid(logit_ref[:, head : head + 1])
        overlap = mul_nt(key, key)
        scores = jnp.where(rows >= cols, mul_nt(query, key), 0.0)
        inverse = unit_lower_inverse(jnp.where(rows > cols, strength * overlap, 0.0))
        solved = mul(inverse, jnp.concatenate([strength * key, strength * value], axis=1))
        solved_ref[head] = solved
        square_ref[head, :, 0:GROUP] = inverse
        square_ref[head, :, GROUP : 2 * GROUP] = scores
        mixed = mul(scores, solved)
        reach_ref[:, lanes] = scale * (query - mixed[:, 0:HEAD])
        zero_out_ref[:, lanes] = scale * mixed[:, HEAD:]
        pushed = mul(key.T, solved)
        big_rows, big_cols = grid_indices(HEAD)
        step = jnp.where(big_rows == big_cols, 1.0, 0.0) - pushed[:, 0:HEAD]
        step_ref[head] = step
        fresh_ref[head] = pushed[:, HEAD:]
        moved = mul(step, running[head] * keep)
        running[head, :, 0:HEAD] = moved[:, 0:HEAD]
        running[head, :, HEAD:] = moved[:, HEAD:] + pushed[:, HEAD:]
    total_ref[...] = running[...]


def outputs_kernel(
    heads,
    keep_ref,
    incoming_ref,
    step_ref,
    fresh_ref,
    reach_ref,
    zero_out_ref,
    gain_ref,
    state_ref,
    mixed_ref,
    normed_ref,
    running,
):
    block = pl.program_id(0)
    keep = keep_ref[block]

    @pl.when(block == 0)
    def _():
        running[...] = incoming_ref[...]

    for head in range(heads):
        lanes = slice(head * HEAD, (head + 1) * HEAD)
        state = running[head] * keep
        state_ref[head] = state
        running[head] = mul(step_ref[head], state) + fresh_ref[head]
        mixed = mul(reach_ref[:, lanes], state) + zero_out_ref[:, lanes]
        mixed_ref[:, lanes] = mixed
        inverse_rms = lax.rsqrt(jnp.mean(mixed * mixed, axis=-1, keepdims=True) + EPSILON)
        normed_ref[:, lanes] = (mixed * inverse_rms * gain_ref[...]).astype(jnp.bfloat16)


def tail_kernel(
    heads,
    keep_ref,
    d_normed_ref,
    mixed_ref,
    gain_ref,
    step_ref,
    reach_ref,
    d_mixed_ref,
    d_state_ref,
    d_gain_ref,
    running,
):
    block = pl.num_programs(0) - 1 - pl.program_id(0)
    keep = keep_ref[block]

    @pl.when(pl.program_id(0) == 0)
    def _():
        running[...] = jnp.zeros_like(running)
        d_gain_ref[...] = jnp.zeros_like(d_gain_ref)

    gain_sum = jnp.zeros((1, HEAD), jnp.float32)
    for head in range(heads):
        lanes = slice(head * HEAD, (head + 1) * HEAD)
        mixed = mixed_ref[:, lanes]
        d_normed = d_normed_ref[:, lanes]
        inverse_rms = lax.rsqrt(jnp.mean(mixed * mixed, axis=-1, keepdims=True) + EPSILON)
        unit = mixed * inverse_rms
        gain_sum = gain_sum + jnp.sum(d_normed * unit, axis=0, keepdims=True)
        d_unit = d_normed * gain_ref[...]
        d_mixed = inverse_rms * (d_unit - unit * jnp.mean(d_unit * unit, axis=-1, keepdims=True))
        d_mixed_ref[:, lanes] = d_mixed
        running[head] = keep * (
            mul(step_ref[head].T, running[head]) + mul(reach_ref[:, lanes].T, d_mixed)
        )
    d_gain_ref[...] += gain_sum
    d_state_ref[...] = running[...]


def back_kernel(
    heads,
    keep_ref,
    outgoing_ref,
    pre_ref,
    edge_ref,
    logit_ref,
    taps_ref,
    conv_ref,
    solved_ref,
    square_ref,
    step_ref,
    reach_ref,
    state_ref,
    d_mixed_ref,
    d_pre_ref,
    d_tail_ref,
    d_edge_ref,
    d_logit_ref,
    d_taps_ref,
    d_history,
    edge_history,
    running,
):
    count = pl.num_programs(0)
    block = count - 1 - pl.program_id(0)
    keep = keep_ref[block]
    scale = HEAD**-0.5
    rows, cols = grid_indices(GROUP)

    @pl.when(pl.program_id(0) == 0)
    def _():
        running[...] = outgoing_ref[...]
        d_history[GROUP : GROUP + 8, :] = jnp.zeros((8, d_history.shape[1]), jnp.float32)
        d_taps_ref[...] = jnp.zeros_like(d_taps_ref)

    @pl.when(pl.program_id(0) > 0)
    def _():
        d_history[GROUP : GROUP + 8, :] = d_history[0:8, :] * keep_ref[block + 1]

    def act_of(column):
        conv = conv_ref[:, column * HEAD : (column + 1) * HEAD]
        gate = sigmoid(conv)
        return conv * gate, gate * (1.0 + conv * (1.0 - gate))

    def d_unit(unit, inverse_norm, grad):
        return inverse_norm * (grad - unit * jnp.sum(unit * grad, axis=-1, keepdims=True))

    for head in range(heads):
        lanes = slice(head * HEAD, (head + 1) * HEAD)
        query, query_slope = act_of(head)
        query_scale = unit_scale(query)
        query = query * query_scale
        key, key_slope = act_of(heads + head)
        key_scale = unit_scale(key)
        key = key * key_scale
        value, value_slope = act_of(2 * heads + head)
        strength = sigmoid(logit_ref[:, head : head + 1])
        solved = solved_ref[head]
        inverse = square_ref[head, :, 0:GROUP]
        scores = square_ref[head, :, GROUP : 2 * GROUP]
        state = state_ref[head]
        d_state = running[head]
        d_mixed = d_mixed_ref[:, lanes]
        d_out = scale * d_mixed
        running[head] = keep * (
            mul(step_ref[head].T, d_state) + mul(reach_ref[:, lanes].T, d_mixed)
        )
        overlap = mul_nt(key, key)
        fresh = solved[:, HEAD:] - mul(solved[:, 0:HEAD], state)
        d_fresh = mul(scores.T, d_out) + mul(key, d_state)
        d_scores = jnp.where(rows >= cols, mul_nt(d_out, fresh), 0.0)
        d_query = mul_nt(d_out, state) + mul(d_scores, key)
        d_key = mul(d_scores.T, query) + mul_nt(fresh, d_state)
        d_solved = jnp.concatenate([-mul_nt(d_fresh, state), d_fresh], axis=1)
        d_right = mul(inverse.T, d_solved)
        d_strict = jnp.where(rows > cols, -mul_nt(d_right, solved), 0.0)
        d_overlap = strength * d_strict
        d_key = (
            d_key + strength * d_right[:, 0:HEAD] + mul(d_overlap + d_overlap.T, key)
        )
        d_value = strength * d_right[:, HEAD:]
        d_strength = (
            jnp.sum(d_right[:, 0:HEAD] * key, axis=-1, keepdims=True)
            + jnp.sum(d_right[:, HEAD:] * value, axis=-1, keepdims=True)
            + jnp.sum(d_strict * overlap, axis=-1, keepdims=True)
        )
        d_logit_ref[:, head : head + 1] = d_strength * strength * (1.0 - strength)
        for column, d_conv in (
            (head, d_unit(query, query_scale, d_query) * query_slope),
            (heads + head, d_unit(key, key_scale, d_key) * key_slope),
            (2 * heads + head, d_value * value_slope),
        ):
            d_history[0:GROUP, column * HEAD : (column + 1) * HEAD] = d_conv

    for column in range(3 * heads):
        lanes = slice(column * HEAD, (column + 1) * HEAD)
        pre = pre_ref[:, lanes].astype(jnp.float32)
        total = jnp.zeros((GROUP, HEAD), jnp.float32)
        for tap in range(TAPS):
            part = d_history[TAPS - 1 - tap : TAPS - 1 - tap + GROUP, lanes]
            total = total + taps_ref[tap : tap + 1, lanes] * part
            d_taps_ref[tap : tap + 1, lanes] += jnp.sum(pre * part, axis=0, keepdims=True)
        d_pre_ref[:, lanes] = total.astype(jnp.bfloat16)

        @pl.when(block == count - 1)
        def _(total=total, lanes=lanes):
            d_tail_ref[:, lanes] = total[GROUP - 8 :, :]

    @pl.when(block == 0)
    def _():
        edge_history[0:8, :] = jnp.zeros((8, edge_history.shape[1]), jnp.float32)
        edge_history[8:16, :] = d_history[0:8, :] * keep
        total = jnp.zeros(d_edge_ref.shape, jnp.float32)
        for tap in range(TAPS):
            part = edge_history[TAPS - 1 - tap : TAPS - 1 - tap + 8, :]
            total = total + taps_ref[tap : tap + 1, :] * part
            d_taps_ref[tap : tap + 1, :] += jnp.sum(edge_ref[...] * part, axis=0, keepdims=True)
        d_edge_ref[...] = total


def passed_along(value, axis, by):
    count = lax.axis_size(axis)
    pairs = [(i, i + by) for i in range(count) if 0 <= i + by < count]
    return lax.ppermute(value, axis, pairs)


def adamw(weight, first, second, grad, rate, decay):
    first = FIRST_DECAY * first + (1.0 - FIRST_DECAY) * grad
    second = SECOND_DECAY * second + (1.0 - SECOND_DECAY) * grad * grad
    stepped = (
        first
        / (1.0 - FIRST_DECAY**STEP)
        / (jnp.sqrt(second / (1.0 - SECOND_DECAY**STEP)) + ADAM_EPSILON)
    )
    return (weight - rate * (stepped + decay * weight), first, second)


def f32(*shape):
    return jax.ShapeDtypeStruct(shape, jnp.float32)


def bf16(*shape):
    return jax.ShapeDtypeStruct(shape, jnp.bfloat16)


class Rule:
    def __init__(self, keep, heads, row_count):
        self.keep, self.heads, self.rows = keep, heads, row_count
        self.count = row_count // GROUP
        self.params = pltpu.CompilerParams(
            dimension_semantics=("arbitrary",), vmem_limit_bytes=48 * 1024 * 1024
        )

    def rows_spec(self, width, back=False):
        last = self.count - 1
        if back:
            return pl.BlockSpec((GROUP, width), lambda n: (last - n, 0))
        return pl.BlockSpec((GROUP, width), lambda n: (n, 0))

    def block_spec(self, shape, back=False):
        last = self.count - 1
        if back:
            return pl.BlockSpec((None,) + shape, lambda n: (last - n, 0, 0, 0))
        return pl.BlockSpec((None,) + shape, lambda n: (n, 0, 0, 0))

    def whole(self, *shape):
        return pl.BlockSpec(shape, lambda n: (0,) * len(shape))

    def smem(self):
        return pl.BlockSpec(memory_space=pltpu.SMEM)

    def maps(self, pre, edge, logits, taps):
        heads, rows, count, inner = self.heads, self.rows, self.count, self.heads * HEAD
        return pl.pallas_call(
            functools.partial(maps_kernel, heads),
            grid=(count,),
            in_specs=[
                self.smem(),
                self.rows_spec(3 * inner),
                self.whole(8, 3 * inner),
                self.rows_spec(heads),
                self.whole(TAPS, 3 * inner),
            ],
            out_specs=[
                self.rows_spec(3 * inner),
                self.block_spec((heads, GROUP, 2 * HEAD)),
                self.block_spec((heads, GROUP, 2 * GROUP)),
                self.block_spec((heads, HEAD, HEAD)),
                self.block_spec((heads, HEAD, HEAD)),
                self.rows_spec(inner),
                self.rows_spec(inner),
                self.whole(heads, HEAD, 2 * HEAD),
            ],
            out_shape=[
                f32(rows, 3 * inner),
                f32(count, heads, GROUP, 2 * HEAD),
                f32(count, heads, GROUP, 2 * GROUP),
                f32(count, heads, HEAD, HEAD),
                f32(count, heads, HEAD, HEAD),
                f32(rows, inner),
                f32(rows, inner),
                f32(heads, HEAD, 2 * HEAD),
            ],
            scratch_shapes=[
                pltpu.VMEM((GROUP + 8, 3 * inner), jnp.float32),
                pltpu.VMEM((heads, HEAD, 2 * HEAD), jnp.float32),
            ],
            compiler_params=self.params,
            name="delta_maps",
        )(self.keep, pre, edge, logits, taps)

    def outputs(self, incoming, step, fresh, reach, zero_out, gain):
        heads, rows, count, inner = self.heads, self.rows, self.count, self.heads * HEAD
        return pl.pallas_call(
            functools.partial(outputs_kernel, heads),
            grid=(count,),
            in_specs=[
                self.smem(),
                self.whole(heads, HEAD, HEAD),
                self.block_spec((heads, HEAD, HEAD)),
                self.block_spec((heads, HEAD, HEAD)),
                self.rows_spec(inner),
                self.rows_spec(inner),
                self.whole(1, HEAD),
            ],
            out_specs=[
                self.block_spec((heads, HEAD, HEAD)),
                self.rows_spec(inner),
                self.rows_spec(inner),
            ],
            out_shape=[f32(count, heads, HEAD, HEAD), f32(rows, inner), bf16(rows, inner)],
            scratch_shapes=[pltpu.VMEM((heads, HEAD, HEAD), jnp.float32)],
            compiler_params=self.params,
            name="delta_outputs",
        )(self.keep, incoming, step, fresh, reach, zero_out, gain)

    def tail(self, d_normed, mixed, gain, step, reach):
        heads, rows, count, inner = self.heads, self.rows, self.count, self.heads * HEAD
        return pl.pallas_call(
            functools.partial(tail_kernel, heads),
            grid=(count,),
            in_specs=[
                self.smem(),
                self.rows_spec(inner, True),
                self.rows_spec(inner, True),
                self.whole(1, HEAD),
                self.block_spec((heads, HEAD, HEAD), True),
                self.rows_spec(inner, True),
            ],
            out_specs=[
                self.rows_spec(inner, True),
                self.whole(heads, HEAD, HEAD),
                self.whole(1, HEAD),
            ],
            out_shape=[f32(rows, inner), f32(heads, HEAD, HEAD), f32(1, HEAD)],
            scratch_shapes=[pltpu.VMEM((heads, HEAD, HEAD), jnp.float32)],
            compiler_params=self.params,
            name="delta_tail",
        )(self.keep, d_normed, mixed, gain, step, reach)

    def back(self, outgoing, pre, edge, logits, taps, conv, solved, square, step, reach, state, d_mixed):
        heads, rows, count, inner = self.heads, self.rows, self.count, self.heads * HEAD
        return pl.pallas_call(
            functools.partial(back_kernel, heads),
            grid=(count,),
            in_specs=[
                self.smem(),
                self.whole(heads, HEAD, HEAD),
                self.rows_spec(3 * inner, True),
                self.whole(8, 3 * inner),
                self.rows_spec(heads, True),
                self.whole(TAPS, 3 * inner),
                self.rows_spec(3 * inner, True),
                self.block_spec((heads, GROUP, 2 * HEAD), True),
                self.block_spec((heads, GROUP, 2 * GROUP), True),
                self.block_spec((heads, HEAD, HEAD), True),
                self.rows_spec(inner, True),
                self.block_spec((heads, HEAD, HEAD), True),
                self.rows_spec(inner, True),
            ],
            out_specs=[
                self.rows_spec(3 * inner, True),
                self.whole(8, 3 * inner),
                self.whole(8, 3 * inner),
                self.rows_spec(heads, True),
                self.whole(TAPS, 3 * inner),
            ],
            out_shape=[
                bf16(rows, 3 * inner),
                f32(8, 3 * inner),
                f32(8, 3 * inner),
                f32(rows, heads),
                f32(TAPS, 3 * inner),
            ],
            scratch_shapes=[
                pltpu.VMEM((GROUP + 8, 3 * inner), jnp.float32),
                pltpu.VMEM((16, 3 * inner), jnp.float32),
                pltpu.VMEM((heads, HEAD, HEAD), jnp.float32),
            ],
            compiler_params=self.params,
            name="delta_back",
        )(
            self.keep, outgoing, pre, edge, logits, taps, conv, solved, square, step, reach, state,
            d_mixed,
        )


def rms_unit(values):
    return values * lax.rsqrt(jnp.mean(values * values, axis=-1, keepdims=True) + EPSILON)


def rms_back(values, gain_vec, grad):
    inverse_rms = lax.rsqrt(jnp.mean(values * values, axis=-1, keepdims=True) + EPSILON)
    unit = values * inverse_rms
    d_unit = grad * gain_vec
    d_values = inverse_rms * (d_unit - unit * jnp.mean(d_unit * unit, axis=-1, keepdims=True))
    return d_values, jnp.sum(grad * unit, axis=0)


def low(values):
    return values.astype(jnp.bfloat16)


def product(left, right, dims=((1,), (0,))):
    return lax.dot_general(left, right, (dims, ((), ())), preferred_element_type=jnp.float32)


def rows_summed(partial):
    return lax.psum_scatter(low(partial), "shard", scatter_dimension=0, tiled=True)


def rows_joined(rows):
    return lax.all_gather(rows, "shard", axis=0, tiled=True)


def per_device(
    hidden_in,
    out_grad,
    deal,
    lengths,
    qkv_weight,
    qkv_first,
    qkv_second,
    beta_weight,
    beta_first,
    beta_second,
    out_weight,
    out_first,
    out_second,
    gate_up_weight,
    gate_up_first,
    gate_up_second,
    down_weight,
    down_first,
    down_second,
    conv_weight,
    conv_first,
    conv_second,
    gains,
    gains_first,
    gains_second,
):
    row_count, model_width = hidden_in.shape
    heads = beta_weight.shape[1]
    inner = qkv_weight.shape[2]
    units = down_weight.shape[0]
    longest = {4: 4096, 16: 8192}[lengths.shape[0]]
    hops = min(lax.axis_size("seq") - 1, -(-longest // row_count))
    target = deal // row_count
    order = jnp.argsort(target, stable=True)
    got_x, got_dy, got_place = (
        lax.all_to_all(hidden_in[order], "seq", split_axis=0, concat_axis=0, tiled=True),
        lax.all_to_all(out_grad[order], "seq", split_axis=0, concat_axis=0, tiled=True),
        lax.all_to_all(deal[order] % row_count, "seq", split_axis=0, concat_axis=0, tiled=True),
    )
    arranged = jnp.argsort(got_place)
    chain_x = got_x[arranged].astype(jnp.float32)
    chain_dy = got_dy[arranged]
    first_place = lax.axis_index("seq") * row_count
    places = first_place + jnp.arange(0, row_count, GROUP, dtype=jnp.int32)
    starts = jnp.cumsum(lengths) - lengths
    keep = jnp.all(starts[None, :] != places[:, None], axis=1).astype(jnp.float32)
    quarter = row_count // lax.axis_size("shard")
    first_row = lax.axis_index("shard") * quarter

    def own_rows(values):
        return lax.dynamic_slice_in_dim(values, first_row, quarter, 0)

    qkv_mat = lax.all_gather(low(qkv_weight).reshape(-1, 3 * inner), "seq", axis=0, tiled=True)
    beta_mat = lax.all_gather(low(beta_weight), "seq", axis=0, tiled=True)
    gate_up_mat = lax.all_gather(
        low(gate_up_weight).reshape(-1, 2 * units), "seq", axis=0, tiled=True
    )
    out_mat = lax.all_gather(low(out_weight), "seq", axis=1, tiled=True)
    down_mat = lax.all_gather(low(down_weight), "seq", axis=1, tiled=True)
    gain_in = gains[:model_width]
    gain_ff = gains[model_width : 2 * model_width]
    gain_out = gains[2 * model_width :].reshape(1, HEAD)
    conv_mat = conv_weight.reshape(TAPS, 3 * inner)

    normed_in = low(rms_unit(chain_x) * gain_in)
    projected = low(product(normed_in, qkv_mat))
    logits = product(normed_in, beta_mat)
    edge_rows = passed_along(projected[row_count - 8 :], "seq", 1).astype(jnp.float32)
    edge_rows = edge_rows * (jnp.arange(8) >= 8 - (TAPS - 1)).astype(jnp.float32)[:, None]
    rule = Rule(keep, heads, row_count)
    conv, solved, square, step, fresh, reach, zero_out, total = rule.maps(
        projected, edge_rows, logits, conv_mat
    )
    whole_step, whole_fresh = total[:, :, :HEAD], total[:, :, HEAD:]
    incoming = jnp.zeros((heads, HEAD, HEAD), jnp.float32)
    for hop in range(hops):
        advanced = whole_fresh
        if hop:
            advanced = advanced + jnp.einsum(
                "hde,hef->hdf", whole_step, incoming, precision=PRECISE
            )
        incoming = passed_along(advanced, "seq", 1)
    state, mixed, normed = rule.outputs(incoming, step, fresh, reach, zero_out, gain_out)

    residual = own_rows(chain_x) + rows_summed(product(normed, out_mat)).astype(jnp.float32)
    normed_ff = rows_joined(low(rms_unit(residual) * gain_ff))
    gate_up_out = product(normed_ff, gate_up_mat)
    gate, up = gate_up_out[:, :units], gate_up_out[:, units:]
    opened = jax.nn.sigmoid(gate)
    hidden_units = low(gate * opened * up)
    result = residual + rows_summed(product(hidden_units, down_mat)).astype(jnp.float32)
    result = rows_joined(low(result))

    d_hidden = product(chain_dy, down_mat, ((1,), (1,)))
    d_gate = low(d_hidden * up * (opened * (1.0 + gate * (1.0 - opened))))
    d_up = low(d_hidden * (gate * opened))
    d_gate_up = jnp.concatenate([d_gate, d_up], axis=1)
    d_normed_ff = rows_summed(product(d_gate_up, gate_up_mat, ((1,), (1,)))).astype(jnp.float32)
    d_residual, grad_gain_ff = rms_back(residual, gain_ff, d_normed_ff)
    d_residual = own_rows(chain_dy).astype(jnp.float32) + d_residual
    d_mix = rows_joined(low(d_residual))
    grad_down = product(hidden_units, chain_dy, ((0,), (0,)))
    grad_gate_up = product(normed_ff, d_gate_up, ((0,), (0,)))
    grad_out = product(normed, d_mix, ((0,), (0,)))
    d_normed = product(d_mix, out_mat, ((1,), (1,)))
    d_mixed, d_first_state, grad_gain_out = rule.tail(d_normed, mixed, gain_out, step, reach)
    flipped = jnp.swapaxes(whole_step, 1, 2)
    outgoing = jnp.zeros((heads, HEAD, HEAD), jnp.float32)
    for hop in range(hops):
        advanced = d_first_state
        if hop:
            advanced = advanced + jnp.einsum("hde,hef->hdf", flipped, outgoing, precision=PRECISE)
        outgoing = passed_along(advanced, "seq", -1)
    d_pre, d_tail, d_edge, d_logits, grad_taps = rule.back(
        outgoing, projected, edge_rows, logits, conv_mat, conv, solved, square, step, reach, state,
        d_mixed,
    )
    d_tail = low(d_tail + passed_along(d_edge, "seq", -1))
    d_pre = lax.dynamic_update_slice(d_pre, d_tail, (row_count - 8, 0))
    d_logits = low(d_logits)
    grad_qkv = product(normed_in, d_pre, ((0,), (0,)))
    grad_beta = product(normed_in, d_logits, ((0,), (0,)))
    d_normed_in = rows_summed(
        product(d_pre, qkv_mat, ((1,), (1,))) + product(d_logits, beta_mat, ((1,), (1,)))
    ).astype(jnp.float32)
    d_input, grad_gain_in = rms_back(own_rows(chain_x), gain_in, d_normed_in)
    d_input = rows_joined(low(d_residual + d_input))

    def seq_summed(grad, dim):
        return lax.psum_scatter(low(grad), "seq", scatter_dimension=dim, tiled=True).astype(
            jnp.float32
        )

    red_qkv = seq_summed(grad_qkv, 0).reshape(qkv_weight.shape)
    red_beta = lax.psum_scatter(grad_beta, "seq", scatter_dimension=0, tiled=True)
    red_gate_up = seq_summed(grad_gate_up, 0).reshape(gate_up_weight.shape)
    red_out = seq_summed(grad_out, 1)
    red_down = seq_summed(grad_down, 1)
    grad_gains = jnp.concatenate([grad_gain_in, grad_gain_ff, grad_gain_out.reshape(HEAD)])
    red_gains = lax.psum(grad_gains, ("seq", "shard"))
    red_conv = lax.psum(grad_taps.reshape(conv_weight.shape), "seq")
    qkv_new = adamw(qkv_weight, qkv_first, qkv_second, red_qkv, RATE_WIDE, SHRINK)
    beta_new = adamw(beta_weight, beta_first, beta_second, red_beta, RATE_WIDE, SHRINK)
    out_new = adamw(out_weight, out_first, out_second, red_out, RATE_WIDE, SHRINK)
    gate_up_new = adamw(
        gate_up_weight, gate_up_first, gate_up_second, red_gate_up, RATE_WIDE, SHRINK
    )
    down_new = adamw(down_weight, down_first, down_second, red_down, RATE_DOWN, SHRINK)
    conv_new = adamw(conv_weight, conv_first, conv_second, red_conv, RATE_CONV, 0.0)
    gains_new = adamw(gains, gains_first, gains_second, red_gains, RATE_GAIN, 0.0)
    back_out, back_grad = (
        lax.all_to_all(result[got_place], "seq", split_axis=0, concat_axis=0, tiled=True),
        lax.all_to_all(d_input[got_place], "seq", split_axis=0, concat_axis=0, tiled=True),
    )
    restore = jnp.argsort(order)
    return (
        back_out[restore],
        back_grad[restore],
        *qkv_new,
        *beta_new,
        *out_new,
        *gate_up_new,
        *down_new,
        *conv_new,
        *gains_new,
    )


def solution(mesh):
    return jax.shard_map(
        per_device,
        mesh=mesh,
        in_specs=(
            P("seq", None),
            P("seq", None),
            P("seq"),
            P(),
            P("seq", None, "shard"),
            P("seq", None, "shard"),
            P("seq", None, "shard"),
            P("seq", "shard"),
            P("seq", "shard"),
            P("seq", "shard"),
            P("shard", "seq"),
            P("shard", "seq"),
            P("shard", "seq"),
            P("seq", None, "shard"),
            P("seq", None, "shard"),
            P("seq", None, "shard"),
            P("shard", "seq"),
            P("shard", "seq"),
            P("shard", "seq"),
            P(None, None, "shard"),
            P(None, None, "shard"),
            P(None, None, "shard"),
            P(),
            P(),
            P(),
        ),
        out_specs=(
            P("seq", None),
            P("seq", None),
            P("seq", None, "shard"),
            P("seq", None, "shard"),
            P("seq", None, "shard"),
            P("seq", "shard"),
            P("seq", "shard"),
            P("seq", "shard"),
            P("shard", "seq"),
            P("shard", "seq"),
            P("shard", "seq"),
            P("seq", None, "shard"),
            P("seq", None, "shard"),
            P("seq", None, "shard"),
            P("shard", "seq"),
            P("shard", "seq"),
            P("shard", "seq"),
            P(None, None, "shard"),
            P(None, None, "shard"),
            P(None, None, "shard"),
            P(),
            P(),
            P(),
        ),
        check_vma=False,
    )
```

```python
import functools

import jax
import jax.numpy as jnp
from jax import lax
from jax.experimental import pallas as pl
from jax.experimental.pallas import tpu as pltpu
from jax.sharding import PartitionSpec as P

HEAD = 128
TAPS = 4
GROUP = 64
BUSY_FLOPS = 10_000_000
MAPS_BATCH = 4
CHAIN_BATCH = 4
BACK_BATCH = 2
STEP = 10


EPSILON = 1e-06
PRECISE = lax.Precision.HIGHEST
MESH = pl.DeviceIdType.MESH
FIRST_DECAY = 0.9
SECOND_DECAY = 0.95
ADAM_EPSILON = 1e-08
RATE_WIDE = 0.044
RATE_DOWN = 0.027
RATE_CONV = 0.8
RATE_GAIN = 0.3
SHRINK = 0.1


def halves(value):
    high = value.astype(jnp.bfloat16)
    return high, (value - high.astype(jnp.float32)).astype(jnp.bfloat16)


def mul(left, right, dims=((1,), (0,))):
    def one(a, b):
        return lax.dot_general(a, b, (dims, ((), ())), preferred_element_type=jnp.float32)

    left_high, left_low = halves(left)
    right_high, right_low = halves(right)
    return one(left_high, right_high) + (one(left_high, right_low) + one(left_low, right_high))


def mul_nt(left, right):
    return mul(left, right, ((1,), (1,)))


def grid_indices(size):
    return (
        lax.broadcasted_iota(jnp.int32, (size, size), 0),
        lax.broadcasted_iota(jnp.int32, (size, size), 1),
    )


def unit_lower_inverses(strict_parts):
    size = strict_parts[0].shape[0]
    rows, cols = grid_indices(size)
    inverses = [jnp.where(rows == cols, 1.0, 0.0) for _ in strict_parts]
    level = 0
    while (1 << level) < size:
        corner = (
            ((rows >> (level + 1)) == (cols >> (level + 1)))
            & (((rows >> level) & 1) == 1)
            & (((cols >> level) & 1) == 0)
        )
        parts = [jnp.where(corner, strict, 0.0) for strict in strict_parts]
        if level == 0:
            inverses = [inverse - part for inverse, part in zip(inverses, parts)]
        else:
            inner = [mul(part, inverse) for inverse, part in zip(inverses, parts)]
            outer = [mul(inverse, part) for inverse, part in zip(inverses, inner)]
            inverses = [inverse - part for inverse, part in zip(inverses, outer)]
        level += 1
    return inverses


def sigmoid(value):
    return 1.0 / (1.0 + jnp.exp(-value))


def unit_scale(act):
    return lax.rsqrt(jnp.sum(act * act, axis=-1, keepdims=True) + EPSILON)


def head_lanes(column):
    return slice(column * HEAD, (column + 1) * HEAD)


def maps_kernel(
    heads,
    batch,
    keep_ref,
    pre_ref,
    edge_ref,
    logit_ref,
    taps_ref,
    conv_ref,
    solved_ref,
    square_ref,
    step_ref,
    fresh_ref,
    reach_ref,
    zero_out_ref,
    total_ref,
    history,
    running,
):
    turn = pl.program_id(0)
    scale = HEAD**-0.5
    pairs = [(item, head) for item in range(batch) for head in range(heads)]
    keeps = [keep_ref[turn * batch + item] for item in range(batch)]

    @pl.when(turn == 0)
    def _():
        history[0, 0:8, :] = edge_ref[...] * keeps[0]
        rows, cols = grid_indices(HEAD)
        start = jnp.where(rows == cols, 1.0, 0.0)
        for head in range(heads):
            running[head, :, 0:HEAD] = start
            running[head, :, HEAD : 2 * HEAD] = jnp.zeros((HEAD, HEAD), jnp.float32)

    @pl.when(turn > 0)
    def _():
        history[0, 0:8, :] = history[batch - 1, GROUP : GROUP + 8, :] * keeps[0]

    for item in range(batch):
        history[item, 8 : GROUP + 8, :] = pre_ref[
            item * GROUP : (item + 1) * GROUP, :
        ].astype(jnp.float32)
        if item:
            history[item, 0:8, :] = history[item - 1, GROUP : GROUP + 8, :] * keeps[item]

    def conv_of(item, column):
        cols = head_lanes(column)
        total = taps_ref[0:1, cols] * history[item, 5 : 5 + GROUP, cols]
        for tap in range(1, TAPS):
            shifted = history[item, 5 + tap : 5 + tap + GROUP, cols]
            total = total + taps_ref[tap : tap + 1, cols] * shifted
        conv_ref[item * GROUP : (item + 1) * GROUP, cols] = total
        return total * sigmoid(total)

    rows, cols = grid_indices(GROUP)
    big_rows, big_cols = grid_indices(HEAD)
    keys = [conv_of(item, heads + head) for item, head in pairs]
    keys = [key * unit_scale(key) for key in keys]
    strengths = [
        sigmoid(logit_ref[item * GROUP : (item + 1) * GROUP, head : head + 1])
        for item, head in pairs
    ]
    overlaps = [mul_nt(key, key) for key in keys]
    inverses = unit_lower_inverses(
        [
            jnp.where(rows > cols, strength * overlap, 0.0)
            for strength, overlap in zip(strengths, overlaps)
        ]
    )
    queries = [conv_of(item, head) for item, head in pairs]
    queries = [query * unit_scale(query) for query in queries]
    scores = [
        jnp.where(rows >= cols, mul_nt(query, key), 0.0) for query, key in zip(queries, keys)
    ]
    values = [conv_of(item, 2 * heads + head) for item, head in pairs]
    solved = [
        mul(inverse, jnp.concatenate([strength * key, strength * value], axis=1))
        for inverse, strength, key, value in zip(inverses, strengths, keys, values)
    ]
    pushed = [mul(key.T, part) for key, part in zip(keys, solved)]
    mixed = [mul(score, part) for score, part in zip(scores, solved)]
    steps = [jnp.where(big_rows == big_cols, 1.0, 0.0) - part[:, 0:HEAD] for part in pushed]
    for index, (item, head) in enumerate(pairs):
        here = slice(item * GROUP, (item + 1) * GROUP)
        solved_ref[item, head] = solved[index]
        square_ref[item, head, :, 0:GROUP] = inverses[index]
        square_ref[item, head, :, GROUP : 2 * GROUP] = scores[index]
        reach_ref[here, head_lanes(head)] = scale * (queries[index] - mixed[index][:, 0:HEAD])
        zero_out_ref[here, head_lanes(head)] = scale * mixed[index][:, HEAD:]
        step_ref[item, head] = steps[index]
        fresh_ref[item, head] = pushed[index][:, HEAD:]
    now = [running[head] for head in range(heads)]
    for item in range(batch):
        first = item * heads
        moved = [mul(steps[first + head], now[head] * keeps[item]) for head in range(heads)]
        now = [
            jnp.concatenate(
                [moved[head][:, 0:HEAD], moved[head][:, HEAD:] + pushed[first + head][:, HEAD:]],
                axis=1,
            )
            for head in range(heads)
        ]
    for head in range(heads):
        running[head] = now[head]
    total_ref[...] = running[...]


def outputs_kernel(
    heads,
    batch,
    keep_ref,
    incoming_ref,
    step_ref,
    fresh_ref,
    reach_ref,
    zero_out_ref,
    gain_ref,
    state_ref,
    mixed_ref,
    normed_ref,
    running,
):
    turn = pl.program_id(0)

    @pl.when(turn == 0)
    def _():
        running[...] = incoming_ref[...]

    now = [running[head] for head in range(heads)]
    states = []
    for item in range(batch):
        keep = keep_ref[turn * batch + item]
        now = [state * keep for state in now]
        states.append(now)
        now = [
            mul(step_ref[item, head], now[head]) + fresh_ref[item, head] for head in range(heads)
        ]
    for head in range(heads):
        running[head] = now[head]
    for item in range(batch):
        here = slice(item * GROUP, (item + 1) * GROUP)
        outs = [
            mul(reach_ref[here, head_lanes(head)], states[item][head])
            + zero_out_ref[here, head_lanes(head)]
            for head in range(heads)
        ]
        for head, mixed in enumerate(outs):
            state_ref[item, head] = states[item][head]
            mixed_ref[here, head_lanes(head)] = mixed
            inverse_rms = lax.rsqrt(jnp.mean(mixed * mixed, axis=-1, keepdims=True) + EPSILON)
            normed_ref[here, head_lanes(head)] = (mixed * inverse_rms * gain_ref[...]).astype(
                jnp.bfloat16
            )


def tail_kernel(
    heads,
    batch,
    keep_ref,
    d_normed_ref,
    mixed_ref,
    gain_ref,
    step_ref,
    reach_ref,
    d_mixed_ref,
    d_state_ref,
    d_gain_ref,
    running,
):
    turn = pl.num_programs(0) - 1 - pl.program_id(0)

    @pl.when(pl.program_id(0) == 0)
    def _():
        running[...] = jnp.zeros_like(running)
        d_gain_ref[...] = jnp.zeros_like(d_gain_ref)

    gain_sum = jnp.zeros((1, HEAD), jnp.float32)
    pulled = []
    for item in range(batch):
        here = slice(item * GROUP, (item + 1) * GROUP)
        grads = []
        for head in range(heads):
            mixed = mixed_ref[here, head_lanes(head)]
            d_normed = d_normed_ref[here, head_lanes(head)]
            inverse_rms = lax.rsqrt(jnp.mean(mixed * mixed, axis=-1, keepdims=True) + EPSILON)
            unit = mixed * inverse_rms
            gain_sum = gain_sum + jnp.sum(d_normed * unit, axis=0, keepdims=True)
            d_unit = d_normed * gain_ref[...]
            d_mixed = inverse_rms * (
                d_unit - unit * jnp.mean(d_unit * unit, axis=-1, keepdims=True)
            )
            d_mixed_ref[here, head_lanes(head)] = d_mixed
            grads.append(d_mixed)
        pulled.append(
            [mul(reach_ref[here, head_lanes(head)].T, grads[head]) for head in range(heads)]
        )
    now = [running[head] for head in range(heads)]
    for item in reversed(range(batch)):
        keep = keep_ref[turn * batch + item]
        now = [
            keep * (mul(step_ref[item, head].T, now[head]) + pulled[item][head])
            for head in range(heads)
        ]
    for head in range(heads):
        running[head] = now[head]
    d_gain_ref[...] += gain_sum
    d_state_ref[...] = running[...]


def back_kernel(
    heads,
    batch,
    keep_ref,
    outgoing_ref,
    pre_ref,
    edge_ref,
    logit_ref,
    taps_ref,
    conv_ref,
    solved_ref,
    square_ref,
    step_ref,
    reach_ref,
    state_ref,
    d_mixed_ref,
    d_pre_ref,
    d_tail_ref,
    d_edge_ref,
    d_taps_ref,
    d_history,
    edge_history,
    running,
):
    count = pl.num_programs(0)
    turn = count - 1 - pl.program_id(0)
    scale = HEAD**-0.5
    rows, cols = grid_indices(GROUP)
    pairs = [(item, head) for item in range(batch) for head in range(heads)]
    indices = range(len(pairs))
    keeps = [keep_ref[turn * batch + item] for item in range(batch)]

    @pl.when(pl.program_id(0) == 0)
    def _():
        running[...] = outgoing_ref[...]
        d_history[batch - 1, GROUP : GROUP + 8, :] = jnp.zeros(
            (8, d_history.shape[2]), jnp.float32
        )
        d_taps_ref[...] = jnp.zeros_like(d_taps_ref)

    @pl.when(pl.program_id(0) > 0)
    def _():
        d_history[batch - 1, GROUP : GROUP + 8, :] = (
            d_history[0, 0:8, :] * keep_ref[(turn + 1) * batch]
        )

    def spot(item):
        return slice(item * GROUP, (item + 1) * GROUP)

    def act_of(item, column):
        conv = conv_ref[spot(item), head_lanes(column)]
        return conv * sigmoid(conv)

    def slope_of(item, column):
        conv = conv_ref[spot(item), head_lanes(column)]
        gate = sigmoid(conv)
        return gate * (1.0 + conv * (1.0 - gate))

    def d_unit(unit, inverse_norm, grad):
        return inverse_norm * (grad - unit * jnp.sum(unit * grad, axis=-1, keepdims=True))

    d_mixed = [d_mixed_ref[spot(item), head_lanes(head)] for item, head in pairs]
    pulled = [
        mul(reach_ref[spot(item), head_lanes(head)].T, d_mixed[index])
        for index, (item, head) in enumerate(pairs)
    ]
    d_states = [None] * len(pairs)
    now = [running[head] for head in range(heads)]
    for item in reversed(range(batch)):
        first = item * heads
        d_states[first : first + heads] = now
        now = [
            keeps[item] * (mul(step_ref[item, head].T, now[head]) + pulled[first + head])
            for head in range(heads)
        ]
    for head in range(heads):
        running[head] = now[head]

    d_out = [scale * grad for grad in d_mixed]
    states = [state_ref[item, head] for item, head in pairs]
    solved = [solved_ref[item, head] for item, head in pairs]
    scores = [square_ref[item, head, :, GROUP : 2 * GROUP] for item, head in pairs]
    acts = [act_of(item, heads + head) for item, head in pairs]
    key_scales = [unit_scale(act) for act in acts]
    keys = [act * size for act, size in zip(acts, key_scales)]
    fresh = [
        solved[index][:, HEAD:] - mul(solved[index][:, 0:HEAD], states[index])
        for index in indices
    ]
    d_fresh = [
        mul(scores[index].T, d_out[index]) + mul(keys[index], d_states[index])
        for index in indices
    ]
    d_scores = [
        jnp.where(rows >= cols, mul_nt(d_out[index], fresh[index]), 0.0) for index in indices
    ]
    d_solved = [
        jnp.concatenate([-mul_nt(d_fresh[index], states[index]), d_fresh[index]], axis=1)
        for index in indices
    ]
    d_right = [
        mul(square_ref[item, head, :, 0:GROUP].T, d_solved[index])
        for index, (item, head) in enumerate(pairs)
    ]
    d_queries = [
        mul_nt(d_out[index], states[index]) + mul(d_scores[index], keys[index])
        for index in indices
    ]
    acts = [act_of(item, head) for item, head in pairs]
    query_scales = [unit_scale(act) for act in acts]
    queries = [act * size for act, size in zip(acts, query_scales)]
    d_keys = [
        mul(d_scores[index].T, queries[index]) + mul_nt(fresh[index], d_states[index])
        for index in indices
    ]
    d_strict = [
        jnp.where(rows > cols, -mul_nt(d_right[index], solved[index]), 0.0) for index in indices
    ]
    strengths = [
        sigmoid(logit_ref[spot(item), head : head + 1]) for item, head in pairs
    ]
    overlaps = [mul_nt(key, key) for key in keys]
    both = [
        strengths[index] * d_strict[index] + (strengths[index] * d_strict[index]).T
        for index in indices
    ]
    d_keys = [
        d_keys[index]
        + strengths[index] * d_right[index][:, 0:HEAD]
        + mul(both[index], keys[index])
        for index in indices
    ]
    d_logits = []
    for index, (item, head) in enumerate(pairs):
        strength = strengths[index]
        value = act_of(item, 2 * heads + head)
        d_strength = (
            jnp.sum(d_right[index][:, 0:HEAD] * keys[index], axis=-1, keepdims=True)
            + jnp.sum(d_right[index][:, HEAD:] * value, axis=-1, keepdims=True)
            + jnp.sum(d_strict[index] * overlaps[index], axis=-1, keepdims=True)
        )
        d_logits.append(d_strength * strength * (1.0 - strength))
        for column, grad in (
            (head, d_unit(queries[index], query_scales[index], d_queries[index])),
            (heads + head, d_unit(keys[index], key_scales[index], d_keys[index])),
            (2 * heads + head, strength * d_right[index][:, HEAD:]),
        ):
            d_history[item, 0:GROUP, head_lanes(column)] = grad * slope_of(item, column)

    spread = lax.broadcasted_iota(jnp.int32, (GROUP, HEAD), 1)
    for item in range(batch):
        placed = jnp.zeros((GROUP, HEAD), jnp.float32)
        for head in range(heads):
            placed = jnp.where(spread == head, d_logits[item * heads + head], placed)
        d_pre_ref[spot(item), 3 * heads * HEAD :] = placed.astype(jnp.bfloat16)

    for item in reversed(range(batch - 1)):
        d_history[item, GROUP : GROUP + 8, :] = d_history[item + 1, 0:8, :] * keeps[item + 1]
    for column in range(3 * heads):
        lanes = head_lanes(column)
        for item in range(batch):
            pre = pre_ref[spot(item), lanes].astype(jnp.float32)
            total = jnp.zeros((GROUP, HEAD), jnp.float32)
            for tap in range(TAPS):
                part = d_history[item, TAPS - 1 - tap : TAPS - 1 - tap + GROUP, lanes]
                total = total + taps_ref[tap : tap + 1, lanes] * part
                d_taps_ref[tap : tap + 1, lanes] += jnp.sum(pre * part, axis=0, keepdims=True)
            d_pre_ref[spot(item), lanes] = total.astype(jnp.bfloat16)
        d_tail_ref[:, lanes] = jnp.where(
            turn == count - 1, total[GROUP - 8 :, :], d_tail_ref[:, lanes]
        )

    @pl.when(turn == 0)
    def _():
        edge_history[0:8, :] = jnp.zeros((8, edge_history.shape[1]), jnp.float32)
        edge_history[8:16, :] = d_history[0, 0:8, :] * keeps[0]
        total = jnp.zeros(d_edge_ref.shape, jnp.float32)
        for tap in range(TAPS):
            part = edge_history[TAPS - 1 - tap : TAPS - 1 - tap + 8, :]
            total = total + taps_ref[tap : tap + 1, :] * part
            d_taps_ref[tap : tap + 1, :] += jnp.sum(edge_ref[...] * part, axis=0, keepdims=True)
        d_edge_ref[...] = total


def passed_along(value, axis, by):
    count = lax.axis_size(axis)
    pairs = [(i, i + by) for i in range(count) if 0 <= i + by < count]
    return lax.ppermute(value, axis, pairs)


def adamw(weight, first, second, grad, rate, decay):
    first = FIRST_DECAY * first + (1.0 - FIRST_DECAY) * grad
    second = SECOND_DECAY * second + (1.0 - SECOND_DECAY) * grad * grad
    stepped = (
        first
        / (1.0 - FIRST_DECAY**STEP)
        / (jnp.sqrt(second / (1.0 - SECOND_DECAY**STEP)) + ADAM_EPSILON)
    )
    return (weight - rate * (stepped + decay * weight), first, second)


def f32(*shape):
    return jax.ShapeDtypeStruct(shape, jnp.float32)


def bf16(*shape):
    return jax.ShapeDtypeStruct(shape, jnp.bfloat16)


class Rule:
    def __init__(self, keep, heads, row_count):
        self.keep, self.heads, self.rows = keep, heads, row_count
        self.count = row_count // GROUP
        self.params = pltpu.CompilerParams(
            dimension_semantics=("arbitrary",), vmem_limit_bytes=48 * 1024 * 1024
        )

    def rows_spec(self, width, batch, back=False):
        last = self.count // batch - 1
        if back:
            return pl.BlockSpec((batch * GROUP, width), lambda n: (last - n, 0))
        return pl.BlockSpec((batch * GROUP, width), lambda n: (n, 0))

    def block_spec(self, shape, batch, back=False):
        last = self.count // batch - 1
        if back:
            return pl.BlockSpec((batch,) + shape, lambda n: (last - n, 0, 0, 0))
        return pl.BlockSpec((batch,) + shape, lambda n: (n, 0, 0, 0))

    def whole(self, *shape):
        return pl.BlockSpec(shape, lambda n: (0,) * len(shape))

    def smem(self):
        return pl.BlockSpec(memory_space=pltpu.SMEM)

    def maps(self, pre, edge, logits, taps):
        heads, rows, count, inner = self.heads, self.rows, self.count, self.heads * HEAD
        return pl.pallas_call(
            functools.partial(maps_kernel, heads, MAPS_BATCH),
            grid=(count // MAPS_BATCH,),
            in_specs=[
                self.smem(),
                self.rows_spec(3 * inner, MAPS_BATCH),
                self.whole(8, 3 * inner),
                self.rows_spec(heads, MAPS_BATCH),
                self.whole(TAPS, 3 * inner),
            ],
            out_specs=[
                self.rows_spec(3 * inner, MAPS_BATCH),
                self.block_spec((heads, GROUP, 2 * HEAD), MAPS_BATCH),
                self.block_spec((heads, GROUP, 2 * GROUP), MAPS_BATCH),
                self.block_spec((heads, HEAD, HEAD), MAPS_BATCH),
                self.block_spec((heads, HEAD, HEAD), MAPS_BATCH),
                self.rows_spec(inner, MAPS_BATCH),
                self.rows_spec(inner, MAPS_BATCH),
                self.whole(heads, HEAD, 2 * HEAD),
            ],
            out_shape=[
                f32(rows, 3 * inner),
                f32(count, heads, GROUP, 2 * HEAD),
                f32(count, heads, GROUP, 2 * GROUP),
                f32(count, heads, HEAD, HEAD),
                f32(count, heads, HEAD, HEAD),
                f32(rows, inner),
                f32(rows, inner),
                f32(heads, HEAD, 2 * HEAD),
            ],
            scratch_shapes=[
                pltpu.VMEM((MAPS_BATCH, GROUP + 8, 3 * inner), jnp.float32),
                pltpu.VMEM((heads, HEAD, 2 * HEAD), jnp.float32),
            ],
            compiler_params=self.params,
            cost_estimate=busy(35),
            name="delta_maps",
        )(self.keep, pre, edge, logits, taps)

    def outputs(self, incoming, step, fresh, reach, zero_out, gain):
        heads, rows, count, inner = self.heads, self.rows, self.count, self.heads * HEAD
        return pl.pallas_call(
            functools.partial(outputs_kernel, heads, CHAIN_BATCH),
            grid=(count // CHAIN_BATCH,),
            in_specs=[
                self.smem(),
                self.whole(heads, HEAD, HEAD),
                self.block_spec((heads, HEAD, HEAD), CHAIN_BATCH),
                self.block_spec((heads, HEAD, HEAD), CHAIN_BATCH),
                self.rows_spec(inner, CHAIN_BATCH),
                self.rows_spec(inner, CHAIN_BATCH),
                self.whole(1, HEAD),
            ],
            out_specs=[
                self.block_spec((heads, HEAD, HEAD), CHAIN_BATCH),
                self.rows_spec(inner, CHAIN_BATCH),
                self.rows_spec(inner, CHAIN_BATCH),
            ],
            out_shape=[f32(count, heads, HEAD, HEAD), f32(rows, inner), bf16(rows, inner)],
            scratch_shapes=[pltpu.VMEM((heads, HEAD, HEAD), jnp.float32)],
            compiler_params=self.params,
            cost_estimate=busy(9),
            name="delta_outputs",
        )(self.keep, incoming, step, fresh, reach, zero_out, gain)

    def tail(self, d_normed, mixed, gain, step, reach):
        heads, rows, count, inner = self.heads, self.rows, self.count, self.heads * HEAD
        return pl.pallas_call(
            functools.partial(tail_kernel, heads, CHAIN_BATCH),
            grid=(count // CHAIN_BATCH,),
            in_specs=[
                self.smem(),
                self.rows_spec(inner, CHAIN_BATCH, True),
                self.rows_spec(inner, CHAIN_BATCH, True),
                self.whole(1, HEAD),
                self.block_spec((heads, HEAD, HEAD), CHAIN_BATCH, True),
                self.rows_spec(inner, CHAIN_BATCH, True),
            ],
            out_specs=[
                self.rows_spec(inner, CHAIN_BATCH, True),
                self.whole(heads, HEAD, HEAD),
                self.whole(1, HEAD),
            ],
            out_shape=[f32(rows, inner), f32(heads, HEAD, HEAD), f32(1, HEAD)],
            scratch_shapes=[pltpu.VMEM((heads, HEAD, HEAD), jnp.float32)],
            compiler_params=self.params,
            cost_estimate=busy(11),
            name="delta_tail",
        )(self.keep, d_normed, mixed, gain, step, reach)

    def back(self, outgoing, pre, edge, logits, taps, conv, solved, square, step, reach, state, d_mixed):
        heads, rows, count, inner = self.heads, self.rows, self.count, self.heads * HEAD
        return pl.pallas_call(
            functools.partial(back_kernel, heads, BACK_BATCH),
            grid=(count // BACK_BATCH,),
            in_specs=[
                self.smem(),
                self.whole(heads, HEAD, HEAD),
                self.rows_spec(3 * inner, BACK_BATCH, True),
                self.whole(8, 3 * inner),
                self.rows_spec(heads, BACK_BATCH, True),
                self.whole(TAPS, 3 * inner),
                self.rows_spec(3 * inner, BACK_BATCH, True),
                self.block_spec((heads, GROUP, 2 * HEAD), BACK_BATCH, True),
                self.block_spec((heads, GROUP, 2 * GROUP), BACK_BATCH, True),
                self.block_spec((heads, HEAD, HEAD), BACK_BATCH, True),
                self.rows_spec(inner, BACK_BATCH, True),
                self.block_spec((heads, HEAD, HEAD), BACK_BATCH, True),
                self.rows_spec(inner, BACK_BATCH, True),
            ],
            out_specs=[
                self.rows_spec(3 * inner + HEAD, BACK_BATCH, True),
                self.whole(8, 3 * inner),
                self.whole(8, 3 * inner),
                self.whole(TAPS, 3 * inner),
            ],
            out_shape=[
                bf16(rows, 3 * inner + HEAD),
                f32(8, 3 * inner),
                f32(8, 3 * inner),
                f32(TAPS, 3 * inner),
            ],
            scratch_shapes=[
                pltpu.VMEM((BACK_BATCH, GROUP + 8, 3 * inner), jnp.float32),
                pltpu.VMEM((16, 3 * inner), jnp.float32),
                pltpu.VMEM((heads, HEAD, HEAD), jnp.float32),
            ],
            compiler_params=self.params,
            cost_estimate=busy(45),
            name="delta_back",
        )(
            self.keep, outgoing, pre, edge, logits, taps, conv, solved, square, step, reach, state,
            d_mixed,
        )


def rms_unit(values):
    return values * lax.rsqrt(jnp.mean(values * values, axis=-1, keepdims=True) + EPSILON)


def rms_back(values, gain_vec, grad):
    inverse_rms = lax.rsqrt(jnp.mean(values * values, axis=-1, keepdims=True) + EPSILON)
    unit = values * inverse_rms
    d_unit = grad * gain_vec
    d_values = inverse_rms * (d_unit - unit * jnp.mean(d_unit * unit, axis=-1, keepdims=True))
    return d_values, jnp.sum(grad * unit, axis=0)


def low(values):
    return values.astype(jnp.bfloat16)


def product(left, right, dims=((1,), (0,))):
    return lax.dot_general(left, right, (dims, ((), ())), preferred_element_type=jnp.float32)


def rows_summed(partial):
    return lax.psum_scatter(low(partial), "shard", scatter_dimension=0, tiled=True)


def rows_joined(rows):
    return lax.all_gather(rows, "shard", axis=0, tiled=True)


def seq_summed(grad, dim):
    return lax.psum_scatter(grad, "seq", scatter_dimension=dim, tiled=True)


def one_hot(indices, size):
    return (jnp.arange(size, dtype=jnp.int32)[:, None] == indices[None, :]).astype(jnp.bfloat16)


def moved(matrix, values):
    return low(product(matrix, values))


def moved_back(matrix, values):
    return low(product(matrix, values, ((0,), (0,))))


def busy(micros):
    return pl.CostEstimate(flops=micros * BUSY_FLOPS, bytes_accessed=0, transcendentals=0)


def ends(count):
    me = lax.axis_index("shard")
    return me, me > 0, me < count - 1


def meet_neighbours(count):
    me, has_left, has_right = ends(count)
    barrier = pltpu.get_barrier_semaphore()

    @pl.when(has_left)
    def _():
        pl.semaphore_signal(barrier, inc=1, device_id={"shard": me - 1}, device_id_type=MESH)

    @pl.when(has_right)
    def _():
        pl.semaphore_signal(barrier, inc=1, device_id={"shard": me + 1}, device_id_type=MESH)

    pl.semaphore_wait(barrier, has_left.astype(jnp.int32) + has_right.astype(jnp.int32))


def join_kernel(count, parts, own_ref, out_ref, own_sem, send_sem, recv_sem):
    me, has_left, has_right = ends(count)
    size = own_ref.shape[0] // parts
    meet_neighbours(count)
    own_copy = pltpu.make_async_copy(own_ref, out_ref.at[me], own_sem)
    own_copy.start()

    def piece_copy(way, block, part, source, target):
        rows = pl.ds(part * size, size)
        return pltpu.make_async_remote_copy(
            src_ref=source.at[rows] if source is own_ref else source.at[block, rows],
            dst_ref=out_ref.at[block, rows],
            send_sem=send_sem.at[way, block, part],
            recv_sem=recv_sem.at[block, part],
            device_id={"shard": target},
            device_id_type=MESH,
        )

    def each(action):
        for far in range(count):
            for part in range(parts):
                for way, present, onward, block, target in (
                    (0, me >= far, has_right, me - far, me + 1),
                    (1, me + far < count, has_left, me + far, me - 1),
                ):
                    action(far, part, way, present, onward, block, target)

    def start(far, part, way, present, onward, block, target):
        source = own_ref if far == 0 else out_ref

        if far:

            @pl.when(present)
            def _():
                piece_copy(way, block, part, out_ref, target).wait_recv()

        @pl.when(present & onward)
        def _():
            piece_copy(way, block, part, source, target).start()

    def finish(far, part, way, present, onward, block, target):
        source = own_ref if far == 0 else out_ref

        @pl.when(present & onward)
        def _():
            piece_copy(way, block, part, source, target).wait_send()

    each(start)
    each(finish)
    own_copy.wait()


def join_rows(rows, count, ident, parts=4):
    size, width = rows.shape
    return pl.pallas_call(
        functools.partial(join_kernel, count, parts),
        out_shape=jax.ShapeDtypeStruct((count, size, width), rows.dtype),
        in_specs=[pl.BlockSpec(memory_space=pl.ANY)],
        out_specs=pl.BlockSpec(memory_space=pl.ANY),
        scratch_shapes=[
            pltpu.SemaphoreType.DMA(()),
            pltpu.SemaphoreType.DMA((2, count, parts)),
            pltpu.SemaphoreType.DMA((count, parts)),
        ],
        compiler_params=pltpu.CompilerParams(collective_id=ident, has_side_effects=True),
        cost_estimate=busy(70),
        name="join_rows",
    )(rows).reshape(count * size, width)


def swap_kernel(count, to_columns, in_ref, out_ref, own_sem, send_sem, recv_sem):
    me = lax.axis_index("shard")
    barrier = pltpu.get_barrier_semaphore()
    for hop in range(1, count):
        other = lax.rem(me + hop, count)
        pl.semaphore_signal(barrier, inc=1, device_id={"shard": other}, device_id_type=MESH)
    pl.semaphore_wait(barrier, count - 1)
    if to_columns:
        width = in_ref.shape[2]
    else:
        width = out_ref.shape[2]

    def columns(ref, index):
        return ref.at[:, pl.ds(pl.multiple_of(index * width, width), width)]

    def source(block):
        return in_ref.at[block] if to_columns else columns(in_ref, block)

    def landing(block):
        return columns(out_ref, block) if to_columns else out_ref.at[block]

    own_copy = pltpu.make_async_copy(source(me), landing(me), own_sem)
    own_copy.start()

    def block_copy(hop):
        other = lax.rem(me + hop, count)
        return pltpu.make_async_remote_copy(
            src_ref=source(other),
            dst_ref=landing(me),
            send_sem=send_sem.at[hop],
            recv_sem=recv_sem.at[hop],
            device_id={"shard": other},
            device_id_type=MESH,
        )

    for hop in range(1, count):
        block_copy(hop).start()
    for hop in range(1, count):
        block_copy(hop).wait()
    own_copy.wait()


def swap_blocks(value, count, ident, to_columns):
    if to_columns:
        _, size, width = value.shape
        shape = (size, count * width)
    else:
        size, width = value.shape[0], value.shape[1] // count
        shape = (count, size, width)
    return pl.pallas_call(
        functools.partial(swap_kernel, count, to_columns),
        out_shape=jax.ShapeDtypeStruct(shape, value.dtype),
        in_specs=[pl.BlockSpec(memory_space=pl.ANY)],
        out_specs=pl.BlockSpec(memory_space=pl.ANY),
        scratch_shapes=[
            pltpu.SemaphoreType.DMA(()),
            pltpu.SemaphoreType.DMA((count,)),
            pltpu.SemaphoreType.DMA((count,)),
        ],
        compiler_params=pltpu.CompilerParams(collective_id=ident, has_side_effects=True),
        cost_estimate=busy(23),
        name="swap_blocks",
    )(value)


def relay_kernel(heads, hops, back, total_ref, fresh_ref, out_ref, sending, landing, send_sem, recv_sem):
    count = lax.axis_size("seq")
    me = lax.axis_index("seq")
    if back:
        follows, precedes, target, origin = me < count - 1, me > 0, me - 1, me + 1
    else:
        follows, precedes, target, origin = me > 0, me < count - 1, me + 1, me - 1
    barrier = pltpu.get_barrier_semaphore()

    @pl.when(follows)
    def _():
        pl.semaphore_signal(barrier, inc=1, device_id={"seq": origin}, device_id_type=MESH)

    @pl.when(precedes)
    def _():
        pl.semaphore_signal(barrier, inc=1, device_id={"seq": target}, device_id_type=MESH)

    pl.semaphore_wait(barrier, follows.astype(jnp.int32) + precedes.astype(jnp.int32))

    def state_copy(hop, head):
        return pltpu.make_async_remote_copy(
            src_ref=sending.at[hop, head],
            dst_ref=landing.at[hop, head],
            send_sem=send_sem.at[hop, head],
            recv_sem=recv_sem.at[hop, head],
            device_id={"seq": target},
            device_id_type=MESH,
        )

    for hop in range(hops):
        for head in range(heads):
            fresh = fresh_ref[head]
            if hop == 0:
                sending[hop, head] = low(fresh)
            else:

                @pl.when(follows)
                def _():
                    state_copy(hop - 1, head).wait_recv()
                    step = total_ref[head, :, 0:HEAD]
                    step = step.T if back else step
                    sending[hop, head] = low(
                        fresh + mul(step, landing[hop - 1, head].astype(jnp.float32))
                    )

                @pl.when(jnp.logical_not(follows))
                def _():
                    sending[hop, head] = low(fresh)

            @pl.when(precedes)
            def _():
                state_copy(hop, head).start()

    for head in range(heads):

        @pl.when(follows)
        def _():
            state_copy(hops - 1, head).wait_recv()
            out_ref[head] = landing[hops - 1, head].astype(jnp.float32)

        @pl.when(jnp.logical_not(follows))
        def _():
            out_ref[head] = jnp.zeros((HEAD, HEAD), jnp.float32)

    @pl.when(precedes)
    def _():
        for hop in range(hops):
            for head in range(heads):
                state_copy(hop, head).wait_send()


def relayed(total, fresh, hops, back, ident):
    heads = fresh.shape[0]
    return pl.pallas_call(
        functools.partial(relay_kernel, heads, hops, back),
        out_shape=jax.ShapeDtypeStruct((heads, HEAD, HEAD), jnp.float32),
        in_specs=[pl.BlockSpec(memory_space=pltpu.VMEM)] * 2,
        out_specs=pl.BlockSpec(memory_space=pltpu.VMEM),
        scratch_shapes=[
            pltpu.VMEM((hops, heads, HEAD, HEAD), jnp.bfloat16),
            pltpu.VMEM((hops, heads, HEAD, HEAD), jnp.bfloat16),
            pltpu.SemaphoreType.DMA((hops, heads)),
            pltpu.SemaphoreType.DMA((hops, heads)),
        ],
        compiler_params=pltpu.CompilerParams(collective_id=ident, has_side_effects=True),
        cost_estimate=busy(15),
        name="relay_back" if back else "relay",
    )(total, fresh)


def last_join_kernel(
    count,
    parts,
    shared,
    own_ref,
    small_ref,
    out_ref,
    small_out,
    seq_slots,
    layer_slots,
    own_sem,
    send_sem,
    recv_sem,
    seq_send,
    seq_recv,
    layer_send,
    layer_recv,
):
    me, has_left, has_right = ends(count)
    size = own_ref.shape[0] // parts
    devices = lax.axis_size("seq")
    here = lax.axis_index("seq")
    barrier = pltpu.get_barrier_semaphore()
    for hop in range(1, devices):
        other = lax.rem(here + hop, devices)
        pl.semaphore_signal(barrier, inc=1, device_id={"seq": other}, device_id_type=MESH)
    for hop in range(1, count):
        other = lax.rem(me + hop, count)
        pl.semaphore_signal(barrier, inc=1, device_id={"shard": other}, device_id_type=MESH)
    pl.semaphore_wait(barrier, devices + count - 2)
    own_copy = pltpu.make_async_copy(own_ref, out_ref.at[me], own_sem)
    own_copy.start()

    def seq_copy(hop):
        return pltpu.make_async_remote_copy(
            src_ref=small_ref,
            dst_ref=seq_slots.at[here],
            send_sem=seq_send.at[hop],
            recv_sem=seq_recv.at[hop],
            device_id={"seq": lax.rem(here + hop, devices)},
            device_id_type=MESH,
        )

    def layer_copy(hop):
        return pltpu.make_async_remote_copy(
            src_ref=small_out.at[pl.ds(0, shared)],
            dst_ref=layer_slots.at[me],
            send_sem=layer_send.at[hop],
            recv_sem=layer_recv.at[hop],
            device_id={"shard": lax.rem(me + hop, count)},
            device_id_type=MESH,
        )

    def piece_copy(way, block, part, source, target):
        rows = pl.ds(part * size, size)
        return pltpu.make_async_remote_copy(
            src_ref=source.at[rows] if source is own_ref else source.at[block, rows],
            dst_ref=out_ref.at[block, rows],
            send_sem=send_sem.at[way, block, part],
            recv_sem=recv_sem.at[block, part],
            device_id={"shard": target},
            device_id_type=MESH,
        )

    def each(far, action):
        for part in range(parts):
            for way, present, onward, block, target in (
                (0, me >= far, has_right, me - far, me + 1),
                (1, me + far < count, has_left, me + far, me - 1),
            ):
                action(far, part, way, present, onward, block, target)

    def start(far, part, way, present, onward, block, target):
        if far:

            @pl.when(present)
            def _():
                piece_copy(way, block, part, out_ref, target).wait_recv()

        @pl.when(present & onward)
        def _():
            piece_copy(way, block, part, out_ref if far else own_ref, target).start()

    def finish(far, part, way, present, onward, block, target):
        @pl.when(present & onward)
        def _():
            piece_copy(way, block, part, out_ref if far else own_ref, target).wait_send()

    def seq_start(hop, carry):
        seq_copy(hop).start()
        return carry

    def seq_finish(hop, carry):
        seq_copy(hop).wait()
        return carry

    lax.fori_loop(1, devices, seq_start, 0)
    seq_slots[here] = small_ref[...]
    each(0, start)
    lax.fori_loop(1, devices, seq_finish, 0)
    total = seq_slots[0]
    for index in range(1, devices):
        total = total + seq_slots[index]
    small_out[...] = total
    for hop in range(1, count):
        layer_copy(hop).start()
    layer_slots[me] = total[0:shared]
    for far in range(1, count):
        each(far, start)
    for hop in range(1, count):
        layer_copy(hop).wait()
    total = layer_slots[0]
    for index in range(1, count):
        total = total + layer_slots[index]
    small_out[0:shared, :] = total
    for far in range(count):
        each(far, finish)
    own_copy.wait()


def join_rows_and_sum(rows, small, shared, count, ident, parts=4):
    size, width = rows.shape
    devices = lax.axis_size("seq")
    joined, summed = pl.pallas_call(
        functools.partial(last_join_kernel, count, parts, shared),
        out_shape=[jax.ShapeDtypeStruct((count, size, width), rows.dtype), f32(*small.shape)],
        in_specs=[pl.BlockSpec(memory_space=pl.ANY), pl.BlockSpec(memory_space=pltpu.VMEM)],
        out_specs=[pl.BlockSpec(memory_space=pl.ANY), pl.BlockSpec(memory_space=pltpu.VMEM)],
        scratch_shapes=[
            pltpu.VMEM((devices,) + small.shape, jnp.float32),
            pltpu.VMEM((count, shared, small.shape[1]), jnp.float32),
            pltpu.SemaphoreType.DMA(()),
            pltpu.SemaphoreType.DMA((2, count, parts)),
            pltpu.SemaphoreType.DMA((count, parts)),
            pltpu.SemaphoreType.DMA((devices,)),
            pltpu.SemaphoreType.DMA((devices,)),
            pltpu.SemaphoreType.DMA((count,)),
            pltpu.SemaphoreType.DMA((count,)),
        ],
        compiler_params=pltpu.CompilerParams(collective_id=ident, has_side_effects=True),
        cost_estimate=busy(70),
        name="join_rows_and_sum",
    )(rows, small)
    return joined.reshape(count * size, width), summed


def total_join_kernel(
    count,
    parts,
    grads_ref,
    weights_ref,
    rows_ref,
    own_ref,
    out_ref,
    joined_ref,
    weigh_ref,
    grads,
    weights,
    rows_in,
    part_ref,
    weighed,
    from_left,
    from_right,
    load_sem,
    weigh_sem,
    own_sem,
    send_sem,
    recv_sem,
    join_send,
    join_recv,
):
    me, has_left, has_right = ends(count)
    size = out_ref.shape[0] // parts
    tile = 2 * HEAD
    width = out_ref.shape[1]
    loads = [
        pltpu.make_async_copy(source, target, load_sem.at[index])
        for index, (source, target) in enumerate(
            ((grads_ref, grads), (weights_ref, weights), (rows_ref, rows_in))
        )
    ]
    for load in loads:
        load.start()
    meet_neighbours(count)
    own_copy = pltpu.make_async_copy(own_ref, joined_ref.at[me], own_sem)
    own_copy.start()

    def sum_copy(way, block, part, source, target):
        rows = pl.ds(part * size, size)
        landing = (from_left, from_right)[way]
        return pltpu.make_async_remote_copy(
            src_ref=source.at[block, rows],
            dst_ref=landing.at[block, rows],
            send_sem=send_sem.at[way, block, part],
            recv_sem=recv_sem.at[way, block, part],
            device_id={"shard": target},
            device_id_type=MESH,
        )

    def join_copy(way, block, part, source, target):
        rows = pl.ds(part * size, size)
        return pltpu.make_async_remote_copy(
            src_ref=source.at[rows] if source is own_ref else source.at[block, rows],
            dst_ref=joined_ref.at[block, rows],
            send_sem=join_send.at[way, block, part],
            recv_sem=join_recv.at[block, part],
            device_id={"shard": target},
            device_id_type=MESH,
        )

    def sum_way(way, block):
        if way == 0:
            return me < block, has_left, me + 1
        return me > block, has_right, me - 1

    def join_way(far, way):
        if way == 0:
            return me >= far, has_right, me - far, me + 1
        return me + far < count, has_left, me + far, me - 1

    def join_start(far, way, part):
        present, onward, block, target = join_way(far, way)
        if far:

            @pl.when(present)
            def _():
                join_copy(way, block, part, joined_ref, target).wait_recv()

        @pl.when(present & onward)
        def _():
            join_copy(way, block, part, joined_ref if far else own_ref, target).start()

    def sum_start(way, block, part):
        sends, receives, target = sum_way(way, block)
        landing = (from_left, from_right)[way]
        rows = pl.ds(part * size, size)

        @pl.when(sends & receives)
        def _():
            sum_copy(way, block, part, landing, target).wait_recv()
            landing[block, rows, :] = (
                landing[block, rows, :].astype(jnp.float32)
                + part_ref[block, rows, :].astype(jnp.float32)
            ).astype(jnp.bfloat16)
            sum_copy(way, block, part, landing, target).start()

    for part in range(parts):
        for way in range(2):
            join_start(0, way, part)
    loads[0].wait()
    loads[1].wait()

    def block_turn(turn, carry):
        block = jnp.int32(0)
        for place in range(count):
            by_distance = sorted(range(count), key=lambda other: -abs(other - place))
            for index, other in enumerate(by_distance):
                block = jnp.where((me == place) & (turn == index), other, block)

        def tile_turn(index, inner_carry):
            across = pl.ds(pl.multiple_of(index * tile, tile), tile)
            part_ref[block, :, across] = low(
                product(grads[block], weights[across, :], ((1,), (1,)))
            )
            return inner_carry

        lax.fori_loop(0, width // tile, tile_turn, 0)

        @pl.when((block > me) & jnp.logical_not(has_left))
        def _():
            for part in range(parts):
                sum_copy(0, block, part, part_ref, me + 1).start()

        @pl.when((block < me) & jnp.logical_not(has_right))
        def _():
            for part in range(parts):
                sum_copy(1, block, part, part_ref, me - 1).start()

        return carry

    lax.fori_loop(0, count, block_turn, 0)
    loads[2].wait()
    wide = weights.shape[1]
    rows_total = count * out_ref.shape[0]

    def weigh_store(turn):
        rows = pl.ds(pl.multiple_of(turn * tile, tile), tile)
        return pltpu.make_async_copy(weighed.at[rows], weigh_ref.at[rows], weigh_sem.at[turn])

    def weigh_turn(turn, carry):
        rows = pl.ds(pl.multiple_of(turn * tile, tile), tile)
        turned = rows_in[:, rows].T

        def weigh_tile(first, span):
            against = grads[:, :, pl.ds(first, span)].reshape(rows_total, span)
            weighed[rows, pl.ds(first, span)] = low(product(turned, against))

        def tile_turn(index, inner_carry):
            weigh_tile(pl.multiple_of(index * tile, tile), tile)
            return inner_carry

        lax.fori_loop(0, wide // tile, tile_turn, 0)
        if wide % tile:
            weigh_tile(wide // tile * tile, wide % tile)
        weigh_store(turn).start()
        return carry

    for step in range(count):
        if step == min(2, count - 1):
            lax.fori_loop(0, width // tile, weigh_turn, 0)
        for part in range(parts):
            if step:
                for way in range(2):
                    join_start(step, way, part)
            if step < count - 1:
                sum_start(0, count - 1 - step, part)
                sum_start(1, step, part)

    for block in range(count):

        @pl.when(me == block)
        def _():
            for part in range(parts):
                rows = pl.ds(part * size, size)
                total = part_ref[block, rows, :].astype(jnp.float32)
                if block > 0:
                    sum_copy(0, block, part, from_left, me).wait_recv()
                    total = total + from_left[block, rows, :].astype(jnp.float32)
                if block < count - 1:
                    sum_copy(1, block, part, from_right, me).wait_recv()
                    total = total + from_right[block, rows, :].astype(jnp.float32)
                out_ref[rows, :] = total

    for step in range(count):
        for part in range(parts):
            for way in range(2):
                present, onward, block, target = join_way(step, way)

                @pl.when(present & onward)
                def _():
                    source = joined_ref if step else own_ref
                    join_copy(way, block, part, source, target).wait_send()

            if step < count - 1:
                for way, block in ((0, count - 1 - step), (1, step)):
                    sends, _, target = sum_way(way, block)

                    @pl.when(sends)
                    def _():
                        sum_copy(way, block, part, part_ref, target).wait_send()

    own_copy.wait()

    def weigh_finish(turn, carry):
        weigh_store(turn).wait()
        return carry

    lax.fori_loop(0, width // tile, weigh_finish, 0)


def total_and_join(grads, weights, rows, own, count, ident, parts=4):
    size, width = own.shape
    wide = grads.shape[1]
    total, joined, weighed = pl.pallas_call(
        functools.partial(total_join_kernel, count, parts),
        out_shape=[
            jax.ShapeDtypeStruct((size, width), jnp.float32),
            jax.ShapeDtypeStruct((count, size, width), own.dtype),
            bf16(width, wide),
        ],
        in_specs=[pl.BlockSpec(memory_space=pl.ANY)] * 4,
        out_specs=[pl.BlockSpec(memory_space=pltpu.VMEM)] + [pl.BlockSpec(memory_space=pl.ANY)] * 2,
        scratch_shapes=[
            pltpu.VMEM((count, size, wide), jnp.bfloat16),
            pltpu.VMEM((width, wide), jnp.bfloat16),
            pltpu.VMEM((count * size, width), jnp.bfloat16),
            pltpu.VMEM((count, size, width), jnp.bfloat16),
            pltpu.VMEM((width, wide), jnp.bfloat16),
            pltpu.VMEM((count, size, width), jnp.bfloat16),
            pltpu.VMEM((count, size, width), jnp.bfloat16),
            pltpu.SemaphoreType.DMA((3,)),
            pltpu.SemaphoreType.DMA((width // (2 * HEAD),)),
            pltpu.SemaphoreType.DMA(()),
            pltpu.SemaphoreType.DMA((2, count, parts)),
            pltpu.SemaphoreType.DMA((2, count, parts)),
            pltpu.SemaphoreType.DMA((2, count, parts)),
            pltpu.SemaphoreType.DMA((count, parts)),
        ],
        compiler_params=pltpu.CompilerParams(
            collective_id=ident, has_side_effects=True, vmem_limit_bytes=60 * 1024 * 1024
        ),
        cost_estimate=busy(95),
        name="total_and_join",
    )(grads.reshape(count, size, wide), weights, rows, own)
    return total, joined.reshape(count * size, width), weighed


def feed_kernel(
    count,
    parts,
    own_ref,
    dy_ref,
    gate_up_ref,
    down_ref,
    down_part_out,
    grad_open_out,
    grad_down_out,
    total_ref,
    gate_up,
    down,
    dy,
    rows_all,
    hidden,
    d_both,
    partial,
    landing,
    down_part,
    open_stage,
    down_stage,
    load_sem,
    part_sem,
    open_sem,
    down_sem,
    join_send,
    join_recv,
    sum_send,
    sum_recv,
):
    me, has_left, has_right = ends(count)
    units, width = down.shape
    piece = own_ref.shape[0] // parts
    tile = 2 * HEAD
    loads = [
        pltpu.make_async_copy(gate_up_ref, gate_up, load_sem.at[0]),
        pltpu.make_async_copy(dy_ref, dy, load_sem.at[1]),
        pltpu.make_async_copy(down_ref, down, load_sem.at[2]),
    ]
    for load in loads:
        load.start()
    rows_all[me] = own_ref[...]
    meet_neighbours(count)

    def part_store(block):
        return pltpu.make_async_copy(
            down_part.at[block], down_part_out.at[block], part_sem.at[block]
        )

    def open_store(turn):
        slot = lax.rem(turn, 2)
        rows = pl.ds(pl.multiple_of(turn * tile, tile), tile)
        return pltpu.make_async_copy(
            open_stage.at[slot], grad_open_out.at[rows], open_sem.at[slot]
        )

    def down_store(turn, size):
        slot = lax.rem(turn, 2)
        rows = pl.ds(pl.multiple_of(turn * tile, tile), size)
        return pltpu.make_async_copy(
            down_stage.at[slot, pl.ds(0, size)], grad_down_out.at[rows], down_sem.at[slot]
        )

    def join_copy(way, block, part):
        rows = pl.ds(part * piece, piece)
        return pltpu.make_async_remote_copy(
            src_ref=rows_all.at[block, rows],
            dst_ref=rows_all.at[block, rows],
            send_sem=join_send.at[way, block, part],
            recv_sem=join_recv.at[block, part],
            device_id={"shard": me - 1 if way else me + 1},
            device_id_type=MESH,
        )

    def sum_copy(way, block, part, source):
        rows = pl.ds(part * piece, piece)
        target = me - 1 if way else me + 1
        slot = jnp.where(block == target, count, block) if way else block
        return pltpu.make_async_remote_copy(
            src_ref=source.at[block, rows],
            dst_ref=landing.at[slot, rows],
            send_sem=sum_send.at[way, block, part],
            recv_sem=sum_recv.at[way, block, part],
            device_id={"shard": target},
            device_id_type=MESH,
        )

    def open_tile(block, first, size):
        across = pl.ds(first, size)
        beyond = pl.ds(pl.multiple_of(units + first, HEAD), size)
        rows = rows_all[block]
        gate = jnp.dot(rows, gate_up[:, across], preferred_element_type=jnp.float32)
        up = jnp.dot(rows, gate_up[:, beyond], preferred_element_type=jnp.float32)
        d_hidden = product(dy[block], down[across, :], ((1,), (1,)))
        opened = sigmoid(gate)
        wave = gate * opened
        hidden[block, :, across] = low(wave * up)
        d_both[block, :, across] = low(d_hidden * up * (opened * (1.0 + gate * (1.0 - opened))))
        d_both[block, :, beyond] = low(d_hidden * wave)

    def compute(block):
        def open_turn(turn, carry):
            open_tile(block, pl.multiple_of(turn * tile, tile), tile)
            return carry

        lax.fori_loop(0, units // tile, open_turn, 0)
        if units % tile:
            open_tile(block, units // tile * tile, units % tile)

        def close_turn(turn, carry):
            across = pl.ds(pl.multiple_of(turn * tile, tile), tile)
            partial[block, :, across] = low(
                product(d_both[block], gate_up[across, :], ((1,), (1,)))
            )
            return carry

        def down_turn(turn, carry):
            across = pl.ds(pl.multiple_of(turn * tile, tile), tile)
            down_part[block, :, across] = low(product(hidden[block], down[:, across]))
            return carry

        lax.fori_loop(0, width // tile, close_turn, 0)
        lax.fori_loop(0, width // tile, down_turn, 0)

    def slot_turn(slot, carry):
        far = (slot + 1) // 2
        rightward = lax.rem(slot, 2) == 1

        @pl.when(slot == 0)
        def _():
            for part in range(parts):

                @pl.when(has_right)
                def _():
                    join_copy(0, me, part).start()

                @pl.when(has_left)
                def _():
                    join_copy(1, me, part).start()

            for load in loads:
                load.wait()

        @pl.when(rightward)
        def _():
            for part in range(parts):
                for way, present, onward, block in (
                    (0, me >= far, has_right, me - far),
                    (1, me + far < count, has_left, me + far),
                ):

                    @pl.when(present)
                    def _():
                        join_copy(way, block, part).wait_recv()

                    @pl.when(present & onward)
                    def _():
                        join_copy(way, block, part).start()

        block = jnp.where(rightward, me - far, me + far)

        @pl.when((block >= 0) & (block < count))
        def _():
            compute(block)
            part_store(block).start()

            @pl.when((block > me) & jnp.logical_not(has_left))
            def _():
                for part in range(parts):
                    sum_copy(0, block, part, partial).start()

            @pl.when((block < me) & jnp.logical_not(has_right))
            def _():
                for part in range(parts):
                    sum_copy(1, block, part, partial).start()

        return carry

    lax.fori_loop(0, 2 * count - 1, slot_turn, 0)

    def add_on(way, block, part):
        rows = pl.ds(part * piece, piece)
        sum_copy(way, block, part, landing).wait_recv()
        landing[block, rows, :] = low(
            landing[block, rows, :].astype(jnp.float32)
            + partial[block, rows, :].astype(jnp.float32)
        )
        sum_copy(way, block, part, landing).start()

    rows_total = count * own_ref.shape[0]

    def weigh(left, right, stage, across_count):
        turned = left.reshape(rows_total, left.shape[2]).T

        def turn_of(turn, carry):
            across = pl.ds(pl.multiple_of(turn * tile, tile), tile)
            against = right[:, :, across].reshape(rows_total, tile)
            stage[:, across] = low(product(turned, against))
            return carry

        lax.fori_loop(0, across_count, turn_of, 0)

    open_count = width // tile
    down_count, down_rest = units // tile, units % tile

    def late_turn(turn, carry):
        step, part = 2 + turn // parts, lax.rem(turn, parts)

        @pl.when((step < count) & (me < step) & has_left)
        def _():
            add_on(0, step, part)

        @pl.when((step < count) & (me > count - 1 - step) & has_right)
        def _():
            add_on(1, count - 1 - step, part)

        slot = lax.rem(turn, 2)
        cols = pl.ds(pl.multiple_of(turn * tile, tile), tile)

        @pl.when(turn < open_count)
        def _():
            @pl.when(turn >= 2)
            def _():
                open_store(turn - 2).wait()

            weigh(rows_all[:, :, cols], d_both, open_stage.at[slot], 2 * units // tile)
            open_store(turn).start()

        @pl.when(turn < down_count)
        def _():
            @pl.when(turn >= 2)
            def _():
                down_store(turn - 2, tile).wait()

            weigh(hidden[:, :, cols], dy, down_stage.at[slot], width // tile)
            down_store(turn, tile).start()

        return carry

    late_count = max((count - 2) * parts, open_count)
    lax.fori_loop(0, late_count, late_turn, 0)
    for turn in range(max(0, open_count - 2), open_count):
        open_store(turn).wait()
    for turn in range(max(0, down_count - 2), down_count):
        down_store(turn, tile).wait()
    if down_rest:
        weigh(
            hidden[:, :, down_count * tile :],
            dy,
            down_stage.at[down_count % 2, pl.ds(0, down_rest)],
            width // tile,
        )
        down_store(down_count, down_rest).start()

    for part in range(parts):
        rows = pl.ds(part * piece, piece)
        total_ref[rows, :] = partial[me, rows, :].astype(jnp.float32)

        @pl.when(has_left)
        def _():
            sum_copy(0, me, part, landing).wait_recv()
            total_ref[rows, :] += landing[me, rows, :].astype(jnp.float32)

        @pl.when(has_right)
        def _():
            sum_copy(1, me, part, landing).wait_recv()
            total_ref[rows, :] += landing[count, rows, :].astype(jnp.float32)

    for block in range(count):
        for part in range(parts):

            @pl.when((me >= block) & has_right)
            def _():
                join_copy(0, block, part).wait_send()

            @pl.when((me <= block) & has_left)
            def _():
                join_copy(1, block, part).wait_send()

            @pl.when(me < block)
            def _():
                sum_copy(0, block, part, partial).wait_send()

            @pl.when(me > block)
            def _():
                sum_copy(1, block, part, partial).wait_send()

        part_store(block).wait()

    if down_rest:
        down_store(down_count, down_rest).wait()


def feed_forward(own, dy, gate_up_mat, down_mat, count, ident, parts=4):
    size, width = own.shape
    units = down_mat.shape[0]
    dma = pltpu.SemaphoreType.DMA
    down_part, grad_open, grad_down, total = pl.pallas_call(
        functools.partial(feed_kernel, count, parts),
        out_shape=[
            bf16(count, size, width),
            bf16(width, 2 * units),
            bf16(units, width),
            f32(size, width),
        ],
        in_specs=[pl.BlockSpec(memory_space=pltpu.VMEM)] + [pl.BlockSpec(memory_space=pl.ANY)] * 3,
        out_specs=[pl.BlockSpec(memory_space=pl.ANY)] * 3 + [pl.BlockSpec(memory_space=pltpu.VMEM)],
        scratch_shapes=[
            pltpu.VMEM((width, 2 * units), jnp.bfloat16),
            pltpu.VMEM((units, width), jnp.bfloat16),
            pltpu.VMEM((count, size, width), jnp.bfloat16),
            pltpu.VMEM((count, size, width), jnp.bfloat16),
            pltpu.VMEM((count, size, units), jnp.bfloat16),
            pltpu.VMEM((count, size, 2 * units), jnp.bfloat16),
            pltpu.VMEM((count, size, width), jnp.bfloat16),
            pltpu.VMEM((count + 1, size, width), jnp.bfloat16),
            pltpu.VMEM((count, size, width), jnp.bfloat16),
            pltpu.VMEM((2, 2 * HEAD, 2 * units), jnp.bfloat16),
            pltpu.VMEM((2, 2 * HEAD, width), jnp.bfloat16),
            dma((3,)),
            dma((count,)),
            dma((2,)),
            dma((2,)),
            dma((2, count, parts)),
            dma((count, parts)),
            dma((2, count, parts)),
            dma((2, count, parts)),
        ],
        compiler_params=pltpu.CompilerParams(
            collective_id=ident, has_side_effects=True, vmem_limit_bytes=63 * 1024 * 1024
        ),
        cost_estimate=busy(120),
        name="feed_forward",
    )(own, dy.reshape(count, size, width), gate_up_mat, down_mat)
    return down_part.reshape(count * size, width), grad_open, grad_down, total


def per_device(
    hidden_in,
    out_grad,
    deal,
    lengths,
    qkv_weight,
    qkv_first,
    qkv_second,
    beta_weight,
    beta_first,
    beta_second,
    out_weight,
    out_first,
    out_second,
    gate_up_weight,
    gate_up_first,
    gate_up_second,
    down_weight,
    down_first,
    down_second,
    conv_weight,
    conv_first,
    conv_second,
    gains,
    gains_first,
    gains_second,
):
    row_count, model_width = hidden_in.shape
    heads = beta_weight.shape[1]
    inner = qkv_weight.shape[2]
    units = down_weight.shape[0]
    devices = lax.axis_size("seq")
    layers = lax.axis_size("shard")
    place = lax.axis_index("shard")
    longest = {4: 4096, 16: 8192}[lengths.shape[0]]
    hops = min(devices - 1, -(-longest // row_count))
    share = row_count // devices // layers
    quarter = devices * share
    _, order, sent_place = lax.sort(
        (deal // row_count, jnp.arange(row_count, dtype=jnp.int32), deal % row_count), num_keys=1
    )
    ordered = order.reshape(devices, layers, share)
    own_order = lax.dynamic_index_in_dim(ordered, place, 1, keepdims=False).reshape(quarter)
    by_layer = jnp.swapaxes(ordered, 0, 1).reshape(row_count)
    chosen = one_hot(own_order, row_count)
    sorting = one_hot(by_layer, row_count)

    def exchanged(rows):
        width = rows.shape[-1]
        return lax.all_to_all(
            rows.reshape(devices, share, width), "seq", split_axis=0, concat_axis=0, tiled=True
        ).reshape(quarter, width)

    own_x = exchanged(moved_back(chosen, hidden_in)).astype(jnp.float32)
    got_place = lax.all_to_all(
        sent_place.reshape(devices, layers * share, 1),
        "seq",
        split_axis=0,
        concat_axis=0,
        tiled=True,
    )
    got_place = jnp.swapaxes(got_place.reshape(devices, layers, share), 0, 1).reshape(row_count)
    to_chain = one_hot(got_place, row_count)

    sorted_dy, own_x = lax.optimization_barrier(
        (moved_back(one_hot(order, row_count), out_grad), own_x)
    )
    all_dy = lax.all_to_all(
        sorted_dy.reshape(devices, layers, share, model_width),
        "seq",
        split_axis=0,
        concat_axis=0,
        tiled=True,
    )

    first_place = lax.axis_index("seq") * row_count
    places = first_place + jnp.arange(0, row_count, GROUP, dtype=jnp.int32)
    starts = jnp.cumsum(lengths) - lengths
    keep = jnp.all(starts[None, :] != places[:, None], axis=1).astype(jnp.float32)

    beta_pad = jnp.zeros((beta_weight.shape[0], HEAD - heads), jnp.bfloat16)
    mixer_mat = lax.all_gather(
        jnp.concatenate(
            [low(qkv_weight).reshape(-1, 3 * inner), low(beta_weight), beta_pad], axis=1
        ),
        "seq",
        axis=0,
        tiled=True,
    )
    out_low = low(out_weight)
    out_rows = lax.all_to_all(
        jnp.broadcast_to(out_low[None], (layers,) + out_low.shape),
        "shard",
        split_axis=0,
        concat_axis=0,
        tiled=True,
    ).reshape(layers * inner, out_low.shape[1])
    out_rows, own_x = lax.optimization_barrier((out_rows, own_x))
    out_mat = lax.all_gather(out_rows, "seq", axis=1, tiled=True)
    gate_up_mat = lax.all_gather(
        low(gate_up_weight).reshape(-1, 2 * units), "seq", axis=0, tiled=True
    )
    down_mat = lax.all_gather(low(down_weight), "seq", axis=1, tiled=True)
    gain_in = gains[:model_width]
    gain_ff = gains[model_width : 2 * model_width]
    gain_out = gains[2 * model_width :].reshape(1, HEAD)
    conv_mat = conv_weight.reshape(TAPS, 3 * inner)

    normed_in = join_rows(low(rms_unit(own_x) * gain_in), layers, 0)
    normed_in, all_dy = lax.optimization_barrier((normed_in, all_dy))
    all_dy = jnp.swapaxes(all_dy, 0, 1).reshape(row_count, model_width)
    own_dy = lax.dynamic_slice_in_dim(all_dy, place * quarter, quarter, 0)
    mixed_in = product(normed_in, mixer_mat)
    logits = mixed_in[:, 3 * inner :]
    logits_high = low(logits)
    logits_low = low(logits - logits_high.astype(jnp.float32))
    chain_in = product(
        to_chain,
        jnp.concatenate([low(mixed_in[:, : 3 * inner]), logits_high, logits_low], axis=1),
    )
    projected = low(chain_in[:, : 3 * inner])
    logits = (
        chain_in[:, 3 * inner : 3 * inner + heads]
        + chain_in[:, 3 * inner + HEAD : 3 * inner + HEAD + heads]
    )
    edge_rows = passed_along(projected[row_count - 8 :], "seq", 1).astype(jnp.float32)
    edge_rows = edge_rows * (jnp.arange(8) >= 8 - (TAPS - 1)).astype(jnp.float32)[:, None]
    rule = Rule(keep, heads, row_count)
    conv, solved, square, step, fresh, reach, zero_out, total = rule.maps(
        projected, edge_rows, logits, conv_mat
    )
    incoming = relayed(total, total[:, :, HEAD:], hops, False, 7)
    state, mixed, normed = rule.outputs(incoming, step, fresh, reach, zero_out, gain_out)

    normed = moved_back(to_chain, normed)
    own_normed = swap_blocks(normed.reshape(layers, quarter, inner), layers, 1, True)
    residual = own_x + product(own_normed, out_mat)
    result, grad_gate_up, grad_down, d_normed_ff = feed_forward(
        low(rms_unit(residual) * gain_ff), all_dy, gate_up_mat, down_mat, layers, 2
    )
    red_gate_up = seq_summed(grad_gate_up, 0)
    d_residual, grad_gain_ff = rms_back(residual, gain_ff, d_normed_ff)
    d_residual = own_dy.astype(jnp.float32) + d_residual
    own_mix = low(d_residual)
    all_mix = join_rows(own_mix, layers, 4)
    out_own = lax.dynamic_slice_in_dim(out_mat, place * inner, inner, 0)
    d_normed = low(product(all_mix, out_own, ((1,), (1,))))
    grad_out = low(product(normed, all_mix, ((0,), (0,))))
    d_normed, grad_out, result = lax.optimization_barrier((d_normed, grad_out, result))
    result = lax.psum_scatter(result, "shard", scatter_dimension=0, tiled=True)
    red_down = seq_summed(grad_down, 1)
    red_out = seq_summed(grad_out, 1)
    d_normed = product(to_chain, d_normed)
    d_mixed, d_first_state, grad_gain_out = rule.tail(d_normed, mixed, gain_out, step, reach)
    d_mixed, red_gate_up = lax.optimization_barrier((d_mixed, red_gate_up))
    outgoing = relayed(total, d_first_state, hops, True, 8)
    d_pre, d_tail, d_edge, grad_taps = rule.back(
        outgoing, projected, edge_rows, logits, conv_mat, conv, solved, square, step, reach, state,
        d_mixed,
    )
    d_tail = low(d_tail + passed_along(d_edge, "seq", -1))
    d_pre = lax.dynamic_update_slice(d_pre, d_tail, (row_count - 8, 0))
    d_mixed_in = moved_back(to_chain, d_pre)
    d_mixed_in, result, red_gate_up = lax.optimization_barrier((d_mixed_in, result, red_gate_up))
    result = exchanged(low(residual + result.astype(jnp.float32)))
    red_gate_up = red_gate_up.astype(jnp.float32).reshape(gate_up_weight.shape)
    gate_up_new = adamw(
        gate_up_weight, gate_up_first, gate_up_second, red_gate_up, RATE_WIDE, SHRINK
    )
    result, *gate_up_new = lax.optimization_barrier((result, *gate_up_new))
    d_normed_in, result, grad_mixer = total_and_join(
        d_mixed_in, mixer_mat, normed_in, result, layers, 5
    )
    red_mixer = seq_summed(grad_mixer, 0)
    d_normed_in, red_down, red_out = lax.optimization_barrier((d_normed_in, red_down, red_out))
    d_input, grad_gain_in = rms_back(own_x, gain_in, d_normed_in)
    d_input = exchanged(low(d_residual + d_input))
    shared = -(-gains.shape[0] // (8 * HEAD)) * 8
    small = jnp.concatenate(
        [
            grad_gain_in,
            grad_gain_ff,
            grad_gain_out.reshape(HEAD),
            jnp.zeros((shared * HEAD - gains.shape[0],), jnp.float32),
            grad_taps.reshape(-1),
        ]
    ).reshape(-1, HEAD)
    d_input, small_sum = join_rows_and_sum(d_input, small, shared, layers, 6)
    d_input, red_mixer = lax.optimization_barrier((d_input, red_mixer))


    red_mixer = red_mixer.astype(jnp.float32)
    red_qkv = red_mixer[:, : 3 * inner].reshape(qkv_weight.shape)
    red_beta = red_mixer[:, 3 * inner : 3 * inner + heads]
    red_out = red_out.astype(jnp.float32)
    red_down = red_down.astype(jnp.float32)
    red_conv = small_sum[shared:].reshape(conv_weight.shape)
    red_gains = small_sum[:shared].reshape(-1)[: gains.shape[0]]
    qkv_new = adamw(qkv_weight, qkv_first, qkv_second, red_qkv, RATE_WIDE, SHRINK)
    beta_new = adamw(beta_weight, beta_first, beta_second, red_beta, RATE_WIDE, SHRINK)
    out_new = adamw(out_weight, out_first, out_second, red_out, RATE_WIDE, SHRINK)
    down_new = adamw(down_weight, down_first, down_second, red_down, RATE_DOWN, SHRINK)
    conv_new = adamw(conv_weight, conv_first, conv_second, red_conv, RATE_CONV, 0.0)
    gains_new = adamw(gains, gains_first, gains_second, red_gains, RATE_GAIN, 0.0)
    return (
        moved(sorting, result),
        moved(sorting, d_input),
        *qkv_new,
        *beta_new,
        *out_new,
        *gate_up_new,
        *down_new,
        *conv_new,
        *gains_new,
    )


def solution(mesh):
    return jax.shard_map(
        per_device,
        mesh=mesh,
        in_specs=(
            P("seq", None),
            P("seq", None),
            P("seq"),
            P(),
            P("seq", None, "shard"),
            P("seq", None, "shard"),
            P("seq", None, "shard"),
            P("seq", "shard"),
            P("seq", "shard"),
            P("seq", "shard"),
            P("shard", "seq"),
            P("shard", "seq"),
            P("shard", "seq"),
            P("seq", None, "shard"),
            P("seq", None, "shard"),
            P("seq", None, "shard"),
            P("shard", "seq"),
            P("shard", "seq"),
            P("shard", "seq"),
            P(None, None, "shard"),
            P(None, None, "shard"),
            P(None, None, "shard"),
            P(),
            P(),
            P(),
        ),
        out_specs=(
            P("seq", None),
            P("seq", None),
            P("seq", None, "shard"),
            P("seq", None, "shard"),
            P("seq", None, "shard"),
            P("seq", "shard"),
            P("seq", "shard"),
            P("seq", "shard"),
            P("shard", "seq"),
            P("shard", "seq"),
            P("shard", "seq"),
            P("seq", None, "shard"),
            P("seq", None, "shard"),
            P("seq", None, "shard"),
            P("shard", "seq"),
            P("shard", "seq"),
            P("shard", "seq"),
            P(None, None, "shard"),
            P(None, None, "shard"),
            P(None, None, "shard"),
            P(),
            P(),
            P(),
        ),
        check_vma=False,
    )
```

```python
import functools

import jax
import jax.numpy as jnp
from jax import lax
from jax.experimental import pallas as pl
from jax.experimental.pallas import tpu as pltpu
from jax.sharding import PartitionSpec as P

HEAD = 128
TAPS = 4
GROUP = 64
BUSY_FLOPS = 10_000_000
MAPS_BATCH = 4
CHAIN_BATCH = 4
BACK_BATCH = 2
STEP = 10


EPSILON = 1e-06
PRECISE = lax.Precision.HIGHEST
MESH = pl.DeviceIdType.MESH
FIRST_DECAY = 0.9
SECOND_DECAY = 0.95
ADAM_EPSILON = 1e-08
RATE_WIDE = 0.044
RATE_DOWN = 0.027
RATE_CONV = 0.8
RATE_GAIN = 0.3
SHRINK = 0.1


def halves(value):
    high = value.astype(jnp.bfloat16)
    return high, (value - high.astype(jnp.float32)).astype(jnp.bfloat16)


def mul(left, right, dims=((1,), (0,))):
    def one(a, b):
        return lax.dot_general(a, b, (dims, ((), ())), preferred_element_type=jnp.float32)

    left_high, left_low = halves(left)
    right_high, right_low = halves(right)
    return one(left_high, right_high) + (one(left_high, right_low) + one(left_low, right_high))


def mul_nt(left, right):
    return mul(left, right, ((1,), (1,)))


def quick(left, right, dims=((1,), (0,))):
    return lax.dot_general(
        left.astype(jnp.bfloat16),
        right.astype(jnp.bfloat16),
        (dims, ((), ())),
        preferred_element_type=jnp.float32,
    )


def quick_nt(left, right):
    return quick(left, right, ((1,), (1,)))


def grid_indices(size):
    return (
        lax.broadcasted_iota(jnp.int32, (size, size), 0),
        lax.broadcasted_iota(jnp.int32, (size, size), 1),
    )


def unit_lower_inverses(strict_parts):
    size = strict_parts[0].shape[0]
    rows, cols = grid_indices(size)
    inverses = [jnp.where(rows == cols, 1.0, 0.0) for _ in strict_parts]
    level = 0
    while (1 << level) < size:
        corner = (
            ((rows >> (level + 1)) == (cols >> (level + 1)))
            & (((rows >> level) & 1) == 1)
            & (((cols >> level) & 1) == 0)
        )
        parts = [jnp.where(corner, strict, 0.0) for strict in strict_parts]
        if level == 0:
            inverses = [inverse - part for inverse, part in zip(inverses, parts)]
        else:
            inner = [mul(part, inverse) for inverse, part in zip(inverses, parts)]
            outer = [mul(inverse, part) for inverse, part in zip(inverses, inner)]
            inverses = [inverse - part for inverse, part in zip(inverses, outer)]
        level += 1
    return inverses


def sigmoid(value):
    return 1.0 / (1.0 + jnp.exp(-value))


def unit_scale(act):
    return lax.rsqrt(jnp.sum(act * act, axis=-1, keepdims=True) + EPSILON)


def head_lanes(column):
    return slice(column * HEAD, (column + 1) * HEAD)


def maps_kernel(
    heads,
    batch,
    keep_ref,
    pre_ref,
    edge_ref,
    logit_ref,
    taps_ref,
    conv_ref,
    solved_ref,
    square_ref,
    step_ref,
    fresh_ref,
    reach_ref,
    zero_out_ref,
    total_ref,
    history,
    running,
):
    turn = pl.program_id(0)
    scale = HEAD**-0.5
    pairs = [(item, head) for item in range(batch) for head in range(heads)]
    keeps = [keep_ref[turn * batch + item] for item in range(batch)]

    @pl.when(turn == 0)
    def _():
        history[0, 0:8, :] = edge_ref[...] * keeps[0]
        rows, cols = grid_indices(HEAD)
        start = jnp.where(rows == cols, 1.0, 0.0)
        for head in range(heads):
            running[head, :, 0:HEAD] = start
            running[head, :, HEAD : 2 * HEAD] = jnp.zeros((HEAD, HEAD), jnp.float32)

    @pl.when(turn > 0)
    def _():
        history[0, 0:8, :] = history[batch - 1, GROUP : GROUP + 8, :] * keeps[0]

    for item in range(batch):
        history[item, 8 : GROUP + 8, :] = pre_ref[
            item * GROUP : (item + 1) * GROUP, :
        ].astype(jnp.float32)
        if item:
            history[item, 0:8, :] = history[item - 1, GROUP : GROUP + 8, :] * keeps[item]

    def conv_of(item, column):
        cols = head_lanes(column)
        total = taps_ref[0:1, cols] * history[item, 5 : 5 + GROUP, cols]
        for tap in range(1, TAPS):
            shifted = history[item, 5 + tap : 5 + tap + GROUP, cols]
            total = total + taps_ref[tap : tap + 1, cols] * shifted
        conv_ref[item * GROUP : (item + 1) * GROUP, cols] = total
        return total * sigmoid(total)

    rows, cols = grid_indices(GROUP)
    big_rows, big_cols = grid_indices(HEAD)
    keys = [conv_of(item, heads + head) for item, head in pairs]
    keys = [key * unit_scale(key) for key in keys]
    strengths = [
        sigmoid(logit_ref[item * GROUP : (item + 1) * GROUP, head : head + 1])
        for item, head in pairs
    ]
    overlaps = [mul_nt(key, key) for key in keys]
    inverses = unit_lower_inverses(
        [
            jnp.where(rows > cols, strength * overlap, 0.0)
            for strength, overlap in zip(strengths, overlaps)
        ]
    )
    queries = [conv_of(item, head) for item, head in pairs]
    queries = [query * unit_scale(query) for query in queries]
    scores = [
        jnp.where(rows >= cols, mul_nt(query, key), 0.0) for query, key in zip(queries, keys)
    ]
    values = [conv_of(item, 2 * heads + head) for item, head in pairs]
    solved = [
        mul(inverse, jnp.concatenate([strength * key, strength * value], axis=1))
        for inverse, strength, key, value in zip(inverses, strengths, keys, values)
    ]
    pushed = [mul(key.T, part) for key, part in zip(keys, solved)]
    mixed = [mul(score, part) for score, part in zip(scores, solved)]
    steps = [jnp.where(big_rows == big_cols, 1.0, 0.0) - part[:, 0:HEAD] for part in pushed]
    for index, (item, head) in enumerate(pairs):
        here = slice(item * GROUP, (item + 1) * GROUP)
        solved_ref[item, head] = solved[index]
        square_ref[item, head, :, 0:GROUP] = inverses[index]
        square_ref[item, head, :, GROUP : 2 * GROUP] = scores[index]
        reach_ref[here, head_lanes(head)] = scale * (queries[index] - mixed[index][:, 0:HEAD])
        zero_out_ref[here, head_lanes(head)] = scale * mixed[index][:, HEAD:]
        step_ref[item, head] = steps[index]
        fresh_ref[item, head] = pushed[index][:, HEAD:]
    now = [running[head] for head in range(heads)]
    for item in range(batch):
        first = item * heads
        moved = [mul(steps[first + head], now[head] * keeps[item]) for head in range(heads)]
        now = [
            jnp.concatenate(
                [moved[head][:, 0:HEAD], moved[head][:, HEAD:] + pushed[first + head][:, HEAD:]],
                axis=1,
            )
            for head in range(heads)
        ]
    for head in range(heads):
        running[head] = now[head]
    total_ref[...] = running[...]


def outputs_kernel(
    heads,
    batch,
    keep_ref,
    incoming_ref,
    step_ref,
    fresh_ref,
    reach_ref,
    zero_out_ref,
    gain_ref,
    state_ref,
    mixed_ref,
    normed_ref,
    running,
):
    turn = pl.program_id(0)

    @pl.when(turn == 0)
    def _():
        running[...] = incoming_ref[...]

    now = [running[head] for head in range(heads)]
    states = []
    for item in range(batch):
        keep = keep_ref[turn * batch + item]
        now = [state * keep for state in now]
        states.append(now)
        now = [
            mul(step_ref[item, head], now[head]) + fresh_ref[item, head] for head in range(heads)
        ]
    for head in range(heads):
        running[head] = now[head]
    for item in range(batch):
        here = slice(item * GROUP, (item + 1) * GROUP)
        outs = [
            mul(reach_ref[here, head_lanes(head)], states[item][head])
            + zero_out_ref[here, head_lanes(head)]
            for head in range(heads)
        ]
        for head, mixed in enumerate(outs):
            state_ref[item, head] = states[item][head]
            mixed_ref[here, head_lanes(head)] = mixed
            inverse_rms = lax.rsqrt(jnp.mean(mixed * mixed, axis=-1, keepdims=True) + EPSILON)
            normed_ref[here, head_lanes(head)] = (mixed * inverse_rms * gain_ref[...]).astype(
                jnp.bfloat16
            )


def tail_kernel(
    heads,
    batch,
    keep_ref,
    d_normed_ref,
    mixed_ref,
    gain_ref,
    step_ref,
    reach_ref,
    d_mixed_ref,
    d_state_ref,
    d_gain_ref,
    running,
):
    turn = pl.num_programs(0) - 1 - pl.program_id(0)

    @pl.when(pl.program_id(0) == 0)
    def _():
        running[...] = jnp.zeros_like(running)
        d_gain_ref[...] = jnp.zeros_like(d_gain_ref)

    gain_sum = jnp.zeros((1, HEAD), jnp.float32)
    pulled = []
    for item in range(batch):
        here = slice(item * GROUP, (item + 1) * GROUP)
        grads = []
        for head in range(heads):
            mixed = mixed_ref[here, head_lanes(head)]
            d_normed = d_normed_ref[here, head_lanes(head)]
            inverse_rms = lax.rsqrt(jnp.mean(mixed * mixed, axis=-1, keepdims=True) + EPSILON)
            unit = mixed * inverse_rms
            gain_sum = gain_sum + jnp.sum(d_normed * unit, axis=0, keepdims=True)
            d_unit = d_normed * gain_ref[...]
            d_mixed = inverse_rms * (
                d_unit - unit * jnp.mean(d_unit * unit, axis=-1, keepdims=True)
            )
            d_mixed_ref[here, head_lanes(head)] = d_mixed
            grads.append(d_mixed)
        pulled.append(
            [mul(reach_ref[here, head_lanes(head)].T, grads[head]) for head in range(heads)]
        )
    now = [running[head] for head in range(heads)]
    for item in reversed(range(batch)):
        keep = keep_ref[turn * batch + item]
        now = [
            keep * (mul(step_ref[item, head].T, now[head]) + pulled[item][head])
            for head in range(heads)
        ]
    for head in range(heads):
        running[head] = now[head]
    d_gain_ref[...] += gain_sum
    d_state_ref[...] = running[...]


def back_kernel(
    heads,
    batch,
    keep_ref,
    outgoing_ref,
    pre_ref,
    edge_ref,
    logit_ref,
    taps_ref,
    conv_ref,
    solved_ref,
    square_ref,
    step_ref,
    reach_ref,
    state_ref,
    d_mixed_ref,
    d_pre_ref,
    d_tail_ref,
    d_edge_ref,
    d_taps_ref,
    d_history,
    edge_history,
    running,
):
    count = pl.num_programs(0)
    turn = count - 1 - pl.program_id(0)
    scale = HEAD**-0.5
    rows, cols = grid_indices(GROUP)
    pairs = [(item, head) for item in range(batch) for head in range(heads)]
    indices = range(len(pairs))
    keeps = [keep_ref[turn * batch + item] for item in range(batch)]

    @pl.when(pl.program_id(0) == 0)
    def _():
        running[...] = outgoing_ref[...]
        d_history[batch - 1, GROUP : GROUP + 8, :] = jnp.zeros(
            (8, d_history.shape[2]), jnp.float32
        )
        d_taps_ref[...] = jnp.zeros_like(d_taps_ref)

    @pl.when(pl.program_id(0) > 0)
    def _():
        d_history[batch - 1, GROUP : GROUP + 8, :] = (
            d_history[0, 0:8, :] * keep_ref[(turn + 1) * batch]
        )

    def spot(item):
        return slice(item * GROUP, (item + 1) * GROUP)

    def act_of(item, column):
        conv = conv_ref[spot(item), head_lanes(column)]
        return conv * sigmoid(conv)

    def slope_of(item, column):
        conv = conv_ref[spot(item), head_lanes(column)]
        gate = sigmoid(conv)
        return gate * (1.0 + conv * (1.0 - gate))

    def d_unit(unit, inverse_norm, grad):
        return inverse_norm * (grad - unit * jnp.sum(unit * grad, axis=-1, keepdims=True))

    d_mixed = [d_mixed_ref[spot(item), head_lanes(head)] for item, head in pairs]
    pulled = [
        mul(reach_ref[spot(item), head_lanes(head)].T, d_mixed[index])
        for index, (item, head) in enumerate(pairs)
    ]
    d_states = [None] * len(pairs)
    now = [running[head] for head in range(heads)]
    for item in reversed(range(batch)):
        first = item * heads
        d_states[first : first + heads] = now
        now = [
            keeps[item] * (mul(step_ref[item, head].T, now[head]) + pulled[first + head])
            for head in range(heads)
        ]
    for head in range(heads):
        running[head] = now[head]

    d_out = [scale * grad for grad in d_mixed]
    states = [state_ref[item, head] for item, head in pairs]
    solved = [solved_ref[item, head] for item, head in pairs]
    scores = [square_ref[item, head, :, GROUP : 2 * GROUP] for item, head in pairs]
    acts = [act_of(item, heads + head) for item, head in pairs]
    key_scales = [unit_scale(act) for act in acts]
    keys = [act * size for act, size in zip(acts, key_scales)]
    fresh = [
        solved[index][:, HEAD:] - quick(solved[index][:, 0:HEAD], states[index])
        for index in indices
    ]
    d_fresh = [
        quick(scores[index].T, d_out[index]) + quick(keys[index], d_states[index])
        for index in indices
    ]
    d_scores = [
        jnp.where(rows >= cols, quick_nt(d_out[index], fresh[index]), 0.0) for index in indices
    ]
    d_solved = [
        jnp.concatenate([-quick_nt(d_fresh[index], states[index]), d_fresh[index]], axis=1)
        for index in indices
    ]
    d_right = [
        quick(square_ref[item, head, :, 0:GROUP].T, d_solved[index])
        for index, (item, head) in enumerate(pairs)
    ]
    d_queries = [
        quick_nt(d_out[index], states[index]) + quick(d_scores[index], keys[index])
        for index in indices
    ]
    acts = [act_of(item, head) for item, head in pairs]
    query_scales = [unit_scale(act) for act in acts]
    queries = [act * size for act, size in zip(acts, query_scales)]
    d_keys = [
        quick(d_scores[index].T, queries[index]) + quick_nt(fresh[index], d_states[index])
        for index in indices
    ]
    d_strict = [
        jnp.where(rows > cols, -quick_nt(d_right[index], solved[index]), 0.0) for index in indices
    ]
    strengths = [
        sigmoid(logit_ref[spot(item), head : head + 1]) for item, head in pairs
    ]
    overlaps = [quick_nt(key, key) for key in keys]
    both = [
        strengths[index] * d_strict[index] + (strengths[index] * d_strict[index]).T
        for index in indices
    ]
    d_keys = [
        d_keys[index]
        + strengths[index] * d_right[index][:, 0:HEAD]
        + quick(both[index], keys[index])
        for index in indices
    ]
    d_logits = []
    for index, (item, head) in enumerate(pairs):
        strength = strengths[index]
        value = act_of(item, 2 * heads + head)
        d_strength = (
            jnp.sum(d_right[index][:, 0:HEAD] * keys[index], axis=-1, keepdims=True)
            + jnp.sum(d_right[index][:, HEAD:] * value, axis=-1, keepdims=True)
            + jnp.sum(d_strict[index] * overlaps[index], axis=-1, keepdims=True)
        )
        d_logits.append(d_strength * strength * (1.0 - strength))
        for column, grad in (
            (head, d_unit(queries[index], query_scales[index], d_queries[index])),
            (heads + head, d_unit(keys[index], key_scales[index], d_keys[index])),
            (2 * heads + head, strength * d_right[index][:, HEAD:]),
        ):
            d_history[item, 0:GROUP, head_lanes(column)] = grad * slope_of(item, column)

    spread = lax.broadcasted_iota(jnp.int32, (GROUP, HEAD), 1)
    for item in range(batch):
        placed = jnp.zeros((GROUP, HEAD), jnp.float32)
        for head in range(heads):
            placed = jnp.where(spread == head, d_logits[item * heads + head], placed)
        d_pre_ref[spot(item), 3 * heads * HEAD :] = placed.astype(jnp.bfloat16)

    for item in reversed(range(batch - 1)):
        d_history[item, GROUP : GROUP + 8, :] = d_history[item + 1, 0:8, :] * keeps[item + 1]
    for column in range(3 * heads):
        lanes = head_lanes(column)
        for item in range(batch):
            pre = pre_ref[spot(item), lanes].astype(jnp.float32)
            total = jnp.zeros((GROUP, HEAD), jnp.float32)
            for tap in range(TAPS):
                part = d_history[item, TAPS - 1 - tap : TAPS - 1 - tap + GROUP, lanes]
                total = total + taps_ref[tap : tap + 1, lanes] * part
                d_taps_ref[tap : tap + 1, lanes] += jnp.sum(pre * part, axis=0, keepdims=True)
            d_pre_ref[spot(item), lanes] = total.astype(jnp.bfloat16)
        d_tail_ref[:, lanes] = jnp.where(
            turn == count - 1, total[GROUP - 8 :, :], d_tail_ref[:, lanes]
        )

    @pl.when(turn == 0)
    def _():
        edge_history[0:8, :] = jnp.zeros((8, edge_history.shape[1]), jnp.float32)
        edge_history[8:16, :] = d_history[0, 0:8, :] * keeps[0]
        total = jnp.zeros(d_edge_ref.shape, jnp.float32)
        for tap in range(TAPS):
            part = edge_history[TAPS - 1 - tap : TAPS - 1 - tap + 8, :]
            total = total + taps_ref[tap : tap + 1, :] * part
            d_taps_ref[tap : tap + 1, :] += jnp.sum(edge_ref[...] * part, axis=0, keepdims=True)
        d_edge_ref[...] = total


def passed_along(value, axis, by):
    count = lax.axis_size(axis)
    pairs = [(i, i + by) for i in range(count) if 0 <= i + by < count]
    return lax.ppermute(value, axis, pairs)


def adamw(weight, first, second, grad, rate, decay):
    first = FIRST_DECAY * first + (1.0 - FIRST_DECAY) * grad
    second = SECOND_DECAY * second + (1.0 - SECOND_DECAY) * grad * grad
    stepped = (
        first
        / (1.0 - FIRST_DECAY**STEP)
        / (jnp.sqrt(second / (1.0 - SECOND_DECAY**STEP)) + ADAM_EPSILON)
    )
    return (weight - rate * (stepped + decay * weight), first, second)


def f32(*shape):
    return jax.ShapeDtypeStruct(shape, jnp.float32)


def bf16(*shape):
    return jax.ShapeDtypeStruct(shape, jnp.bfloat16)


class Rule:
    def __init__(self, keep, heads, row_count):
        self.keep, self.heads, self.rows = keep, heads, row_count
        self.count = row_count // GROUP
        self.params = pltpu.CompilerParams(
            dimension_semantics=("arbitrary",), vmem_limit_bytes=48 * 1024 * 1024
        )

    def rows_spec(self, width, batch, back=False):
        last = self.count // batch - 1
        if back:
            return pl.BlockSpec((batch * GROUP, width), lambda n: (last - n, 0))
        return pl.BlockSpec((batch * GROUP, width), lambda n: (n, 0))

    def block_spec(self, shape, batch, back=False):
        last = self.count // batch - 1
        if back:
            return pl.BlockSpec((batch,) + shape, lambda n: (last - n, 0, 0, 0))
        return pl.BlockSpec((batch,) + shape, lambda n: (n, 0, 0, 0))

    def whole(self, *shape):
        return pl.BlockSpec(shape, lambda n: (0,) * len(shape))

    def smem(self):
        return pl.BlockSpec(memory_space=pltpu.SMEM)

    def maps(self, pre, edge, logits, taps):
        heads, rows, count, inner = self.heads, self.rows, self.count, self.heads * HEAD
        return pl.pallas_call(
            functools.partial(maps_kernel, heads, MAPS_BATCH),
            grid=(count // MAPS_BATCH,),
            in_specs=[
                self.smem(),
                self.rows_spec(3 * inner, MAPS_BATCH),
                self.whole(8, 3 * inner),
                self.rows_spec(heads, MAPS_BATCH),
                self.whole(TAPS, 3 * inner),
            ],
            out_specs=[
                self.rows_spec(3 * inner, MAPS_BATCH),
                self.block_spec((heads, GROUP, 2 * HEAD), MAPS_BATCH),
                self.block_spec((heads, GROUP, 2 * GROUP), MAPS_BATCH),
                self.block_spec((heads, HEAD, HEAD), MAPS_BATCH),
                self.block_spec((heads, HEAD, HEAD), MAPS_BATCH),
                self.rows_spec(inner, MAPS_BATCH),
                self.rows_spec(inner, MAPS_BATCH),
                self.whole(heads, HEAD, 2 * HEAD),
            ],
            out_shape=[
                f32(rows, 3 * inner),
                f32(count, heads, GROUP, 2 * HEAD),
                f32(count, heads, GROUP, 2 * GROUP),
                f32(count, heads, HEAD, HEAD),
                f32(count, heads, HEAD, HEAD),
                f32(rows, inner),
                f32(rows, inner),
                f32(heads, HEAD, 2 * HEAD),
            ],
            scratch_shapes=[
                pltpu.VMEM((MAPS_BATCH, GROUP + 8, 3 * inner), jnp.float32),
                pltpu.VMEM((heads, HEAD, 2 * HEAD), jnp.float32),
            ],
            compiler_params=self.params,
            cost_estimate=busy(35),
            name="delta_maps",
        )(self.keep, pre, edge, logits, taps)

    def outputs(self, incoming, step, fresh, reach, zero_out, gain):
        heads, rows, count, inner = self.heads, self.rows, self.count, self.heads * HEAD
        return pl.pallas_call(
            functools.partial(outputs_kernel, heads, CHAIN_BATCH),
            grid=(count // CHAIN_BATCH,),
            in_specs=[
                self.smem(),
                self.whole(heads, HEAD, HEAD),
                self.block_spec((heads, HEAD, HEAD), CHAIN_BATCH),
                self.block_spec((heads, HEAD, HEAD), CHAIN_BATCH),
                self.rows_spec(inner, CHAIN_BATCH),
                self.rows_spec(inner, CHAIN_BATCH),
                self.whole(1, HEAD),
            ],
            out_specs=[
                self.block_spec((heads, HEAD, HEAD), CHAIN_BATCH),
                self.rows_spec(inner, CHAIN_BATCH),
                self.rows_spec(inner, CHAIN_BATCH),
            ],
            out_shape=[f32(count, heads, HEAD, HEAD), f32(rows, inner), bf16(rows, inner)],
            scratch_shapes=[pltpu.VMEM((heads, HEAD, HEAD), jnp.float32)],
            compiler_params=self.params,
            cost_estimate=busy(9),
            name="delta_outputs",
        )(self.keep, incoming, step, fresh, reach, zero_out, gain)

    def tail(self, d_normed, mixed, gain, step, reach):
        heads, rows, count, inner = self.heads, self.rows, self.count, self.heads * HEAD
        return pl.pallas_call(
            functools.partial(tail_kernel, heads, CHAIN_BATCH),
            grid=(count // CHAIN_BATCH,),
            in_specs=[
                self.smem(),
                self.rows_spec(inner, CHAIN_BATCH, True),
                self.rows_spec(inner, CHAIN_BATCH, True),
                self.whole(1, HEAD),
                self.block_spec((heads, HEAD, HEAD), CHAIN_BATCH, True),
                self.rows_spec(inner, CHAIN_BATCH, True),
            ],
            out_specs=[
                self.rows_spec(inner, CHAIN_BATCH, True),
                self.whole(heads, HEAD, HEAD),
                self.whole(1, HEAD),
            ],
            out_shape=[f32(rows, inner), f32(heads, HEAD, HEAD), f32(1, HEAD)],
            scratch_shapes=[pltpu.VMEM((heads, HEAD, HEAD), jnp.float32)],
            compiler_params=self.params,
            cost_estimate=busy(11),
            name="delta_tail",
        )(self.keep, d_normed, mixed, gain, step, reach)

    def back(self, outgoing, pre, edge, logits, taps, conv, solved, square, step, reach, state, d_mixed):
        heads, rows, count, inner = self.heads, self.rows, self.count, self.heads * HEAD
        return pl.pallas_call(
            functools.partial(back_kernel, heads, BACK_BATCH),
            grid=(count // BACK_BATCH,),
            in_specs=[
                self.smem(),
                self.whole(heads, HEAD, HEAD),
                self.rows_spec(3 * inner, BACK_BATCH, True),
                self.whole(8, 3 * inner),
                self.rows_spec(heads, BACK_BATCH, True),
                self.whole(TAPS, 3 * inner),
                self.rows_spec(3 * inner, BACK_BATCH, True),
                self.block_spec((heads, GROUP, 2 * HEAD), BACK_BATCH, True),
                self.block_spec((heads, GROUP, 2 * GROUP), BACK_BATCH, True),
                self.block_spec((heads, HEAD, HEAD), BACK_BATCH, True),
                self.rows_spec(inner, BACK_BATCH, True),
                self.block_spec((heads, HEAD, HEAD), BACK_BATCH, True),
                self.rows_spec(inner, BACK_BATCH, True),
            ],
            out_specs=[
                self.rows_spec(3 * inner + HEAD, BACK_BATCH, True),
                self.whole(8, 3 * inner),
                self.whole(8, 3 * inner),
                self.whole(TAPS, 3 * inner),
            ],
            out_shape=[
                bf16(rows, 3 * inner + HEAD),
                f32(8, 3 * inner),
                f32(8, 3 * inner),
                f32(TAPS, 3 * inner),
            ],
            scratch_shapes=[
                pltpu.VMEM((BACK_BATCH, GROUP + 8, 3 * inner), jnp.float32),
                pltpu.VMEM((16, 3 * inner), jnp.float32),
                pltpu.VMEM((heads, HEAD, HEAD), jnp.float32),
            ],
            compiler_params=self.params,
            cost_estimate=busy(45),
            name="delta_back",
        )(
            self.keep, outgoing, pre, edge, logits, taps, conv, solved, square, step, reach, state,
            d_mixed,
        )


def rms_unit(values):
    return values * lax.rsqrt(jnp.mean(values * values, axis=-1, keepdims=True) + EPSILON)


def rms_back(values, gain_vec, grad):
    inverse_rms = lax.rsqrt(jnp.mean(values * values, axis=-1, keepdims=True) + EPSILON)
    unit = values * inverse_rms
    d_unit = grad * gain_vec
    d_values = inverse_rms * (d_unit - unit * jnp.mean(d_unit * unit, axis=-1, keepdims=True))
    return d_values, jnp.sum(grad * unit, axis=0)


def low(values):
    return values.astype(jnp.bfloat16)


def product(left, right, dims=((1,), (0,))):
    return lax.dot_general(left, right, (dims, ((), ())), preferred_element_type=jnp.float32)


def rows_summed(partial):
    return lax.psum_scatter(low(partial), "shard", scatter_dimension=0, tiled=True)


def rows_joined(rows):
    return lax.all_gather(rows, "shard", axis=0, tiled=True)


def seq_summed(grad, dim):
    return lax.psum_scatter(grad, "seq", scatter_dimension=dim, tiled=True)


def one_hot(indices, size):
    return (jnp.arange(size, dtype=jnp.int32)[:, None] == indices[None, :]).astype(jnp.bfloat16)


def moved(matrix, values):
    return low(product(matrix, values))


def moved_back(matrix, values):
    return low(product(matrix, values, ((0,), (0,))))


def busy(micros):
    return pl.CostEstimate(flops=micros * BUSY_FLOPS, bytes_accessed=0, transcendentals=0)


def ends(count):
    me = lax.axis_index("shard")
    return me, me > 0, me < count - 1


def meet_neighbours(count):
    me, has_left, has_right = ends(count)
    barrier = pltpu.get_barrier_semaphore()

    @pl.when(has_left)
    def _():
        pl.semaphore_signal(barrier, inc=1, device_id={"shard": me - 1}, device_id_type=MESH)

    @pl.when(has_right)
    def _():
        pl.semaphore_signal(barrier, inc=1, device_id={"shard": me + 1}, device_id_type=MESH)

    pl.semaphore_wait(barrier, has_left.astype(jnp.int32) + has_right.astype(jnp.int32))


def join_kernel(count, parts, own_ref, out_ref, own_sem, send_sem, recv_sem):
    me, has_left, has_right = ends(count)
    size = own_ref.shape[0] // parts
    meet_neighbours(count)
    own_copy = pltpu.make_async_copy(own_ref, out_ref.at[me], own_sem)
    own_copy.start()

    def piece_copy(way, block, part, source, target):
        rows = pl.ds(part * size, size)
        return pltpu.make_async_remote_copy(
            src_ref=source.at[rows] if source is own_ref else source.at[block, rows],
            dst_ref=out_ref.at[block, rows],
            send_sem=send_sem.at[way, block, part],
            recv_sem=recv_sem.at[block, part],
            device_id={"shard": target},
            device_id_type=MESH,
        )

    def each(action):
        for far in range(count):
            for part in range(parts):
                for way, present, onward, block, target in (
                    (0, me >= far, has_right, me - far, me + 1),
                    (1, me + far < count, has_left, me + far, me - 1),
                ):
                    action(far, part, way, present, onward, block, target)

    def start(far, part, way, present, onward, block, target):
        source = own_ref if far == 0 else out_ref

        if far:

            @pl.when(present)
            def _():
                piece_copy(way, block, part, out_ref, target).wait_recv()

        @pl.when(present & onward)
        def _():
            piece_copy(way, block, part, source, target).start()

    def finish(far, part, way, present, onward, block, target):
        source = own_ref if far == 0 else out_ref

        @pl.when(present & onward)
        def _():
            piece_copy(way, block, part, source, target).wait_send()

    each(start)
    each(finish)
    own_copy.wait()


def join_rows(rows, count, ident, parts=4):
    size, width = rows.shape
    return pl.pallas_call(
        functools.partial(join_kernel, count, parts),
        out_shape=jax.ShapeDtypeStruct((count, size, width), rows.dtype),
        in_specs=[pl.BlockSpec(memory_space=pl.ANY)],
        out_specs=pl.BlockSpec(memory_space=pl.ANY),
        scratch_shapes=[
            pltpu.SemaphoreType.DMA(()),
            pltpu.SemaphoreType.DMA((2, count, parts)),
            pltpu.SemaphoreType.DMA((count, parts)),
        ],
        compiler_params=pltpu.CompilerParams(collective_id=ident, has_side_effects=True),
        cost_estimate=busy(70),
        name="join_rows",
    )(rows).reshape(count * size, width)


def swap_kernel(count, to_columns, in_ref, out_ref, own_sem, send_sem, recv_sem):
    me = lax.axis_index("shard")
    barrier = pltpu.get_barrier_semaphore()
    for hop in range(1, count):
        other = lax.rem(me + hop, count)
        pl.semaphore_signal(barrier, inc=1, device_id={"shard": other}, device_id_type=MESH)
    pl.semaphore_wait(barrier, count - 1)
    if to_columns:
        width = in_ref.shape[2]
    else:
        width = out_ref.shape[2]

    def columns(ref, index):
        return ref.at[:, pl.ds(pl.multiple_of(index * width, width), width)]

    def source(block):
        return in_ref.at[block] if to_columns else columns(in_ref, block)

    def landing(block):
        return columns(out_ref, block) if to_columns else out_ref.at[block]

    own_copy = pltpu.make_async_copy(source(me), landing(me), own_sem)
    own_copy.start()

    def block_copy(hop):
        other = lax.rem(me + hop, count)
        return pltpu.make_async_remote_copy(
            src_ref=source(other),
            dst_ref=landing(me),
            send_sem=send_sem.at[hop],
            recv_sem=recv_sem.at[hop],
            device_id={"shard": other},
            device_id_type=MESH,
        )

    for hop in range(1, count):
        block_copy(hop).start()
    for hop in range(1, count):
        block_copy(hop).wait()
    own_copy.wait()


def swap_blocks(value, count, ident, to_columns):
    if to_columns:
        _, size, width = value.shape
        shape = (size, count * width)
    else:
        size, width = value.shape[0], value.shape[1] // count
        shape = (count, size, width)
    return pl.pallas_call(
        functools.partial(swap_kernel, count, to_columns),
        out_shape=jax.ShapeDtypeStruct(shape, value.dtype),
        in_specs=[pl.BlockSpec(memory_space=pl.ANY)],
        out_specs=pl.BlockSpec(memory_space=pl.ANY),
        scratch_shapes=[
            pltpu.SemaphoreType.DMA(()),
            pltpu.SemaphoreType.DMA((count,)),
            pltpu.SemaphoreType.DMA((count,)),
        ],
        compiler_params=pltpu.CompilerParams(collective_id=ident, has_side_effects=True),
        cost_estimate=busy(23),
        name="swap_blocks",
    )(value)


def relay_kernel(heads, hops, back, total_ref, fresh_ref, out_ref, sending, landing, send_sem, recv_sem):
    count = lax.axis_size("seq")
    me = lax.axis_index("seq")
    if back:
        follows, precedes, target, origin = me < count - 1, me > 0, me - 1, me + 1
    else:
        follows, precedes, target, origin = me > 0, me < count - 1, me + 1, me - 1
    barrier = pltpu.get_barrier_semaphore()

    @pl.when(follows)
    def _():
        pl.semaphore_signal(barrier, inc=1, device_id={"seq": origin}, device_id_type=MESH)

    @pl.when(precedes)
    def _():
        pl.semaphore_signal(barrier, inc=1, device_id={"seq": target}, device_id_type=MESH)

    pl.semaphore_wait(barrier, follows.astype(jnp.int32) + precedes.astype(jnp.int32))

    def state_copy(hop, head):
        return pltpu.make_async_remote_copy(
            src_ref=sending.at[hop, head],
            dst_ref=landing.at[hop, head],
            send_sem=send_sem.at[hop, head],
            recv_sem=recv_sem.at[hop, head],
            device_id={"seq": target},
            device_id_type=MESH,
        )

    for hop in range(hops):
        for head in range(heads):
            fresh = fresh_ref[head]
            if hop == 0:
                sending[hop, head] = low(fresh)
            else:

                @pl.when(follows)
                def _():
                    state_copy(hop - 1, head).wait_recv()
                    step = total_ref[head, :, 0:HEAD]
                    step = step.T if back else step
                    sending[hop, head] = low(
                        fresh + mul(step, landing[hop - 1, head].astype(jnp.float32))
                    )

                @pl.when(jnp.logical_not(follows))
                def _():
                    sending[hop, head] = low(fresh)

            @pl.when(precedes)
            def _():
                state_copy(hop, head).start()

    for head in range(heads):

        @pl.when(follows)
        def _():
            state_copy(hops - 1, head).wait_recv()
            out_ref[head] = landing[hops - 1, head].astype(jnp.float32)

        @pl.when(jnp.logical_not(follows))
        def _():
            out_ref[head] = jnp.zeros((HEAD, HEAD), jnp.float32)

    @pl.when(precedes)
    def _():
        for hop in range(hops):
            for head in range(heads):
                state_copy(hop, head).wait_send()


def relayed(total, fresh, hops, back, ident):
    heads = fresh.shape[0]
    return pl.pallas_call(
        functools.partial(relay_kernel, heads, hops, back),
        out_shape=jax.ShapeDtypeStruct((heads, HEAD, HEAD), jnp.float32),
        in_specs=[pl.BlockSpec(memory_space=pltpu.VMEM)] * 2,
        out_specs=pl.BlockSpec(memory_space=pltpu.VMEM),
        scratch_shapes=[
            pltpu.VMEM((hops, heads, HEAD, HEAD), jnp.bfloat16),
            pltpu.VMEM((hops, heads, HEAD, HEAD), jnp.bfloat16),
            pltpu.SemaphoreType.DMA((hops, heads)),
            pltpu.SemaphoreType.DMA((hops, heads)),
        ],
        compiler_params=pltpu.CompilerParams(collective_id=ident, has_side_effects=True),
        cost_estimate=busy(15),
        name="relay_back" if back else "relay",
    )(total, fresh)


def last_join_kernel(
    count,
    parts,
    shared,
    own_ref,
    small_ref,
    out_ref,
    small_out,
    seq_slots,
    layer_slots,
    own_sem,
    send_sem,
    recv_sem,
    seq_send,
    seq_recv,
    layer_send,
    layer_recv,
):
    me, has_left, has_right = ends(count)
    size = own_ref.shape[0] // parts
    devices = lax.axis_size("seq")
    here = lax.axis_index("seq")
    barrier = pltpu.get_barrier_semaphore()
    for hop in range(1, devices):
        other = lax.rem(here + hop, devices)
        pl.semaphore_signal(barrier, inc=1, device_id={"seq": other}, device_id_type=MESH)
    for hop in range(1, count):
        other = lax.rem(me + hop, count)
        pl.semaphore_signal(barrier, inc=1, device_id={"shard": other}, device_id_type=MESH)
    pl.semaphore_wait(barrier, devices + count - 2)
    own_copy = pltpu.make_async_copy(own_ref, out_ref.at[me], own_sem)
    own_copy.start()

    def seq_copy(hop):
        return pltpu.make_async_remote_copy(
            src_ref=small_ref,
            dst_ref=seq_slots.at[here],
            send_sem=seq_send.at[hop],
            recv_sem=seq_recv.at[hop],
            device_id={"seq": lax.rem(here + hop, devices)},
            device_id_type=MESH,
        )

    def layer_copy(hop):
        return pltpu.make_async_remote_copy(
            src_ref=small_out.at[pl.ds(0, shared)],
            dst_ref=layer_slots.at[me],
            send_sem=layer_send.at[hop],
            recv_sem=layer_recv.at[hop],
            device_id={"shard": lax.rem(me + hop, count)},
            device_id_type=MESH,
        )

    def piece_copy(way, block, part, source, target):
        rows = pl.ds(part * size, size)
        return pltpu.make_async_remote_copy(
            src_ref=source.at[rows] if source is own_ref else source.at[block, rows],
            dst_ref=out_ref.at[block, rows],
            send_sem=send_sem.at[way, block, part],
            recv_sem=recv_sem.at[block, part],
            device_id={"shard": target},
            device_id_type=MESH,
        )

    def each(far, action):
        for part in range(parts):
            for way, present, onward, block, target in (
                (0, me >= far, has_right, me - far, me + 1),
                (1, me + far < count, has_left, me + far, me - 1),
            ):
                action(far, part, way, present, onward, block, target)

    def start(far, part, way, present, onward, block, target):
        if far:

            @pl.when(present)
            def _():
                piece_copy(way, block, part, out_ref, target).wait_recv()

        @pl.when(present & onward)
        def _():
            piece_copy(way, block, part, out_ref if far else own_ref, target).start()

    def finish(far, part, way, present, onward, block, target):
        @pl.when(present & onward)
        def _():
            piece_copy(way, block, part, out_ref if far else own_ref, target).wait_send()

    def seq_start(hop, carry):
        seq_copy(hop).start()
        return carry

    def seq_finish(hop, carry):
        seq_copy(hop).wait()
        return carry

    lax.fori_loop(1, devices, seq_start, 0)
    seq_slots[here] = small_ref[...]
    each(0, start)
    lax.fori_loop(1, devices, seq_finish, 0)
    total = seq_slots[0]
    for index in range(1, devices):
        total = total + seq_slots[index]
    small_out[...] = total
    for hop in range(1, count):
        layer_copy(hop).start()
    layer_slots[me] = total[0:shared]
    for far in range(1, count):
        each(far, start)
    for hop in range(1, count):
        layer_copy(hop).wait()
    total = layer_slots[0]
    for index in range(1, count):
        total = total + layer_slots[index]
    small_out[0:shared, :] = total
    for far in range(count):
        each(far, finish)
    own_copy.wait()


def join_rows_and_sum(rows, small, shared, count, ident, parts=4):
    size, width = rows.shape
    devices = lax.axis_size("seq")
    joined, summed = pl.pallas_call(
        functools.partial(last_join_kernel, count, parts, shared),
        out_shape=[jax.ShapeDtypeStruct((count, size, width), rows.dtype), f32(*small.shape)],
        in_specs=[pl.BlockSpec(memory_space=pl.ANY), pl.BlockSpec(memory_space=pltpu.VMEM)],
        out_specs=[pl.BlockSpec(memory_space=pl.ANY), pl.BlockSpec(memory_space=pltpu.VMEM)],
        scratch_shapes=[
            pltpu.VMEM((devices,) + small.shape, jnp.float32),
            pltpu.VMEM((count, shared, small.shape[1]), jnp.float32),
            pltpu.SemaphoreType.DMA(()),
            pltpu.SemaphoreType.DMA((2, count, parts)),
            pltpu.SemaphoreType.DMA((count, parts)),
            pltpu.SemaphoreType.DMA((devices,)),
            pltpu.SemaphoreType.DMA((devices,)),
            pltpu.SemaphoreType.DMA((count,)),
            pltpu.SemaphoreType.DMA((count,)),
        ],
        compiler_params=pltpu.CompilerParams(collective_id=ident, has_side_effects=True),
        cost_estimate=busy(70),
        name="join_rows_and_sum",
    )(rows, small)
    return joined.reshape(count * size, width), summed


def start_kernel(
    x_ref,
    place_ref,
    out_ref,
    x_got,
    place_got,
    out_got,
    own_sem,
    x_send,
    x_recv,
    place_send,
    place_recv,
    out_send,
    out_recv,
):
    count, me = lax.axis_size("shard"), lax.axis_index("shard")
    devices, here = lax.axis_size("seq"), lax.axis_index("seq")
    barrier = pltpu.get_barrier_semaphore()

    def greet(hop, carry):
        other = lax.rem(here + hop, devices)
        pl.semaphore_signal(barrier, inc=1, device_id={"seq": other}, device_id_type=MESH)
        return carry

    lax.fori_loop(1, devices, greet, 0)
    for hop in range(1, count):
        other = lax.rem(me + hop, count)
        pl.semaphore_signal(barrier, inc=1, device_id={"shard": other}, device_id_type=MESH)
    own_copies = [
        pltpu.make_async_copy(x_ref.at[here], x_got.at[here], own_sem.at[0]),
        pltpu.make_async_copy(place_ref.at[here], place_got.at[here], own_sem.at[1]),
        pltpu.make_async_copy(out_ref, out_got.at[me], own_sem.at[2]),
    ]
    for copy in own_copies:
        copy.start()
    pl.semaphore_wait(barrier, devices + count - 2)

    def seq_copies(hop):
        other = lax.rem(here + hop, devices)
        return [
            pltpu.make_async_remote_copy(
                src_ref=source.at[other],
                dst_ref=target.at[here],
                send_sem=send.at[hop],
                recv_sem=recv.at[hop],
                device_id={"seq": other},
                device_id_type=MESH,
            )
            for source, target, send, recv in (
                (x_ref, x_got, x_send, x_recv),
                (place_ref, place_got, place_send, place_recv),
            )
        ]

    def out_copy(hop):
        return pltpu.make_async_remote_copy(
            src_ref=out_ref,
            dst_ref=out_got.at[me],
            send_sem=out_send.at[hop],
            recv_sem=out_recv.at[hop],
            device_id={"shard": lax.rem(me + hop, count)},
            device_id_type=MESH,
        )

    def start(hop, carry):
        for copy in seq_copies(hop):
            copy.start()
        return carry

    def finish(hop, carry):
        for copy in seq_copies(hop):
            copy.wait()
        return carry

    lax.fori_loop(1, devices, start, 0)
    for hop in range(1, count):
        out_copy(hop).start()
    lax.fori_loop(1, devices, finish, 0)
    for hop in range(1, count):
        out_copy(hop).wait()
    for copy in own_copies:
        copy.wait()


def start_exchange(rows, places, out_low, layers, ident):
    devices = rows.shape[0]
    dma = pltpu.SemaphoreType.DMA
    return pl.pallas_call(
        start_kernel,
        out_shape=[
            jax.ShapeDtypeStruct(rows.shape, rows.dtype),
            jax.ShapeDtypeStruct(places.shape, places.dtype),
            jax.ShapeDtypeStruct((layers,) + out_low.shape, out_low.dtype),
        ],
        in_specs=[pl.BlockSpec(memory_space=pl.ANY)] * 3,
        out_specs=[pl.BlockSpec(memory_space=pl.ANY)] * 3,
        scratch_shapes=[
            dma((3,)),
            dma((devices,)),
            dma((devices,)),
            dma((devices,)),
            dma((devices,)),
            dma((layers,)),
            dma((layers,)),
        ],
        compiler_params=pltpu.CompilerParams(collective_id=ident, has_side_effects=True),
        cost_estimate=busy(20),
        name="start_exchange",
    )(rows, places, out_low)


def total_join_kernel(
    count,
    parts,
    grads_ref,
    weights_ref,
    rows_ref,
    own_ref,
    out_ref,
    joined_ref,
    weigh_ref,
    grads,
    weights,
    rows_in,
    part_ref,
    weighed,
    from_left,
    from_right,
    load_sem,
    weigh_sem,
    own_sem,
    send_sem,
    recv_sem,
    join_send,
    join_recv,
):
    me, has_left, has_right = ends(count)
    size = out_ref.shape[0] // parts
    tile = 2 * HEAD
    width = out_ref.shape[1]
    loads = [
        pltpu.make_async_copy(source, target, load_sem.at[index])
        for index, (source, target) in enumerate(
            ((grads_ref, grads), (weights_ref, weights), (rows_ref, rows_in))
        )
    ]
    for load in loads:
        load.start()
    meet_neighbours(count)
    own_copy = pltpu.make_async_copy(own_ref, joined_ref.at[me], own_sem)
    own_copy.start()

    def sum_copy(way, block, part, source, target):
        rows = pl.ds(part * size, size)
        landing = (from_left, from_right)[way]
        return pltpu.make_async_remote_copy(
            src_ref=source.at[block, rows],
            dst_ref=landing.at[block, rows],
            send_sem=send_sem.at[way, block, part],
            recv_sem=recv_sem.at[way, block, part],
            device_id={"shard": target},
            device_id_type=MESH,
        )

    def join_copy(way, block, part, source, target):
        rows = pl.ds(part * size, size)
        return pltpu.make_async_remote_copy(
            src_ref=source.at[rows] if source is own_ref else source.at[block, rows],
            dst_ref=joined_ref.at[block, rows],
            send_sem=join_send.at[way, block, part],
            recv_sem=join_recv.at[block, part],
            device_id={"shard": target},
            device_id_type=MESH,
        )

    def sum_way(way, block):
        if way == 0:
            return me < block, has_left, me + 1
        return me > block, has_right, me - 1

    def join_way(far, way):
        if way == 0:
            return me >= far, has_right, me - far, me + 1
        return me + far < count, has_left, me + far, me - 1

    def join_start(far, way, part):
        present, onward, block, target = join_way(far, way)
        if far:

            @pl.when(present)
            def _():
                join_copy(way, block, part, joined_ref, target).wait_recv()

        @pl.when(present & onward)
        def _():
            join_copy(way, block, part, joined_ref if far else own_ref, target).start()

    def sum_start(way, block, part):
        sends, receives, target = sum_way(way, block)
        landing = (from_left, from_right)[way]
        rows = pl.ds(part * size, size)

        @pl.when(sends & receives)
        def _():
            sum_copy(way, block, part, landing, target).wait_recv()
            landing[block, rows, :] = (
                landing[block, rows, :].astype(jnp.float32)
                + part_ref[block, rows, :].astype(jnp.float32)
            ).astype(jnp.bfloat16)
            sum_copy(way, block, part, landing, target).start()

    for part in range(parts):
        for way in range(2):
            join_start(0, way, part)
    loads[0].wait()
    loads[1].wait()

    def block_turn(turn, carry):
        block = jnp.int32(0)
        for place in range(count):
            by_distance = sorted(range(count), key=lambda other: -abs(other - place))
            for index, other in enumerate(by_distance):
                block = jnp.where((me == place) & (turn == index), other, block)

        def tile_turn(index, inner_carry):
            across = pl.ds(pl.multiple_of(index * tile, tile), tile)
            part_ref[block, :, across] = low(
                product(grads[block], weights[across, :], ((1,), (1,)))
            )
            return inner_carry

        lax.fori_loop(0, width // tile, tile_turn, 0)

        @pl.when((block > me) & jnp.logical_not(has_left))
        def _():
            for part in range(parts):
                sum_copy(0, block, part, part_ref, me + 1).start()

        @pl.when((block < me) & jnp.logical_not(has_right))
        def _():
            for part in range(parts):
                sum_copy(1, block, part, part_ref, me - 1).start()

        return carry

    lax.fori_loop(0, count, block_turn, 0)
    loads[2].wait()
    wide = weights.shape[1]
    rows_total = count * out_ref.shape[0]

    def weigh_store(turn):
        rows = pl.ds(pl.multiple_of(turn * tile, tile), tile)
        return pltpu.make_async_copy(weighed.at[rows], weigh_ref.at[rows], weigh_sem.at[turn])

    def weigh_turn(turn, carry):
        rows = pl.ds(pl.multiple_of(turn * tile, tile), tile)
        turned = rows_in[:, rows].T

        def weigh_tile(first, span):
            against = grads[:, :, pl.ds(first, span)].reshape(rows_total, span)
            weighed[rows, pl.ds(first, span)] = low(product(turned, against))

        def tile_turn(index, inner_carry):
            weigh_tile(pl.multiple_of(index * tile, tile), tile)
            return inner_carry

        lax.fori_loop(0, wide // tile, tile_turn, 0)
        if wide % tile:
            weigh_tile(wide // tile * tile, wide % tile)
        weigh_store(turn).start()
        return carry

    for step in range(count):
        if step == min(2, count - 1):
            lax.fori_loop(0, width // tile, weigh_turn, 0)
        for part in range(parts):
            if step:
                for way in range(2):
                    join_start(step, way, part)
            if step < count - 1:
                sum_start(0, count - 1 - step, part)
                sum_start(1, step, part)

    for block in range(count):

        @pl.when(me == block)
        def _():
            for part in range(parts):
                rows = pl.ds(part * size, size)
                total = part_ref[block, rows, :].astype(jnp.float32)
                if block > 0:
                    sum_copy(0, block, part, from_left, me).wait_recv()
                    total = total + from_left[block, rows, :].astype(jnp.float32)
                if block < count - 1:
                    sum_copy(1, block, part, from_right, me).wait_recv()
                    total = total + from_right[block, rows, :].astype(jnp.float32)
                out_ref[rows, :] = total

    for step in range(count):
        for part in range(parts):
            for way in range(2):
                present, onward, block, target = join_way(step, way)

                @pl.when(present & onward)
                def _():
                    source = joined_ref if step else own_ref
                    join_copy(way, block, part, source, target).wait_send()

            if step < count - 1:
                for way, block in ((0, count - 1 - step), (1, step)):
                    sends, _, target = sum_way(way, block)

                    @pl.when(sends)
                    def _():
                        sum_copy(way, block, part, part_ref, target).wait_send()

    own_copy.wait()

    def weigh_finish(turn, carry):
        weigh_store(turn).wait()
        return carry

    lax.fori_loop(0, width // tile, weigh_finish, 0)


def total_and_join(grads, weights, rows, own, count, ident, parts=4):
    size, width = own.shape
    wide = grads.shape[1]
    total, joined, weighed = pl.pallas_call(
        functools.partial(total_join_kernel, count, parts),
        out_shape=[
            jax.ShapeDtypeStruct((size, width), jnp.float32),
            jax.ShapeDtypeStruct((count, size, width), own.dtype),
            bf16(width, wide),
        ],
        in_specs=[pl.BlockSpec(memory_space=pl.ANY)] * 4,
        out_specs=[pl.BlockSpec(memory_space=pltpu.VMEM)] + [pl.BlockSpec(memory_space=pl.ANY)] * 2,
        scratch_shapes=[
            pltpu.VMEM((count, size, wide), jnp.bfloat16),
            pltpu.VMEM((width, wide), jnp.bfloat16),
            pltpu.VMEM((count * size, width), jnp.bfloat16),
            pltpu.VMEM((count, size, width), jnp.bfloat16),
            pltpu.VMEM((width, wide), jnp.bfloat16),
            pltpu.VMEM((count, size, width), jnp.bfloat16),
            pltpu.VMEM((count, size, width), jnp.bfloat16),
            pltpu.SemaphoreType.DMA((3,)),
            pltpu.SemaphoreType.DMA((width // (2 * HEAD),)),
            pltpu.SemaphoreType.DMA(()),
            pltpu.SemaphoreType.DMA((2, count, parts)),
            pltpu.SemaphoreType.DMA((2, count, parts)),
            pltpu.SemaphoreType.DMA((2, count, parts)),
            pltpu.SemaphoreType.DMA((count, parts)),
        ],
        compiler_params=pltpu.CompilerParams(
            collective_id=ident, has_side_effects=True, vmem_limit_bytes=60 * 1024 * 1024
        ),
        cost_estimate=busy(95),
        name="total_and_join",
    )(grads.reshape(count, size, wide), weights, rows, own)
    return total, joined.reshape(count * size, width), weighed


def feed_kernel(
    count,
    parts,
    own_ref,
    dy_ref,
    gate_up_ref,
    down_ref,
    down_part_out,
    grad_open_out,
    grad_down_out,
    total_ref,
    gate_up,
    down,
    dy,
    rows_all,
    hidden,
    d_both,
    partial,
    landing,
    down_part,
    open_stage,
    down_stage,
    load_sem,
    part_sem,
    open_sem,
    down_sem,
    join_send,
    join_recv,
    sum_send,
    sum_recv,
):
    me, has_left, has_right = ends(count)
    units, width = down.shape
    piece = own_ref.shape[0] // parts
    tile = 2 * HEAD
    loads = [
        pltpu.make_async_copy(gate_up_ref, gate_up, load_sem.at[0]),
        pltpu.make_async_copy(dy_ref, dy, load_sem.at[1]),
        pltpu.make_async_copy(down_ref, down, load_sem.at[2]),
    ]
    for load in loads:
        load.start()
    rows_all[me] = own_ref[...]
    meet_neighbours(count)

    def part_store(block):
        return pltpu.make_async_copy(
            down_part.at[block], down_part_out.at[block], part_sem.at[block]
        )

    def open_store(turn):
        slot = lax.rem(turn, 2)
        rows = pl.ds(pl.multiple_of(turn * tile, tile), tile)
        return pltpu.make_async_copy(
            open_stage.at[slot], grad_open_out.at[rows], open_sem.at[slot]
        )

    def down_store(turn, size):
        slot = lax.rem(turn, 2)
        rows = pl.ds(pl.multiple_of(turn * tile, tile), size)
        return pltpu.make_async_copy(
            down_stage.at[slot, pl.ds(0, size)], grad_down_out.at[rows], down_sem.at[slot]
        )

    def join_copy(way, block, part):
        rows = pl.ds(part * piece, piece)
        return pltpu.make_async_remote_copy(
            src_ref=rows_all.at[block, rows],
            dst_ref=rows_all.at[block, rows],
            send_sem=join_send.at[way, block, part],
            recv_sem=join_recv.at[block, part],
            device_id={"shard": me - 1 if way else me + 1},
            device_id_type=MESH,
        )

    def sum_copy(way, block, part, source):
        rows = pl.ds(part * piece, piece)
        target = me - 1 if way else me + 1
        slot = jnp.where(block == target, count, block) if way else block
        return pltpu.make_async_remote_copy(
            src_ref=source.at[block, rows],
            dst_ref=landing.at[slot, rows],
            send_sem=sum_send.at[way, block, part],
            recv_sem=sum_recv.at[way, block, part],
            device_id={"shard": target},
            device_id_type=MESH,
        )

    def open_tile(block, first, size):
        across = pl.ds(first, size)
        beyond = pl.ds(pl.multiple_of(units + first, HEAD), size)
        rows = rows_all[block]
        gate = jnp.dot(rows, gate_up[:, across], preferred_element_type=jnp.float32)
        up = jnp.dot(rows, gate_up[:, beyond], preferred_element_type=jnp.float32)
        d_hidden = product(dy[block], down[across, :], ((1,), (1,)))
        opened = sigmoid(gate)
        wave = gate * opened
        hidden[block, :, across] = low(wave * up)
        d_both[block, :, across] = low(d_hidden * up * (opened * (1.0 + gate * (1.0 - opened))))
        d_both[block, :, beyond] = low(d_hidden * wave)

    def compute(block):
        def open_turn(turn, carry):
            open_tile(block, pl.multiple_of(turn * tile, tile), tile)
            return carry

        lax.fori_loop(0, units // tile, open_turn, 0)
        if units % tile:
            open_tile(block, units // tile * tile, units % tile)

        def close_turn(turn, carry):
            across = pl.ds(pl.multiple_of(turn * tile, tile), tile)
            partial[block, :, across] = low(
                product(d_both[block], gate_up[across, :], ((1,), (1,)))
            )
            return carry

        def down_turn(turn, carry):
            across = pl.ds(pl.multiple_of(turn * tile, tile), tile)
            down_part[block, :, across] = low(product(hidden[block], down[:, across]))
            return carry

        lax.fori_loop(0, width // tile, close_turn, 0)
        lax.fori_loop(0, width // tile, down_turn, 0)

    def slot_turn(slot, carry):
        far = (slot + 1) // 2
        rightward = lax.rem(slot, 2) == 1

        @pl.when(slot == 0)
        def _():
            for part in range(parts):

                @pl.when(has_right)
                def _():
                    join_copy(0, me, part).start()

                @pl.when(has_left)
                def _():
                    join_copy(1, me, part).start()

            for load in loads:
                load.wait()

        @pl.when(rightward)
        def _():
            for part in range(parts):
                for way, present, onward, block in (
                    (0, me >= far, has_right, me - far),
                    (1, me + far < count, has_left, me + far),
                ):

                    @pl.when(present)
                    def _():
                        join_copy(way, block, part).wait_recv()

                    @pl.when(present & onward)
                    def _():
                        join_copy(way, block, part).start()

        block = jnp.where(rightward, me - far, me + far)

        @pl.when((block >= 0) & (block < count))
        def _():
            compute(block)
            part_store(block).start()

            @pl.when((block > me) & jnp.logical_not(has_left))
            def _():
                for part in range(parts):
                    sum_copy(0, block, part, partial).start()

            @pl.when((block < me) & jnp.logical_not(has_right))
            def _():
                for part in range(parts):
                    sum_copy(1, block, part, partial).start()

        return carry

    lax.fori_loop(0, 2 * count - 1, slot_turn, 0)

    def add_on(way, block, part):
        rows = pl.ds(part * piece, piece)
        sum_copy(way, block, part, landing).wait_recv()
        landing[block, rows, :] = low(
            landing[block, rows, :].astype(jnp.float32)
            + partial[block, rows, :].astype(jnp.float32)
        )
        sum_copy(way, block, part, landing).start()

    rows_total = count * own_ref.shape[0]

    def weigh(left, right, stage, across_count):
        turned = left.reshape(rows_total, left.shape[2]).T

        span = across_count * tile // 2

        def turn_of(turn, carry):
            across = pl.ds(pl.multiple_of(turn * span, HEAD), span)
            against = right[:, :, across].reshape(rows_total, span)
            stage[:, across] = low(product(turned, against))
            return carry

        lax.fori_loop(0, 2, turn_of, 0)

    open_count = width // tile
    down_count, down_rest = units // tile, units % tile

    def late_turn(turn, carry):
        step, part = 2 + turn // parts, lax.rem(turn, parts)

        @pl.when((step < count) & (me < step) & has_left)
        def _():
            add_on(0, step, part)

        @pl.when((step < count) & (me > count - 1 - step) & has_right)
        def _():
            add_on(1, count - 1 - step, part)

        slot = lax.rem(turn, 2)
        cols = pl.ds(pl.multiple_of(turn * tile, tile), tile)

        @pl.when(turn < open_count)
        def _():
            @pl.when(turn >= 2)
            def _():
                open_store(turn - 2).wait()

            weigh(rows_all[:, :, cols], d_both, open_stage.at[slot], 2 * units // tile)
            open_store(turn).start()

        @pl.when(turn < down_count)
        def _():
            @pl.when(turn >= 2)
            def _():
                down_store(turn - 2, tile).wait()

            weigh(hidden[:, :, cols], dy, down_stage.at[slot], width // tile)
            down_store(turn, tile).start()

        return carry

    late_count = max((count - 2) * parts, open_count)
    lax.fori_loop(0, late_count, late_turn, 0)
    for turn in range(max(0, open_count - 2), open_count):
        open_store(turn).wait()
    for turn in range(max(0, down_count - 2), down_count):
        down_store(turn, tile).wait()
    if down_rest:
        weigh(
            hidden[:, :, down_count * tile :],
            dy,
            down_stage.at[down_count % 2, pl.ds(0, down_rest)],
            width // tile,
        )
        down_store(down_count, down_rest).start()

    for part in range(parts):
        rows = pl.ds(part * piece, piece)
        total_ref[rows, :] = partial[me, rows, :].astype(jnp.float32)

        @pl.when(has_left)
        def _():
            sum_copy(0, me, part, landing).wait_recv()
            total_ref[rows, :] += landing[me, rows, :].astype(jnp.float32)

        @pl.when(has_right)
        def _():
            sum_copy(1, me, part, landing).wait_recv()
            total_ref[rows, :] += landing[count, rows, :].astype(jnp.float32)

    for block in range(count):
        for part in range(parts):

            @pl.when((me >= block) & has_right)
            def _():
                join_copy(0, block, part).wait_send()

            @pl.when((me <= block) & has_left)
            def _():
                join_copy(1, block, part).wait_send()

            @pl.when(me < block)
            def _():
                sum_copy(0, block, part, partial).wait_send()

            @pl.when(me > block)
            def _():
                sum_copy(1, block, part, partial).wait_send()

        part_store(block).wait()

    if down_rest:
        down_store(down_count, down_rest).wait()


def feed_forward(own, dy, gate_up_mat, down_mat, count, ident, parts=4):
    size, width = own.shape
    units = down_mat.shape[0]
    dma = pltpu.SemaphoreType.DMA
    down_part, grad_open, grad_down, total = pl.pallas_call(
        functools.partial(feed_kernel, count, parts),
        out_shape=[
            bf16(count, size, width),
            bf16(width, 2 * units),
            bf16(units, width),
            f32(size, width),
        ],
        in_specs=[pl.BlockSpec(memory_space=pltpu.VMEM)] + [pl.BlockSpec(memory_space=pl.ANY)] * 3,
        out_specs=[pl.BlockSpec(memory_space=pl.ANY)] * 3 + [pl.BlockSpec(memory_space=pltpu.VMEM)],
        scratch_shapes=[
            pltpu.VMEM((width, 2 * units), jnp.bfloat16),
            pltpu.VMEM((units, width), jnp.bfloat16),
            pltpu.VMEM((count, size, width), jnp.bfloat16),
            pltpu.VMEM((count, size, width), jnp.bfloat16),
            pltpu.VMEM((count, size, units), jnp.bfloat16),
            pltpu.VMEM((count, size, 2 * units), jnp.bfloat16),
            pltpu.VMEM((count, size, width), jnp.bfloat16),
            pltpu.VMEM((count + 1, size, width), jnp.bfloat16),
            pltpu.VMEM((count, size, width), jnp.bfloat16),
            pltpu.VMEM((2, 2 * HEAD, 2 * units), jnp.bfloat16),
            pltpu.VMEM((2, 2 * HEAD, width), jnp.bfloat16),
            dma((3,)),
            dma((count,)),
            dma((2,)),
            dma((2,)),
            dma((2, count, parts)),
            dma((count, parts)),
            dma((2, count, parts)),
            dma((2, count, parts)),
        ],
        compiler_params=pltpu.CompilerParams(
            collective_id=ident, has_side_effects=True, vmem_limit_bytes=63 * 1024 * 1024
        ),
        cost_estimate=busy(120),
        name="feed_forward",
    )(own, dy.reshape(count, size, width), gate_up_mat, down_mat)
    return down_part.reshape(count * size, width), grad_open, grad_down, total


def per_device(
    hidden_in,
    out_grad,
    deal,
    lengths,
    qkv_weight,
    qkv_first,
    qkv_second,
    beta_weight,
    beta_first,
    beta_second,
    out_weight,
    out_first,
    out_second,
    gate_up_weight,
    gate_up_first,
    gate_up_second,
    down_weight,
    down_first,
    down_second,
    conv_weight,
    conv_first,
    conv_second,
    gains,
    gains_first,
    gains_second,
):
    row_count, model_width = hidden_in.shape
    heads = beta_weight.shape[1]
    inner = qkv_weight.shape[2]
    units = down_weight.shape[0]
    devices = lax.axis_size("seq")
    layers = lax.axis_size("shard")
    place = lax.axis_index("shard")
    longest = {4: 4096, 16: 8192}[lengths.shape[0]]
    hops = min(devices - 1, -(-longest // row_count))
    share = row_count // devices // layers
    quarter = devices * share
    _, order, sent_place = lax.sort(
        (deal // row_count, jnp.arange(row_count, dtype=jnp.int32), deal % row_count), num_keys=1
    )
    ordered = order.reshape(devices, layers, share)
    own_order = lax.dynamic_index_in_dim(ordered, place, 1, keepdims=False).reshape(quarter)
    by_layer = jnp.swapaxes(ordered, 0, 1).reshape(row_count)
    chosen = one_hot(own_order, row_count)
    sorting = one_hot(by_layer, row_count)

    def exchanged(rows):
        width = rows.shape[-1]
        return lax.all_to_all(
            rows.reshape(devices, share, width), "seq", split_axis=0, concat_axis=0, tiled=True
        ).reshape(quarter, width)

    plane = (share, model_width) if share % 16 == 0 else (share * model_width // HEAD, HEAD)
    chosen_x = moved_back(chosen, hidden_in).reshape((devices,) + plane)
    sent_place = sent_place.reshape(devices, 1, layers * share)
    sent_place = jnp.pad(sent_place, ((0, 0), (0, 0), (0, -(layers * share) % HEAD)))
    own_x, got_place, out_rows = start_exchange(
        chosen_x, sent_place, low(out_weight), layers, 9
    )
    own_x = own_x.reshape(quarter, model_width).astype(jnp.float32)
    out_rows = out_rows.reshape(layers * inner, out_weight.shape[1])
    got_place = got_place[:, 0, : layers * share]
    all_dy = lax.all_to_all(
        moved_back(one_hot(order, row_count), out_grad).reshape(
            devices, layers, share, model_width
        ),
        "seq",
        split_axis=0,
        concat_axis=0,
        tiled=True,
    )

    first_place = lax.axis_index("seq") * row_count
    places = first_place + jnp.arange(0, row_count, GROUP, dtype=jnp.int32)
    starts = jnp.cumsum(lengths) - lengths
    keep = jnp.all(starts[None, :] != places[:, None], axis=1).astype(jnp.float32)

    beta_pad = jnp.zeros((beta_weight.shape[0], HEAD - heads), jnp.bfloat16)
    mixer_mat = lax.all_gather(
        jnp.concatenate(
            [low(qkv_weight).reshape(-1, 3 * inner), low(beta_weight), beta_pad], axis=1
        ),
        "seq",
        axis=0,
        tiled=True,
    )
    out_mat = lax.all_gather(out_rows, "seq", axis=1, tiled=True)
    gate_up_mat = lax.all_gather(
        low(gate_up_weight).reshape(-1, 2 * units), "seq", axis=0, tiled=True
    )
    down_mat = lax.all_gather(low(down_weight), "seq", axis=1, tiled=True)
    gain_in = gains[:model_width]
    gain_ff = gains[model_width : 2 * model_width]
    gain_out = gains[2 * model_width :].reshape(1, HEAD)
    conv_mat = conv_weight.reshape(TAPS, 3 * inner)

    normed_in = join_rows(low(rms_unit(own_x) * gain_in), layers, 0)
    normed_in, all_dy = lax.optimization_barrier((normed_in, all_dy))
    got_place = jnp.swapaxes(got_place.reshape(devices, layers, share), 0, 1).reshape(row_count)
    to_chain = one_hot(got_place, row_count)
    all_dy = jnp.swapaxes(all_dy, 0, 1).reshape(row_count, model_width)
    own_dy = lax.dynamic_slice_in_dim(all_dy, place * quarter, quarter, 0)
    mixed_in = product(normed_in, mixer_mat)
    logits = mixed_in[:, 3 * inner :]
    logits_high = low(logits)
    logits_low = low(logits - logits_high.astype(jnp.float32))
    chain_in = product(
        to_chain,
        jnp.concatenate([low(mixed_in[:, : 3 * inner]), logits_high, logits_low], axis=1),
    )
    projected = low(chain_in[:, : 3 * inner])
    logits = (
        chain_in[:, 3 * inner : 3 * inner + heads]
        + chain_in[:, 3 * inner + HEAD : 3 * inner + HEAD + heads]
    )
    edge_rows = passed_along(projected[row_count - 8 :], "seq", 1).astype(jnp.float32)
    edge_rows = edge_rows * (jnp.arange(8) >= 8 - (TAPS - 1)).astype(jnp.float32)[:, None]
    rule = Rule(keep, heads, row_count)
    conv, solved, square, step, fresh, reach, zero_out, total = rule.maps(
        projected, edge_rows, logits, conv_mat
    )
    incoming = relayed(total, total[:, :, HEAD:], hops, False, 7)
    state, mixed, normed = rule.outputs(incoming, step, fresh, reach, zero_out, gain_out)

    normed = moved_back(to_chain, normed)
    own_normed = swap_blocks(normed.reshape(layers, quarter, inner), layers, 1, True)
    residual = own_x + product(own_normed, out_mat)
    result, grad_gate_up, grad_down, d_normed_ff = feed_forward(
        low(rms_unit(residual) * gain_ff), all_dy, gate_up_mat, down_mat, layers, 2
    )
    red_down = seq_summed(grad_down, 1)
    d_residual, grad_gain_ff = rms_back(residual, gain_ff, d_normed_ff)
    d_residual = own_dy.astype(jnp.float32) + d_residual
    own_mix = low(d_residual)
    all_mix = join_rows(own_mix, layers, 4)
    out_own = lax.dynamic_slice_in_dim(out_mat, place * inner, inner, 0)
    d_normed = low(product(all_mix, out_own, ((1,), (1,))))
    d_normed, grad_gate_up, result = lax.optimization_barrier((d_normed, grad_gate_up, result))
    result = lax.psum_scatter(result, "shard", scatter_dimension=0, tiled=True)
    red_gate_up = seq_summed(grad_gate_up, 0)
    d_normed = product(to_chain, d_normed)
    d_mixed, d_first_state, grad_gain_out = rule.tail(d_normed, mixed, gain_out, step, reach)
    d_mixed, red_down = lax.optimization_barrier((d_mixed, red_down))
    outgoing = relayed(total, d_first_state, hops, True, 8)
    d_pre, d_tail, d_edge, grad_taps = rule.back(
        outgoing, projected, edge_rows, logits, conv_mat, conv, solved, square, step, reach, state,
        d_mixed,
    )
    d_tail = low(d_tail + passed_along(d_edge, "seq", -1))
    d_pre = lax.dynamic_update_slice(d_pre, d_tail, (row_count - 8, 0))
    d_pre, all_mix = lax.optimization_barrier((d_pre, all_mix))
    d_mixed_in = moved_back(to_chain, d_pre)
    grad_out = low(product(normed, all_mix, ((0,), (0,))))
    red_out = seq_summed(grad_out, 1)
    d_mixed_in, result = lax.optimization_barrier((d_mixed_in, result))
    result = exchanged(low(residual + result.astype(jnp.float32)))
    red_down = red_down.astype(jnp.float32)
    down_new = adamw(down_weight, down_first, down_second, red_down, RATE_DOWN, SHRINK)
    result, *down_new = lax.optimization_barrier((result, *down_new))
    d_normed_in, result, grad_mixer = total_and_join(
        d_mixed_in, mixer_mat, normed_in, result, layers, 5
    )
    d_normed_in, red_gate_up, red_out = lax.optimization_barrier(
        (d_normed_in, red_gate_up, red_out)
    )
    d_input, grad_gain_in = rms_back(own_x, gain_in, d_normed_in)
    d_input = exchanged(low(d_residual + d_input))
    red_gate_up = red_gate_up.astype(jnp.float32).reshape(gate_up_weight.shape)
    gate_up_new = adamw(
        gate_up_weight, gate_up_first, gate_up_second, red_gate_up, RATE_WIDE, SHRINK
    )
    d_input, grad_mixer, *gate_up_new = lax.optimization_barrier(
        (d_input, grad_mixer, *gate_up_new)
    )
    red_mixer = seq_summed(grad_mixer, 0)
    shared = -(-gains.shape[0] // (8 * HEAD)) * 8
    small = jnp.concatenate(
        [
            grad_gain_in,
            grad_gain_ff,
            grad_gain_out.reshape(HEAD),
            jnp.zeros((shared * HEAD - gains.shape[0],), jnp.float32),
            grad_taps.reshape(-1),
        ]
    ).reshape(-1, HEAD)
    d_input, small_sum = join_rows_and_sum(d_input, small, shared, layers, 6)
    d_input, red_mixer = lax.optimization_barrier((d_input, red_mixer))


    red_mixer = red_mixer.astype(jnp.float32)
    red_qkv = red_mixer[:, : 3 * inner].reshape(qkv_weight.shape)
    red_beta = red_mixer[:, 3 * inner : 3 * inner + heads]
    red_out = red_out.astype(jnp.float32)
    red_conv = small_sum[shared:].reshape(conv_weight.shape)
    red_gains = small_sum[:shared].reshape(-1)[: gains.shape[0]]
    qkv_new = adamw(qkv_weight, qkv_first, qkv_second, red_qkv, RATE_WIDE, SHRINK)
    beta_new = adamw(beta_weight, beta_first, beta_second, red_beta, RATE_WIDE, SHRINK)
    out_new = adamw(out_weight, out_first, out_second, red_out, RATE_WIDE, SHRINK)
    conv_new = adamw(conv_weight, conv_first, conv_second, red_conv, RATE_CONV, 0.0)
    gains_new = adamw(gains, gains_first, gains_second, red_gains, RATE_GAIN, 0.0)
    return (
        moved(sorting, result),
        moved(sorting, d_input),
        *qkv_new,
        *beta_new,
        *out_new,
        *gate_up_new,
        *down_new,
        *conv_new,
        *gains_new,
    )


def solution(mesh):
    return jax.shard_map(
        per_device,
        mesh=mesh,
        in_specs=(
            P("seq", None),
            P("seq", None),
            P("seq"),
            P(),
            P("seq", None, "shard"),
            P("seq", None, "shard"),
            P("seq", None, "shard"),
            P("seq", "shard"),
            P("seq", "shard"),
            P("seq", "shard"),
            P("shard", "seq"),
            P("shard", "seq"),
            P("shard", "seq"),
            P("seq", None, "shard"),
            P("seq", None, "shard"),
            P("seq", None, "shard"),
            P("shard", "seq"),
            P("shard", "seq"),
            P("shard", "seq"),
            P(None, None, "shard"),
            P(None, None, "shard"),
            P(None, None, "shard"),
            P(),
            P(),
            P(),
        ),
        out_specs=(
            P("seq", None),
            P("seq", None),
            P("seq", None, "shard"),
            P("seq", None, "shard"),
            P("seq", None, "shard"),
            P("seq", "shard"),
            P("seq", "shard"),
            P("seq", "shard"),
            P("shard", "seq"),
            P("shard", "seq"),
            P("shard", "seq"),
            P("seq", None, "shard"),
            P("seq", None, "shard"),
            P("seq", None, "shard"),
            P("shard", "seq"),
            P("shard", "seq"),
            P("shard", "seq"),
            P(None, None, "shard"),
            P(None, None, "shard"),
            P(None, None, "shard"),
            P(),
            P(),
            P(),
        ),
        check_vma=False,
    )
```

```python
import functools

import jax
import jax.numpy as jnp
from jax import lax
from jax.experimental import pallas as pl
from jax.experimental.pallas import tpu as pltpu
from jax.sharding import PartitionSpec as P

HEAD = 128
TAPS = 4
GROUP = 64
BUSY_FLOPS = 10_000_000
MAPS_BATCH = 4
CHAIN_BATCH = 4
BACK_BATCH = 2
STEP = 10


EPSILON = 1e-06
PRECISE = lax.Precision.HIGHEST
MESH = pl.DeviceIdType.MESH
FIRST_DECAY = 0.9
SECOND_DECAY = 0.95
ADAM_EPSILON = 1e-08
RATE_WIDE = 0.044
RATE_DOWN = 0.027
RATE_CONV = 0.8
RATE_GAIN = 0.3
SHRINK = 0.1


def halves(value):
    high = value.astype(jnp.bfloat16)
    return high, (value - high.astype(jnp.float32)).astype(jnp.bfloat16)


def mul(left, right, dims=((1,), (0,))):
    def one(a, b):
        return lax.dot_general(a, b, (dims, ((), ())), preferred_element_type=jnp.float32)

    left_high, left_low = halves(left)
    right_high, right_low = halves(right)
    return one(left_high, right_high) + (one(left_high, right_low) + one(left_low, right_high))


def mul_nt(left, right):
    return mul(left, right, ((1,), (1,)))


def quick(left, right, dims=((1,), (0,))):
    return lax.dot_general(
        left.astype(jnp.bfloat16),
        right.astype(jnp.bfloat16),
        (dims, ((), ())),
        preferred_element_type=jnp.float32,
    )


def quick_nt(left, right):
    return quick(left, right, ((1,), (1,)))


def grid_indices(size):
    return (
        lax.broadcasted_iota(jnp.int32, (size, size), 0),
        lax.broadcasted_iota(jnp.int32, (size, size), 1),
    )


def unit_lower_inverses(strict_parts):
    size = strict_parts[0].shape[0]
    rows, cols = grid_indices(size)
    inverses = [jnp.where(rows == cols, 1.0, 0.0) for _ in strict_parts]
    level = 0
    while (1 << level) < size:
        corner = (
            ((rows >> (level + 1)) == (cols >> (level + 1)))
            & (((rows >> level) & 1) == 1)
            & (((cols >> level) & 1) == 0)
        )
        parts = [jnp.where(corner, strict, 0.0) for strict in strict_parts]
        if level == 0:
            inverses = [inverse - part for inverse, part in zip(inverses, parts)]
        else:
            inner = [mul(part, inverse) for inverse, part in zip(inverses, parts)]
            outer = [mul(inverse, part) for inverse, part in zip(inverses, inner)]
            inverses = [inverse - part for inverse, part in zip(inverses, outer)]
        level += 1
    return inverses


def sigmoid(value):
    return 1.0 / (1.0 + jnp.exp(-value))


def unit_scale(act):
    return lax.rsqrt(jnp.sum(act * act, axis=-1, keepdims=True) + EPSILON)


def head_lanes(column):
    return slice(column * HEAD, (column + 1) * HEAD)


def maps_kernel(
    heads,
    batch,
    keep_ref,
    pre_ref,
    edge_ref,
    logit_ref,
    taps_ref,
    conv_ref,
    solved_ref,
    square_ref,
    step_ref,
    fresh_ref,
    reach_ref,
    zero_out_ref,
    total_ref,
    history,
    running,
):
    turn = pl.program_id(0)
    scale = HEAD**-0.5
    pairs = [(item, head) for item in range(batch) for head in range(heads)]
    keeps = [keep_ref[turn * batch + item] for item in range(batch)]

    @pl.when(turn == 0)
    def _():
        history[0, 0:8, :] = edge_ref[...] * keeps[0]
        rows, cols = grid_indices(HEAD)
        start = jnp.where(rows == cols, 1.0, 0.0)
        for head in range(heads):
            running[head, :, 0:HEAD] = start
            running[head, :, HEAD : 2 * HEAD] = jnp.zeros((HEAD, HEAD), jnp.float32)

    @pl.when(turn > 0)
    def _():
        history[0, 0:8, :] = history[batch - 1, GROUP : GROUP + 8, :] * keeps[0]

    for item in range(batch):
        history[item, 8 : GROUP + 8, :] = pre_ref[
            item * GROUP : (item + 1) * GROUP, :
        ].astype(jnp.float32)
        if item:
            history[item, 0:8, :] = history[item - 1, GROUP : GROUP + 8, :] * keeps[item]

    def conv_of(item, column):
        cols = head_lanes(column)
        total = taps_ref[0:1, cols] * history[item, 5 : 5 + GROUP, cols]
        for tap in range(1, TAPS):
            shifted = history[item, 5 + tap : 5 + tap + GROUP, cols]
            total = total + taps_ref[tap : tap + 1, cols] * shifted
        conv_ref[item * GROUP : (item + 1) * GROUP, cols] = total
        return total * sigmoid(total)

    rows, cols = grid_indices(GROUP)
    big_rows, big_cols = grid_indices(HEAD)
    keys = [conv_of(item, heads + head) for item, head in pairs]
    keys = [key * unit_scale(key) for key in keys]
    strengths = [
        sigmoid(logit_ref[item * GROUP : (item + 1) * GROUP, head : head + 1])
        for item, head in pairs
    ]
    overlaps = [mul_nt(key, key) for key in keys]
    inverses = unit_lower_inverses(
        [
            jnp.where(rows > cols, strength * overlap, 0.0)
            for strength, overlap in zip(strengths, overlaps)
        ]
    )
    queries = [conv_of(item, head) for item, head in pairs]
    queries = [query * unit_scale(query) for query in queries]
    scores = [
        jnp.where(rows >= cols, mul_nt(query, key), 0.0) for query, key in zip(queries, keys)
    ]
    values = [conv_of(item, 2 * heads + head) for item, head in pairs]
    solved = [
        mul(inverse, jnp.concatenate([strength * key, strength * value], axis=1))
        for inverse, strength, key, value in zip(inverses, strengths, keys, values)
    ]
    pushed = [mul(key.T, part) for key, part in zip(keys, solved)]
    mixed = [mul(score, part) for score, part in zip(scores, solved)]
    steps = [jnp.where(big_rows == big_cols, 1.0, 0.0) - part[:, 0:HEAD] for part in pushed]
    for index, (item, head) in enumerate(pairs):
        here = slice(item * GROUP, (item + 1) * GROUP)
        solved_ref[item, head] = solved[index]
        square_ref[item, head, :, 0:GROUP] = inverses[index]
        square_ref[item, head, :, GROUP : 2 * GROUP] = scores[index]
        reach_ref[here, head_lanes(head)] = scale * (queries[index] - mixed[index][:, 0:HEAD])
        zero_out_ref[here, head_lanes(head)] = scale * mixed[index][:, HEAD:]
        step_ref[item, head] = steps[index]
        fresh_ref[item, head] = pushed[index][:, HEAD:]
    now = [running[head] for head in range(heads)]
    for item in range(batch):
        first = item * heads
        moved = [mul(steps[first + head], now[head] * keeps[item]) for head in range(heads)]
        now = [
            jnp.concatenate(
                [moved[head][:, 0:HEAD], moved[head][:, HEAD:] + pushed[first + head][:, HEAD:]],
                axis=1,
            )
            for head in range(heads)
        ]
    for head in range(heads):
        running[head] = now[head]
    total_ref[...] = running[...]


def outputs_kernel(
    heads,
    batch,
    keep_ref,
    incoming_ref,
    step_ref,
    fresh_ref,
    reach_ref,
    zero_out_ref,
    gain_ref,
    state_ref,
    mixed_ref,
    normed_ref,
    running,
):
    turn = pl.program_id(0)

    @pl.when(turn == 0)
    def _():
        running[...] = incoming_ref[...]

    now = [running[head] for head in range(heads)]
    states = []
    for item in range(batch):
        keep = keep_ref[turn * batch + item]
        now = [state * keep for state in now]
        states.append(now)
        now = [
            mul(step_ref[item, head], now[head]) + fresh_ref[item, head] for head in range(heads)
        ]
    for head in range(heads):
        running[head] = now[head]
    for item in range(batch):
        here = slice(item * GROUP, (item + 1) * GROUP)
        outs = [
            mul(reach_ref[here, head_lanes(head)], states[item][head])
            + zero_out_ref[here, head_lanes(head)]
            for head in range(heads)
        ]
        for head, mixed in enumerate(outs):
            state_ref[item, head] = states[item][head]
            mixed_ref[here, head_lanes(head)] = mixed
            inverse_rms = lax.rsqrt(jnp.mean(mixed * mixed, axis=-1, keepdims=True) + EPSILON)
            normed_ref[here, head_lanes(head)] = (mixed * inverse_rms * gain_ref[...]).astype(
                jnp.bfloat16
            )


def tail_kernel(
    heads,
    batch,
    keep_ref,
    d_normed_ref,
    mixed_ref,
    gain_ref,
    step_ref,
    reach_ref,
    d_mixed_ref,
    d_state_ref,
    d_gain_ref,
    running,
):
    turn = pl.num_programs(0) - 1 - pl.program_id(0)

    @pl.when(pl.program_id(0) == 0)
    def _():
        running[...] = jnp.zeros_like(running)
        d_gain_ref[...] = jnp.zeros_like(d_gain_ref)

    gain_sum = jnp.zeros((1, HEAD), jnp.float32)
    pulled = []
    for item in range(batch):
        here = slice(item * GROUP, (item + 1) * GROUP)
        grads = []
        for head in range(heads):
            mixed = mixed_ref[here, head_lanes(head)]
            d_normed = d_normed_ref[here, head_lanes(head)]
            inverse_rms = lax.rsqrt(jnp.mean(mixed * mixed, axis=-1, keepdims=True) + EPSILON)
            unit = mixed * inverse_rms
            gain_sum = gain_sum + jnp.sum(d_normed * unit, axis=0, keepdims=True)
            d_unit = d_normed * gain_ref[...]
            d_mixed = inverse_rms * (
                d_unit - unit * jnp.mean(d_unit * unit, axis=-1, keepdims=True)
            )
            d_mixed_ref[here, head_lanes(head)] = d_mixed
            grads.append(d_mixed)
        pulled.append(
            [mul(reach_ref[here, head_lanes(head)].T, grads[head]) for head in range(heads)]
        )
    now = [running[head] for head in range(heads)]
    for item in reversed(range(batch)):
        keep = keep_ref[turn * batch + item]
        now = [
            keep * (mul(step_ref[item, head].T, now[head]) + pulled[item][head])
            for head in range(heads)
        ]
    for head in range(heads):
        running[head] = now[head]
    d_gain_ref[...] += gain_sum
    d_state_ref[...] = running[...]


def back_kernel(
    heads,
    batch,
    keep_ref,
    outgoing_ref,
    pre_ref,
    edge_ref,
    logit_ref,
    taps_ref,
    conv_ref,
    solved_ref,
    square_ref,
    step_ref,
    reach_ref,
    state_ref,
    d_mixed_ref,
    d_pre_ref,
    d_tail_ref,
    d_edge_ref,
    d_taps_ref,
    d_history,
    edge_history,
    running,
):
    count = pl.num_programs(0)
    turn = count - 1 - pl.program_id(0)
    scale = HEAD**-0.5
    rows, cols = grid_indices(GROUP)
    pairs = [(item, head) for item in range(batch) for head in range(heads)]
    indices = range(len(pairs))
    keeps = [keep_ref[turn * batch + item] for item in range(batch)]

    @pl.when(pl.program_id(0) == 0)
    def _():
        running[...] = outgoing_ref[...]
        d_history[batch - 1, GROUP : GROUP + 8, :] = jnp.zeros(
            (8, d_history.shape[2]), jnp.float32
        )
        d_taps_ref[...] = jnp.zeros_like(d_taps_ref)

    @pl.when(pl.program_id(0) > 0)
    def _():
        d_history[batch - 1, GROUP : GROUP + 8, :] = (
            d_history[0, 0:8, :] * keep_ref[(turn + 1) * batch]
        )

    def spot(item):
        return slice(item * GROUP, (item + 1) * GROUP)

    def act_of(item, column):
        conv = conv_ref[spot(item), head_lanes(column)]
        return conv * sigmoid(conv)

    def slope_of(item, column):
        conv = conv_ref[spot(item), head_lanes(column)]
        gate = sigmoid(conv)
        return gate * (1.0 + conv * (1.0 - gate))

    def d_unit(unit, inverse_norm, grad):
        return inverse_norm * (grad - unit * jnp.sum(unit * grad, axis=-1, keepdims=True))

    d_mixed = [d_mixed_ref[spot(item), head_lanes(head)] for item, head in pairs]
    pulled = [
        mul(reach_ref[spot(item), head_lanes(head)].T, d_mixed[index])
        for index, (item, head) in enumerate(pairs)
    ]
    d_states = [None] * len(pairs)
    now = [running[head] for head in range(heads)]
    for item in reversed(range(batch)):
        first = item * heads
        d_states[first : first + heads] = now
        now = [
            keeps[item] * (mul(step_ref[item, head].T, now[head]) + pulled[first + head])
            for head in range(heads)
        ]
    for head in range(heads):
        running[head] = now[head]

    d_out = [scale * grad for grad in d_mixed]
    states = [state_ref[item, head] for item, head in pairs]
    solved = [solved_ref[item, head] for item, head in pairs]
    scores = [square_ref[item, head, :, GROUP : 2 * GROUP] for item, head in pairs]
    acts = [act_of(item, heads + head) for item, head in pairs]
    key_scales = [unit_scale(act) for act in acts]
    keys = [act * size for act, size in zip(acts, key_scales)]
    fresh = [
        solved[index][:, HEAD:] - quick(solved[index][:, 0:HEAD], states[index])
        for index in indices
    ]
    d_fresh = [
        quick(scores[index].T, d_out[index]) + quick(keys[index], d_states[index])
        for index in indices
    ]
    d_scores = [
        jnp.where(rows >= cols, quick_nt(d_out[index], fresh[index]), 0.0) for index in indices
    ]
    d_solved = [
        jnp.concatenate([-quick_nt(d_fresh[index], states[index]), d_fresh[index]], axis=1)
        for index in indices
    ]
    d_right = [
        quick(square_ref[item, head, :, 0:GROUP].T, d_solved[index])
        for index, (item, head) in enumerate(pairs)
    ]
    d_queries = [
        quick_nt(d_out[index], states[index]) + quick(d_scores[index], keys[index])
        for index in indices
    ]
    acts = [act_of(item, head) for item, head in pairs]
    query_scales = [unit_scale(act) for act in acts]
    queries = [act * size for act, size in zip(acts, query_scales)]
    d_keys = [
        quick(d_scores[index].T, queries[index]) + quick_nt(fresh[index], d_states[index])
        for index in indices
    ]
    d_strict = [
        jnp.where(rows > cols, -quick_nt(d_right[index], solved[index]), 0.0) for index in indices
    ]
    strengths = [
        sigmoid(logit_ref[spot(item), head : head + 1]) for item, head in pairs
    ]
    overlaps = [quick_nt(key, key) for key in keys]
    both = [
        strengths[index] * d_strict[index] + (strengths[index] * d_strict[index]).T
        for index in indices
    ]
    d_keys = [
        d_keys[index]
        + strengths[index] * d_right[index][:, 0:HEAD]
        + quick(both[index], keys[index])
        for index in indices
    ]
    d_logits = []
    for index, (item, head) in enumerate(pairs):
        strength = strengths[index]
        value = act_of(item, 2 * heads + head)
        d_strength = (
            jnp.sum(d_right[index][:, 0:HEAD] * keys[index], axis=-1, keepdims=True)
            + jnp.sum(d_right[index][:, HEAD:] * value, axis=-1, keepdims=True)
            + jnp.sum(d_strict[index] * overlaps[index], axis=-1, keepdims=True)
        )
        d_logits.append(d_strength * strength * (1.0 - strength))
        for column, grad in (
            (head, d_unit(queries[index], query_scales[index], d_queries[index])),
            (heads + head, d_unit(keys[index], key_scales[index], d_keys[index])),
            (2 * heads + head, strength * d_right[index][:, HEAD:]),
        ):
            d_history[item, 0:GROUP, head_lanes(column)] = grad * slope_of(item, column)

    spread = lax.broadcasted_iota(jnp.int32, (GROUP, HEAD), 1)
    for item in range(batch):
        placed = jnp.zeros((GROUP, HEAD), jnp.float32)
        for head in range(heads):
            placed = jnp.where(spread == head, d_logits[item * heads + head], placed)
        d_pre_ref[spot(item), 3 * heads * HEAD :] = placed.astype(jnp.bfloat16)

    for item in reversed(range(batch - 1)):
        d_history[item, GROUP : GROUP + 8, :] = d_history[item + 1, 0:8, :] * keeps[item + 1]
    for column in range(3 * heads):
        lanes = head_lanes(column)
        for item in range(batch):
            pre = pre_ref[spot(item), lanes].astype(jnp.float32)
            total = jnp.zeros((GROUP, HEAD), jnp.float32)
            for tap in range(TAPS):
                part = d_history[item, TAPS - 1 - tap : TAPS - 1 - tap + GROUP, lanes]
                total = total + taps_ref[tap : tap + 1, lanes] * part
                d_taps_ref[tap : tap + 1, lanes] += jnp.sum(pre * part, axis=0, keepdims=True)
            d_pre_ref[spot(item), lanes] = total.astype(jnp.bfloat16)
        d_tail_ref[:, lanes] = jnp.where(
            turn == count - 1, total[GROUP - 8 :, :], d_tail_ref[:, lanes]
        )

    @pl.when(turn == 0)
    def _():
        edge_history[0:8, :] = jnp.zeros((8, edge_history.shape[1]), jnp.float32)
        edge_history[8:16, :] = d_history[0, 0:8, :] * keeps[0]
        total = jnp.zeros(d_edge_ref.shape, jnp.float32)
        for tap in range(TAPS):
            part = edge_history[TAPS - 1 - tap : TAPS - 1 - tap + 8, :]
            total = total + taps_ref[tap : tap + 1, :] * part
            d_taps_ref[tap : tap + 1, :] += jnp.sum(edge_ref[...] * part, axis=0, keepdims=True)
        d_edge_ref[...] = total


def passed_along(value, axis, by):
    count = lax.axis_size(axis)
    pairs = [(i, i + by) for i in range(count) if 0 <= i + by < count]
    return lax.ppermute(value, axis, pairs)


def adamw(weight, first, second, grad, rate, decay):
    first = FIRST_DECAY * first + (1.0 - FIRST_DECAY) * grad
    second = SECOND_DECAY * second + (1.0 - SECOND_DECAY) * grad * grad
    stepped = (
        first
        / (1.0 - FIRST_DECAY**STEP)
        / (jnp.sqrt(second / (1.0 - SECOND_DECAY**STEP)) + ADAM_EPSILON)
    )
    return (weight - rate * (stepped + decay * weight), first, second)


def f32(*shape):
    return jax.ShapeDtypeStruct(shape, jnp.float32)


def bf16(*shape):
    return jax.ShapeDtypeStruct(shape, jnp.bfloat16)


class Rule:
    def __init__(self, keep, heads, row_count):
        self.keep, self.heads, self.rows = keep, heads, row_count
        self.count = row_count // GROUP
        self.params = pltpu.CompilerParams(
            dimension_semantics=("arbitrary",), vmem_limit_bytes=48 * 1024 * 1024
        )

    def rows_spec(self, width, batch, back=False):
        last = self.count // batch - 1
        if back:
            return pl.BlockSpec((batch * GROUP, width), lambda n: (last - n, 0))
        return pl.BlockSpec((batch * GROUP, width), lambda n: (n, 0))

    def block_spec(self, shape, batch, back=False):
        last = self.count // batch - 1
        if back:
            return pl.BlockSpec((batch,) + shape, lambda n: (last - n, 0, 0, 0))
        return pl.BlockSpec((batch,) + shape, lambda n: (n, 0, 0, 0))

    def whole(self, *shape):
        return pl.BlockSpec(shape, lambda n: (0,) * len(shape))

    def smem(self):
        return pl.BlockSpec(memory_space=pltpu.SMEM)

    def maps(self, pre, edge, logits, taps):
        heads, rows, count, inner = self.heads, self.rows, self.count, self.heads * HEAD
        return pl.pallas_call(
            functools.partial(maps_kernel, heads, MAPS_BATCH),
            grid=(count // MAPS_BATCH,),
            in_specs=[
                self.smem(),
                self.rows_spec(3 * inner, MAPS_BATCH),
                self.whole(8, 3 * inner),
                self.rows_spec(heads, MAPS_BATCH),
                self.whole(TAPS, 3 * inner),
            ],
            out_specs=[
                self.rows_spec(3 * inner, MAPS_BATCH),
                self.block_spec((heads, GROUP, 2 * HEAD), MAPS_BATCH),
                self.block_spec((heads, GROUP, 2 * GROUP), MAPS_BATCH),
                self.block_spec((heads, HEAD, HEAD), MAPS_BATCH),
                self.block_spec((heads, HEAD, HEAD), MAPS_BATCH),
                self.rows_spec(inner, MAPS_BATCH),
                self.rows_spec(inner, MAPS_BATCH),
                self.whole(heads, HEAD, 2 * HEAD),
            ],
            out_shape=[
                f32(rows, 3 * inner),
                f32(count, heads, GROUP, 2 * HEAD),
                f32(count, heads, GROUP, 2 * GROUP),
                f32(count, heads, HEAD, HEAD),
                f32(count, heads, HEAD, HEAD),
                f32(rows, inner),
                f32(rows, inner),
                f32(heads, HEAD, 2 * HEAD),
            ],
            scratch_shapes=[
                pltpu.VMEM((MAPS_BATCH, GROUP + 8, 3 * inner), jnp.float32),
                pltpu.VMEM((heads, HEAD, 2 * HEAD), jnp.float32),
            ],
            compiler_params=self.params,
            cost_estimate=busy(35),
            name="delta_maps",
        )(self.keep, pre, edge, logits, taps)

    def outputs(self, incoming, step, fresh, reach, zero_out, gain):
        heads, rows, count, inner = self.heads, self.rows, self.count, self.heads * HEAD
        return pl.pallas_call(
            functools.partial(outputs_kernel, heads, CHAIN_BATCH),
            grid=(count // CHAIN_BATCH,),
            in_specs=[
                self.smem(),
                self.whole(heads, HEAD, HEAD),
                self.block_spec((heads, HEAD, HEAD), CHAIN_BATCH),
                self.block_spec((heads, HEAD, HEAD), CHAIN_BATCH),
                self.rows_spec(inner, CHAIN_BATCH),
                self.rows_spec(inner, CHAIN_BATCH),
                self.whole(1, HEAD),
            ],
            out_specs=[
                self.block_spec((heads, HEAD, HEAD), CHAIN_BATCH),
                self.rows_spec(inner, CHAIN_BATCH),
                self.rows_spec(inner, CHAIN_BATCH),
            ],
            out_shape=[f32(count, heads, HEAD, HEAD), f32(rows, inner), bf16(rows, inner)],
            scratch_shapes=[pltpu.VMEM((heads, HEAD, HEAD), jnp.float32)],
            compiler_params=self.params,
            cost_estimate=busy(9),
            name="delta_outputs",
        )(self.keep, incoming, step, fresh, reach, zero_out, gain)

    def tail(self, d_normed, mixed, gain, step, reach):
        heads, rows, count, inner = self.heads, self.rows, self.count, self.heads * HEAD
        return pl.pallas_call(
            functools.partial(tail_kernel, heads, CHAIN_BATCH),
            grid=(count // CHAIN_BATCH,),
            in_specs=[
                self.smem(),
                self.rows_spec(inner, CHAIN_BATCH, True),
                self.rows_spec(inner, CHAIN_BATCH, True),
                self.whole(1, HEAD),
                self.block_spec((heads, HEAD, HEAD), CHAIN_BATCH, True),
                self.rows_spec(inner, CHAIN_BATCH, True),
            ],
            out_specs=[
                self.rows_spec(inner, CHAIN_BATCH, True),
                self.whole(heads, HEAD, HEAD),
                self.whole(1, HEAD),
            ],
            out_shape=[f32(rows, inner), f32(heads, HEAD, HEAD), f32(1, HEAD)],
            scratch_shapes=[pltpu.VMEM((heads, HEAD, HEAD), jnp.float32)],
            compiler_params=self.params,
            cost_estimate=busy(11),
            name="delta_tail",
        )(self.keep, d_normed, mixed, gain, step, reach)

    def back(self, outgoing, pre, edge, logits, taps, conv, solved, square, step, reach, state, d_mixed):
        heads, rows, count, inner = self.heads, self.rows, self.count, self.heads * HEAD
        return pl.pallas_call(
            functools.partial(back_kernel, heads, BACK_BATCH),
            grid=(count // BACK_BATCH,),
            in_specs=[
                self.smem(),
                self.whole(heads, HEAD, HEAD),
                self.rows_spec(3 * inner, BACK_BATCH, True),
                self.whole(8, 3 * inner),
                self.rows_spec(heads, BACK_BATCH, True),
                self.whole(TAPS, 3 * inner),
                self.rows_spec(3 * inner, BACK_BATCH, True),
                self.block_spec((heads, GROUP, 2 * HEAD), BACK_BATCH, True),
                self.block_spec((heads, GROUP, 2 * GROUP), BACK_BATCH, True),
                self.block_spec((heads, HEAD, HEAD), BACK_BATCH, True),
                self.rows_spec(inner, BACK_BATCH, True),
                self.block_spec((heads, HEAD, HEAD), BACK_BATCH, True),
                self.rows_spec(inner, BACK_BATCH, True),
            ],
            out_specs=[
                self.rows_spec(3 * inner + HEAD, BACK_BATCH, True),
                self.whole(8, 3 * inner),
                self.whole(8, 3 * inner),
                self.whole(TAPS, 3 * inner),
            ],
            out_shape=[
                bf16(rows, 3 * inner + HEAD),
                f32(8, 3 * inner),
                f32(8, 3 * inner),
                f32(TAPS, 3 * inner),
            ],
            scratch_shapes=[
                pltpu.VMEM((BACK_BATCH, GROUP + 8, 3 * inner), jnp.float32),
                pltpu.VMEM((16, 3 * inner), jnp.float32),
                pltpu.VMEM((heads, HEAD, HEAD), jnp.float32),
            ],
            compiler_params=self.params,
            cost_estimate=busy(45),
            name="delta_back",
        )(
            self.keep, outgoing, pre, edge, logits, taps, conv, solved, square, step, reach, state,
            d_mixed,
        )


def rms_unit(values):
    return values * lax.rsqrt(jnp.mean(values * values, axis=-1, keepdims=True) + EPSILON)


def rms_back(values, gain_vec, grad):
    inverse_rms = lax.rsqrt(jnp.mean(values * values, axis=-1, keepdims=True) + EPSILON)
    unit = values * inverse_rms
    d_unit = grad * gain_vec
    d_values = inverse_rms * (d_unit - unit * jnp.mean(d_unit * unit, axis=-1, keepdims=True))
    return d_values, jnp.sum(grad * unit, axis=0)


def low(values):
    return values.astype(jnp.bfloat16)


def product(left, right, dims=((1,), (0,))):
    return lax.dot_general(left, right, (dims, ((), ())), preferred_element_type=jnp.float32)


def rows_summed(partial):
    return lax.psum_scatter(low(partial), "shard", scatter_dimension=0, tiled=True)


def rows_joined(rows):
    return lax.all_gather(rows, "shard", axis=0, tiled=True)


def seq_summed(grad, dim):
    return lax.psum_scatter(grad, "seq", scatter_dimension=dim, tiled=True)


def one_hot(indices, size):
    return (jnp.arange(size, dtype=jnp.int32)[:, None] == indices[None, :]).astype(jnp.bfloat16)


def moved(matrix, values):
    return low(product(matrix, values))


def moved_back(matrix, values):
    return low(product(matrix, values, ((0,), (0,))))


def busy(micros):
    return pl.CostEstimate(flops=micros * BUSY_FLOPS, bytes_accessed=0, transcendentals=0)


def ends(count):
    me = lax.axis_index("shard")
    return me, me > 0, me < count - 1


def meet_neighbours(count):
    me, has_left, has_right = ends(count)
    barrier = pltpu.get_barrier_semaphore()

    @pl.when(has_left)
    def _():
        pl.semaphore_signal(barrier, inc=1, device_id={"shard": me - 1}, device_id_type=MESH)

    @pl.when(has_right)
    def _():
        pl.semaphore_signal(barrier, inc=1, device_id={"shard": me + 1}, device_id_type=MESH)

    pl.semaphore_wait(barrier, has_left.astype(jnp.int32) + has_right.astype(jnp.int32))


def join_kernel(count, parts, own_ref, out_ref, own_sem, send_sem, recv_sem):
    me, has_left, has_right = ends(count)
    size = own_ref.shape[0] // parts
    meet_neighbours(count)
    own_copy = pltpu.make_async_copy(own_ref, out_ref.at[me], own_sem)
    own_copy.start()

    def piece_copy(way, block, part, source, target):
        rows = pl.ds(part * size, size)
        return pltpu.make_async_remote_copy(
            src_ref=source.at[rows] if source is own_ref else source.at[block, rows],
            dst_ref=out_ref.at[block, rows],
            send_sem=send_sem.at[way, block, part],
            recv_sem=recv_sem.at[block, part],
            device_id={"shard": target},
            device_id_type=MESH,
        )

    def each(action):
        for far in range(count):
            for part in range(parts):
                for way, present, onward, block, target in (
                    (0, me >= far, has_right, me - far, me + 1),
                    (1, me + far < count, has_left, me + far, me - 1),
                ):
                    action(far, part, way, present, onward, block, target)

    def start(far, part, way, present, onward, block, target):
        source = own_ref if far == 0 else out_ref

        if far:

            @pl.when(present)
            def _():
                piece_copy(way, block, part, out_ref, target).wait_recv()

        @pl.when(present & onward)
        def _():
            piece_copy(way, block, part, source, target).start()

    def finish(far, part, way, present, onward, block, target):
        source = own_ref if far == 0 else out_ref

        @pl.when(present & onward)
        def _():
            piece_copy(way, block, part, source, target).wait_send()

    each(start)
    each(finish)
    own_copy.wait()


def join_rows(rows, count, ident, parts=4):
    size, width = rows.shape
    return pl.pallas_call(
        functools.partial(join_kernel, count, parts),
        out_shape=jax.ShapeDtypeStruct((count, size, width), rows.dtype),
        in_specs=[pl.BlockSpec(memory_space=pl.ANY)],
        out_specs=pl.BlockSpec(memory_space=pl.ANY),
        scratch_shapes=[
            pltpu.SemaphoreType.DMA(()),
            pltpu.SemaphoreType.DMA((2, count, parts)),
            pltpu.SemaphoreType.DMA((count, parts)),
        ],
        compiler_params=pltpu.CompilerParams(collective_id=ident, has_side_effects=True),
        cost_estimate=busy(70),
        name="join_rows",
    )(rows).reshape(count * size, width)


def swap_kernel(count, to_columns, in_ref, out_ref, own_sem, send_sem, recv_sem):
    me = lax.axis_index("shard")
    barrier = pltpu.get_barrier_semaphore()
    for hop in range(1, count):
        other = lax.rem(me + hop, count)
        pl.semaphore_signal(barrier, inc=1, device_id={"shard": other}, device_id_type=MESH)
    pl.semaphore_wait(barrier, count - 1)
    if to_columns:
        width = in_ref.shape[2]
    else:
        width = out_ref.shape[2]

    def columns(ref, index):
        return ref.at[:, pl.ds(pl.multiple_of(index * width, width), width)]

    def source(block):
        return in_ref.at[block] if to_columns else columns(in_ref, block)

    def landing(block):
        return columns(out_ref, block) if to_columns else out_ref.at[block]

    own_copy = pltpu.make_async_copy(source(me), landing(me), own_sem)
    own_copy.start()

    def block_copy(hop):
        other = lax.rem(me + hop, count)
        return pltpu.make_async_remote_copy(
            src_ref=source(other),
            dst_ref=landing(me),
            send_sem=send_sem.at[hop],
            recv_sem=recv_sem.at[hop],
            device_id={"shard": other},
            device_id_type=MESH,
        )

    for hop in range(1, count):
        block_copy(hop).start()
    for hop in range(1, count):
        block_copy(hop).wait()
    own_copy.wait()


def swap_blocks(value, count, ident, to_columns):
    if to_columns:
        _, size, width = value.shape
        shape = (size, count * width)
    else:
        size, width = value.shape[0], value.shape[1] // count
        shape = (count, size, width)
    return pl.pallas_call(
        functools.partial(swap_kernel, count, to_columns),
        out_shape=jax.ShapeDtypeStruct(shape, value.dtype),
        in_specs=[pl.BlockSpec(memory_space=pl.ANY)],
        out_specs=pl.BlockSpec(memory_space=pl.ANY),
        scratch_shapes=[
            pltpu.SemaphoreType.DMA(()),
            pltpu.SemaphoreType.DMA((count,)),
            pltpu.SemaphoreType.DMA((count,)),
        ],
        compiler_params=pltpu.CompilerParams(collective_id=ident, has_side_effects=True),
        cost_estimate=busy(23),
        name="swap_blocks",
    )(value)


def relay_kernel(heads, hops, back, total_ref, fresh_ref, out_ref, sending, landing, send_sem, recv_sem):
    count = lax.axis_size("seq")
    me = lax.axis_index("seq")
    if back:
        follows, precedes, target, origin = me < count - 1, me > 0, me - 1, me + 1
    else:
        follows, precedes, target, origin = me > 0, me < count - 1, me + 1, me - 1
    barrier = pltpu.get_barrier_semaphore()

    @pl.when(follows)
    def _():
        pl.semaphore_signal(barrier, inc=1, device_id={"seq": origin}, device_id_type=MESH)

    @pl.when(precedes)
    def _():
        pl.semaphore_signal(barrier, inc=1, device_id={"seq": target}, device_id_type=MESH)

    pl.semaphore_wait(barrier, follows.astype(jnp.int32) + precedes.astype(jnp.int32))

    def state_copy(hop, head):
        return pltpu.make_async_remote_copy(
            src_ref=sending.at[hop, head],
            dst_ref=landing.at[hop, head],
            send_sem=send_sem.at[hop, head],
            recv_sem=recv_sem.at[hop, head],
            device_id={"seq": target},
            device_id_type=MESH,
        )

    for hop in range(hops):
        for head in range(heads):
            fresh = fresh_ref[head]
            if hop == 0:
                sending[hop, head] = low(fresh)
            else:

                @pl.when(follows)
                def _():
                    state_copy(hop - 1, head).wait_recv()
                    step = total_ref[head, :, 0:HEAD]
                    step = step.T if back else step
                    sending[hop, head] = low(
                        fresh + mul(step, landing[hop - 1, head].astype(jnp.float32))
                    )

                @pl.when(jnp.logical_not(follows))
                def _():
                    sending[hop, head] = low(fresh)

            @pl.when(precedes)
            def _():
                state_copy(hop, head).start()

    for head in range(heads):

        @pl.when(follows)
        def _():
            state_copy(hops - 1, head).wait_recv()
            out_ref[head] = landing[hops - 1, head].astype(jnp.float32)

        @pl.when(jnp.logical_not(follows))
        def _():
            out_ref[head] = jnp.zeros((HEAD, HEAD), jnp.float32)

    @pl.when(precedes)
    def _():
        for hop in range(hops):
            for head in range(heads):
                state_copy(hop, head).wait_send()


def relayed(total, fresh, hops, back, ident):
    heads = fresh.shape[0]
    return pl.pallas_call(
        functools.partial(relay_kernel, heads, hops, back),
        out_shape=jax.ShapeDtypeStruct((heads, HEAD, HEAD), jnp.float32),
        in_specs=[pl.BlockSpec(memory_space=pltpu.VMEM)] * 2,
        out_specs=pl.BlockSpec(memory_space=pltpu.VMEM),
        scratch_shapes=[
            pltpu.VMEM((hops, heads, HEAD, HEAD), jnp.bfloat16),
            pltpu.VMEM((hops, heads, HEAD, HEAD), jnp.bfloat16),
            pltpu.SemaphoreType.DMA((hops, heads)),
            pltpu.SemaphoreType.DMA((hops, heads)),
        ],
        compiler_params=pltpu.CompilerParams(collective_id=ident, has_side_effects=True),
        cost_estimate=busy(15),
        name="relay_back" if back else "relay",
    )(total, fresh)


def last_join_kernel(
    count,
    parts,
    shared,
    own_ref,
    small_ref,
    out_ref,
    small_out,
    seq_slots,
    layer_slots,
    own_sem,
    send_sem,
    recv_sem,
    seq_send,
    seq_recv,
    layer_send,
    layer_recv,
):
    me, has_left, has_right = ends(count)
    size = own_ref.shape[0] // parts
    devices = lax.axis_size("seq")
    here = lax.axis_index("seq")
    barrier = pltpu.get_barrier_semaphore()
    for hop in range(1, devices):
        other = lax.rem(here + hop, devices)
        pl.semaphore_signal(barrier, inc=1, device_id={"seq": other}, device_id_type=MESH)
    for hop in range(1, count):
        other = lax.rem(me + hop, count)
        pl.semaphore_signal(barrier, inc=1, device_id={"shard": other}, device_id_type=MESH)
    pl.semaphore_wait(barrier, devices + count - 2)
    own_copy = pltpu.make_async_copy(own_ref, out_ref.at[me], own_sem)
    own_copy.start()

    def seq_copy(hop):
        return pltpu.make_async_remote_copy(
            src_ref=small_ref,
            dst_ref=seq_slots.at[here],
            send_sem=seq_send.at[hop],
            recv_sem=seq_recv.at[hop],
            device_id={"seq": lax.rem(here + hop, devices)},
            device_id_type=MESH,
        )

    def layer_copy(hop):
        return pltpu.make_async_remote_copy(
            src_ref=small_out.at[pl.ds(0, shared)],
            dst_ref=layer_slots.at[me],
            send_sem=layer_send.at[hop],
            recv_sem=layer_recv.at[hop],
            device_id={"shard": lax.rem(me + hop, count)},
            device_id_type=MESH,
        )

    def piece_copy(way, block, part, source, target):
        rows = pl.ds(part * size, size)
        return pltpu.make_async_remote_copy(
            src_ref=source.at[rows] if source is own_ref else source.at[block, rows],
            dst_ref=out_ref.at[block, rows],
            send_sem=send_sem.at[way, block, part],
            recv_sem=recv_sem.at[block, part],
            device_id={"shard": target},
            device_id_type=MESH,
        )

    def each(far, action):
        for part in range(parts):
            for way, present, onward, block, target in (
                (0, me >= far, has_right, me - far, me + 1),
                (1, me + far < count, has_left, me + far, me - 1),
            ):
                action(far, part, way, present, onward, block, target)

    def start(far, part, way, present, onward, block, target):
        if far:

            @pl.when(present)
            def _():
                piece_copy(way, block, part, out_ref, target).wait_recv()

        @pl.when(present & onward)
        def _():
            piece_copy(way, block, part, out_ref if far else own_ref, target).start()

    def finish(far, part, way, present, onward, block, target):
        @pl.when(present & onward)
        def _():
            piece_copy(way, block, part, out_ref if far else own_ref, target).wait_send()

    def seq_start(hop, carry):
        seq_copy(hop).start()
        return carry

    def seq_finish(hop, carry):
        seq_copy(hop).wait()
        return carry

    lax.fori_loop(1, devices, seq_start, 0)
    seq_slots[here] = small_ref[...]
    each(0, start)
    lax.fori_loop(1, devices, seq_finish, 0)
    total = seq_slots[0]
    for index in range(1, devices):
        total = total + seq_slots[index]
    small_out[...] = total
    for hop in range(1, count):
        layer_copy(hop).start()
    layer_slots[me] = total[0:shared]
    for far in range(1, count):
        each(far, start)
    for hop in range(1, count):
        layer_copy(hop).wait()
    total = layer_slots[0]
    for index in range(1, count):
        total = total + layer_slots[index]
    small_out[0:shared, :] = total
    for far in range(count):
        each(far, finish)
    own_copy.wait()


def join_rows_and_sum(rows, small, shared, count, ident, parts=4):
    size, width = rows.shape
    devices = lax.axis_size("seq")
    joined, summed = pl.pallas_call(
        functools.partial(last_join_kernel, count, parts, shared),
        out_shape=[jax.ShapeDtypeStruct((count, size, width), rows.dtype), f32(*small.shape)],
        in_specs=[pl.BlockSpec(memory_space=pl.ANY), pl.BlockSpec(memory_space=pltpu.VMEM)],
        out_specs=[pl.BlockSpec(memory_space=pl.ANY), pl.BlockSpec(memory_space=pltpu.VMEM)],
        scratch_shapes=[
            pltpu.VMEM((devices,) + small.shape, jnp.float32),
            pltpu.VMEM((count, shared, small.shape[1]), jnp.float32),
            pltpu.SemaphoreType.DMA(()),
            pltpu.SemaphoreType.DMA((2, count, parts)),
            pltpu.SemaphoreType.DMA((count, parts)),
            pltpu.SemaphoreType.DMA((devices,)),
            pltpu.SemaphoreType.DMA((devices,)),
            pltpu.SemaphoreType.DMA((count,)),
            pltpu.SemaphoreType.DMA((count,)),
        ],
        compiler_params=pltpu.CompilerParams(collective_id=ident, has_side_effects=True),
        cost_estimate=busy(70),
        name="join_rows_and_sum",
    )(rows, small)
    return joined.reshape(count * size, width), summed


def start_kernel(
    x_ref,
    place_ref,
    out_ref,
    x_got,
    place_got,
    out_got,
    own_sem,
    x_send,
    x_recv,
    place_send,
    place_recv,
    out_send,
    out_recv,
):
    count, me = lax.axis_size("shard"), lax.axis_index("shard")
    devices, here = lax.axis_size("seq"), lax.axis_index("seq")
    barrier = pltpu.get_barrier_semaphore()

    def greet(hop, carry):
        other = lax.rem(here + hop, devices)
        pl.semaphore_signal(barrier, inc=1, device_id={"seq": other}, device_id_type=MESH)
        return carry

    lax.fori_loop(1, devices, greet, 0)
    for hop in range(1, count):
        other = lax.rem(me + hop, count)
        pl.semaphore_signal(barrier, inc=1, device_id={"shard": other}, device_id_type=MESH)
    own_copies = [
        pltpu.make_async_copy(x_ref.at[here], x_got.at[here], own_sem.at[0]),
        pltpu.make_async_copy(place_ref.at[here], place_got.at[here], own_sem.at[1]),
        pltpu.make_async_copy(out_ref, out_got.at[me], own_sem.at[2]),
    ]
    for copy in own_copies:
        copy.start()
    pl.semaphore_wait(barrier, devices + count - 2)

    def seq_copies(hop):
        other = lax.rem(here + hop, devices)
        return [
            pltpu.make_async_remote_copy(
                src_ref=source.at[other],
                dst_ref=target.at[here],
                send_sem=send.at[hop],
                recv_sem=recv.at[hop],
                device_id={"seq": other},
                device_id_type=MESH,
            )
            for source, target, send, recv in (
                (x_ref, x_got, x_send, x_recv),
                (place_ref, place_got, place_send, place_recv),
            )
        ]

    def out_copy(hop):
        return pltpu.make_async_remote_copy(
            src_ref=out_ref,
            dst_ref=out_got.at[me],
            send_sem=out_send.at[hop],
            recv_sem=out_recv.at[hop],
            device_id={"shard": lax.rem(me + hop, count)},
            device_id_type=MESH,
        )

    def start(hop, carry):
        for copy in seq_copies(hop):
            copy.start()
        return carry

    def finish(hop, carry):
        for copy in seq_copies(hop):
            copy.wait()
        return carry

    lax.fori_loop(1, devices, start, 0)
    for hop in range(1, count):
        out_copy(hop).start()
    lax.fori_loop(1, devices, finish, 0)
    for hop in range(1, count):
        out_copy(hop).wait()
    for copy in own_copies:
        copy.wait()


def start_exchange(rows, places, out_low, layers, ident):
    devices = rows.shape[0]
    dma = pltpu.SemaphoreType.DMA
    return pl.pallas_call(
        start_kernel,
        out_shape=[
            jax.ShapeDtypeStruct(rows.shape, rows.dtype),
            jax.ShapeDtypeStruct(places.shape, places.dtype),
            jax.ShapeDtypeStruct((layers,) + out_low.shape, out_low.dtype),
        ],
        in_specs=[pl.BlockSpec(memory_space=pl.ANY)] * 3,
        out_specs=[pl.BlockSpec(memory_space=pl.ANY)] * 3,
        scratch_shapes=[
            dma((3,)),
            dma((devices,)),
            dma((devices,)),
            dma((devices,)),
            dma((devices,)),
            dma((layers,)),
            dma((layers,)),
        ],
        compiler_params=pltpu.CompilerParams(collective_id=ident, has_side_effects=True),
        cost_estimate=busy(20),
        name="start_exchange",
    )(rows, places, out_low)


def total_join_kernel(
    count,
    parts,
    grads_ref,
    weights_ref,
    rows_ref,
    own_ref,
    out_ref,
    joined_ref,
    weigh_ref,
    grads,
    weights,
    rows_in,
    part_ref,
    weighed,
    from_left,
    from_right,
    load_sem,
    weigh_sem,
    own_sem,
    send_sem,
    recv_sem,
    join_send,
    join_recv,
):
    me, has_left, has_right = ends(count)
    size = out_ref.shape[0] // parts
    tile = 2 * HEAD
    width = out_ref.shape[1]
    loads = [
        pltpu.make_async_copy(source, target, load_sem.at[index])
        for index, (source, target) in enumerate(
            ((grads_ref, grads), (weights_ref, weights), (rows_ref, rows_in))
        )
    ]
    for load in loads:
        load.start()
    meet_neighbours(count)
    own_copy = pltpu.make_async_copy(own_ref, joined_ref.at[me], own_sem)
    own_copy.start()

    def sum_copy(way, block, part, source, target):
        rows = pl.ds(part * size, size)
        landing = (from_left, from_right)[way]
        return pltpu.make_async_remote_copy(
            src_ref=source.at[block, rows],
            dst_ref=landing.at[block, rows],
            send_sem=send_sem.at[way, block, part],
            recv_sem=recv_sem.at[way, block, part],
            device_id={"shard": target},
            device_id_type=MESH,
        )

    def join_copy(way, block, part, source, target):
        rows = pl.ds(part * size, size)
        return pltpu.make_async_remote_copy(
            src_ref=source.at[rows] if source is own_ref else source.at[block, rows],
            dst_ref=joined_ref.at[block, rows],
            send_sem=join_send.at[way, block, part],
            recv_sem=join_recv.at[block, part],
            device_id={"shard": target},
            device_id_type=MESH,
        )

    def sum_way(way, block):
        if way == 0:
            return me < block, has_left, me + 1
        return me > block, has_right, me - 1

    def join_way(far, way):
        if way == 0:
            return me >= far, has_right, me - far, me + 1
        return me + far < count, has_left, me + far, me - 1

    def join_start(far, way, part):
        present, onward, block, target = join_way(far, way)
        if far:

            @pl.when(present)
            def _():
                join_copy(way, block, part, joined_ref, target).wait_recv()

        @pl.when(present & onward)
        def _():
            join_copy(way, block, part, joined_ref if far else own_ref, target).start()

    def sum_start(way, block, part):
        sends, receives, target = sum_way(way, block)
        landing = (from_left, from_right)[way]
        rows = pl.ds(part * size, size)

        @pl.when(sends & receives)
        def _():
            sum_copy(way, block, part, landing, target).wait_recv()
            landing[block, rows, :] = (
                landing[block, rows, :].astype(jnp.float32)
                + part_ref[block, rows, :].astype(jnp.float32)
            ).astype(jnp.bfloat16)
            sum_copy(way, block, part, landing, target).start()

    for part in range(parts):
        for way in range(2):
            join_start(0, way, part)
    loads[0].wait()
    loads[1].wait()

    def block_turn(turn, carry):
        block = jnp.int32(0)
        for place in range(count):
            by_distance = sorted(range(count), key=lambda other: -abs(other - place))
            for index, other in enumerate(by_distance):
                block = jnp.where((me == place) & (turn == index), other, block)

        def tile_turn(index, inner_carry):
            across = pl.ds(pl.multiple_of(index * tile, tile), tile)
            part_ref[block, :, across] = low(
                product(grads[block], weights[across, :], ((1,), (1,)))
            )
            return inner_carry

        lax.fori_loop(0, width // tile, tile_turn, 0)

        @pl.when((block > me) & jnp.logical_not(has_left))
        def _():
            for part in range(parts):
                sum_copy(0, block, part, part_ref, me + 1).start()

        @pl.when((block < me) & jnp.logical_not(has_right))
        def _():
            for part in range(parts):
                sum_copy(1, block, part, part_ref, me - 1).start()

        return carry

    lax.fori_loop(0, count, block_turn, 0)
    loads[2].wait()
    wide = weights.shape[1]
    rows_total = count * out_ref.shape[0]

    def weigh_store(turn):
        rows = pl.ds(pl.multiple_of(turn * tile, tile), tile)
        return pltpu.make_async_copy(weighed.at[rows], weigh_ref.at[rows], weigh_sem.at[turn])

    def weigh_turn(turn, carry):
        rows = pl.ds(pl.multiple_of(turn * tile, tile), tile)
        turned = rows_in[:, rows].T

        def weigh_tile(first, span):
            against = grads[:, :, pl.ds(first, span)].reshape(rows_total, span)
            weighed[rows, pl.ds(first, span)] = low(product(turned, against))

        def tile_turn(index, inner_carry):
            weigh_tile(pl.multiple_of(index * tile, tile), tile)
            return inner_carry

        lax.fori_loop(0, wide // tile, tile_turn, 0)
        if wide % tile:
            weigh_tile(wide // tile * tile, wide % tile)
        weigh_store(turn).start()
        return carry

    for step in range(count):
        if step == min(2, count - 1):
            lax.fori_loop(0, width // tile, weigh_turn, 0)
        for part in range(parts):
            if step:
                for way in range(2):
                    join_start(step, way, part)
            if step < count - 1:
                sum_start(0, count - 1 - step, part)
                sum_start(1, step, part)

    for block in range(count):

        @pl.when(me == block)
        def _():
            for part in range(parts):
                rows = pl.ds(part * size, size)
                total = part_ref[block, rows, :].astype(jnp.float32)
                if block > 0:
                    sum_copy(0, block, part, from_left, me).wait_recv()
                    total = total + from_left[block, rows, :].astype(jnp.float32)
                if block < count - 1:
                    sum_copy(1, block, part, from_right, me).wait_recv()
                    total = total + from_right[block, rows, :].astype(jnp.float32)
                out_ref[rows, :] = total

    for step in range(count):
        for part in range(parts):
            for way in range(2):
                present, onward, block, target = join_way(step, way)

                @pl.when(present & onward)
                def _():
                    source = joined_ref if step else own_ref
                    join_copy(way, block, part, source, target).wait_send()

            if step < count - 1:
                for way, block in ((0, count - 1 - step), (1, step)):
                    sends, _, target = sum_way(way, block)

                    @pl.when(sends)
                    def _():
                        sum_copy(way, block, part, part_ref, target).wait_send()

    own_copy.wait()

    def weigh_finish(turn, carry):
        weigh_store(turn).wait()
        return carry

    lax.fori_loop(0, width // tile, weigh_finish, 0)


def total_and_join(grads, weights, rows, own, count, ident, parts=4):
    size, width = own.shape
    wide = grads.shape[1]
    total, joined, weighed = pl.pallas_call(
        functools.partial(total_join_kernel, count, parts),
        out_shape=[
            jax.ShapeDtypeStruct((size, width), jnp.float32),
            jax.ShapeDtypeStruct((count, size, width), own.dtype),
            bf16(width, wide),
        ],
        in_specs=[pl.BlockSpec(memory_space=pl.ANY)] * 4,
        out_specs=[pl.BlockSpec(memory_space=pltpu.VMEM)] + [pl.BlockSpec(memory_space=pl.ANY)] * 2,
        scratch_shapes=[
            pltpu.VMEM((count, size, wide), jnp.bfloat16),
            pltpu.VMEM((width, wide), jnp.bfloat16),
            pltpu.VMEM((count * size, width), jnp.bfloat16),
            pltpu.VMEM((count, size, width), jnp.bfloat16),
            pltpu.VMEM((width, wide), jnp.bfloat16),
            pltpu.VMEM((count, size, width), jnp.bfloat16),
            pltpu.VMEM((count, size, width), jnp.bfloat16),
            pltpu.SemaphoreType.DMA((3,)),
            pltpu.SemaphoreType.DMA((width // (2 * HEAD),)),
            pltpu.SemaphoreType.DMA(()),
            pltpu.SemaphoreType.DMA((2, count, parts)),
            pltpu.SemaphoreType.DMA((2, count, parts)),
            pltpu.SemaphoreType.DMA((2, count, parts)),
            pltpu.SemaphoreType.DMA((count, parts)),
        ],
        compiler_params=pltpu.CompilerParams(
            collective_id=ident, has_side_effects=True, vmem_limit_bytes=60 * 1024 * 1024
        ),
        cost_estimate=busy(95),
        name="total_and_join",
    )(grads.reshape(count, size, wide), weights, rows, own)
    return total, joined.reshape(count * size, width), weighed


def feed_kernel(
    count,
    parts,
    own_ref,
    dy_ref,
    gate_up_ref,
    down_ref,
    down_part_out,
    grad_open_out,
    grad_down_out,
    total_ref,
    gate_up,
    down,
    dy,
    rows_all,
    hidden,
    d_both,
    partial,
    landing,
    down_part,
    open_stage,
    down_stage,
    load_sem,
    part_sem,
    open_sem,
    down_sem,
    join_send,
    join_recv,
    sum_send,
    sum_recv,
):
    me, has_left, has_right = ends(count)
    units, width = down.shape
    piece = own_ref.shape[0] // parts
    tile = 2 * HEAD
    loads = [
        pltpu.make_async_copy(gate_up_ref, gate_up, load_sem.at[0]),
        pltpu.make_async_copy(dy_ref, dy, load_sem.at[1]),
        pltpu.make_async_copy(down_ref, down, load_sem.at[2]),
    ]
    for load in loads:
        load.start()
    rows_all[me] = own_ref[...]
    meet_neighbours(count)

    def part_store(block):
        return pltpu.make_async_copy(
            down_part.at[block], down_part_out.at[block], part_sem.at[block]
        )

    def open_store(turn):
        slot = lax.rem(turn, 2)
        rows = pl.ds(pl.multiple_of(turn * tile, tile), tile)
        return pltpu.make_async_copy(
            open_stage.at[slot], grad_open_out.at[rows], open_sem.at[slot]
        )

    def down_store(turn, size):
        slot = lax.rem(turn, 2)
        rows = pl.ds(pl.multiple_of(turn * tile, tile), size)
        return pltpu.make_async_copy(
            down_stage.at[slot, pl.ds(0, size)], grad_down_out.at[rows], down_sem.at[slot]
        )

    def join_copy(way, block, part):
        rows = pl.ds(part * piece, piece)
        return pltpu.make_async_remote_copy(
            src_ref=rows_all.at[block, rows],
            dst_ref=rows_all.at[block, rows],
            send_sem=join_send.at[way, block, part],
            recv_sem=join_recv.at[block, part],
            device_id={"shard": me - 1 if way else me + 1},
            device_id_type=MESH,
        )

    def sum_copy(way, block, part, source):
        rows = pl.ds(part * piece, piece)
        target = me - 1 if way else me + 1
        slot = jnp.where(block == target, count, block) if way else block
        return pltpu.make_async_remote_copy(
            src_ref=source.at[block, rows],
            dst_ref=landing.at[slot, rows],
            send_sem=sum_send.at[way, block, part],
            recv_sem=sum_recv.at[way, block, part],
            device_id={"shard": target},
            device_id_type=MESH,
        )

    def open_tile(block, first, size):
        across = pl.ds(first, size)
        beyond = pl.ds(pl.multiple_of(units + first, HEAD), size)
        rows = rows_all[block]
        gate = jnp.dot(rows, gate_up[:, across], preferred_element_type=jnp.float32)
        up = jnp.dot(rows, gate_up[:, beyond], preferred_element_type=jnp.float32)
        d_hidden = product(dy[block], down[across, :], ((1,), (1,)))
        opened = sigmoid(gate)
        wave = gate * opened
        hidden[block, :, across] = low(wave * up)
        d_both[block, :, across] = low(d_hidden * up * (opened * (1.0 + gate * (1.0 - opened))))
        d_both[block, :, beyond] = low(d_hidden * wave)

    def compute(block):
        def open_turn(turn, carry):
            open_tile(block, pl.multiple_of(turn * tile, tile), tile)
            return carry

        lax.fori_loop(0, units // tile, open_turn, 0)
        if units % tile:
            open_tile(block, units // tile * tile, units % tile)

        def close_turn(turn, carry):
            across = pl.ds(pl.multiple_of(turn * tile, tile), tile)
            partial[block, :, across] = low(
                product(d_both[block], gate_up[across, :], ((1,), (1,)))
            )
            return carry

        def down_turn(turn, carry):
            across = pl.ds(pl.multiple_of(turn * tile, tile), tile)
            down_part[block, :, across] = low(product(hidden[block], down[:, across]))
            return carry

        lax.fori_loop(0, width // tile, close_turn, 0)
        lax.fori_loop(0, width // tile, down_turn, 0)

    def slot_turn(slot, carry):
        far = (slot + 1) // 2
        rightward = lax.rem(slot, 2) == 1

        @pl.when(slot == 0)
        def _():
            for part in range(parts):

                @pl.when(has_right)
                def _():
                    join_copy(0, me, part).start()

                @pl.when(has_left)
                def _():
                    join_copy(1, me, part).start()

            for load in loads:
                load.wait()

        @pl.when(rightward)
        def _():
            for part in range(parts):
                for way, present, onward, block in (
                    (0, me >= far, has_right, me - far),
                    (1, me + far < count, has_left, me + far),
                ):

                    @pl.when(present)
                    def _():
                        join_copy(way, block, part).wait_recv()

                    @pl.when(present & onward)
                    def _():
                        join_copy(way, block, part).start()

        block = jnp.where(rightward, me - far, me + far)

        @pl.when((block >= 0) & (block < count))
        def _():
            compute(block)
            part_store(block).start()

            @pl.when((block > me) & jnp.logical_not(has_left))
            def _():
                for part in range(parts):
                    sum_copy(0, block, part, partial).start()

            @pl.when((block < me) & jnp.logical_not(has_right))
            def _():
                for part in range(parts):
                    sum_copy(1, block, part, partial).start()

        return carry

    lax.fori_loop(0, 2 * count - 1, slot_turn, 0)

    def add_on(way, block, part):
        rows = pl.ds(part * piece, piece)
        sum_copy(way, block, part, landing).wait_recv()
        landing[block, rows, :] = low(
            landing[block, rows, :].astype(jnp.float32)
            + partial[block, rows, :].astype(jnp.float32)
        )
        sum_copy(way, block, part, landing).start()

    rows_total = count * own_ref.shape[0]

    def weigh(left, right, stage, across_count):
        turned = left.reshape(rows_total, left.shape[2]).T

        span = across_count * tile // 2

        def turn_of(turn, carry):
            across = pl.ds(pl.multiple_of(turn * span, HEAD), span)
            against = right[:, :, across].reshape(rows_total, span)
            stage[:, across] = low(product(turned, against))
            return carry

        lax.fori_loop(0, 2, turn_of, 0)

    open_count = width // tile
    down_count, down_rest = units // tile, units % tile

    def late_turn(turn, carry):
        step, part = 2 + turn // parts, lax.rem(turn, parts)

        @pl.when((step < count) & (me < step) & has_left)
        def _():
            add_on(0, step, part)

        @pl.when((step < count) & (me > count - 1 - step) & has_right)
        def _():
            add_on(1, count - 1 - step, part)

        slot = lax.rem(turn, 2)
        cols = pl.ds(pl.multiple_of(turn * tile, tile), tile)

        @pl.when(turn < open_count)
        def _():
            @pl.when(turn >= 2)
            def _():
                open_store(turn - 2).wait()

            weigh(rows_all[:, :, cols], d_both, open_stage.at[slot], 2 * units // tile)
            open_store(turn).start()

        @pl.when(turn < down_count)
        def _():
            @pl.when(turn >= 2)
            def _():
                down_store(turn - 2, tile).wait()

            weigh(hidden[:, :, cols], dy, down_stage.at[slot], width // tile)
            down_store(turn, tile).start()

        return carry

    late_count = max((count - 2) * parts, open_count)
    lax.fori_loop(0, late_count, late_turn, 0)
    for turn in range(max(0, open_count - 2), open_count):
        open_store(turn).wait()
    for turn in range(max(0, down_count - 2), down_count):
        down_store(turn, tile).wait()
    if down_rest:
        weigh(
            hidden[:, :, down_count * tile :],
            dy,
            down_stage.at[down_count % 2, pl.ds(0, down_rest)],
            width // tile,
        )
        down_store(down_count, down_rest).start()

    for part in range(parts):
        rows = pl.ds(part * piece, piece)
        total_ref[rows, :] = partial[me, rows, :].astype(jnp.float32)

        @pl.when(has_left)
        def _():
            sum_copy(0, me, part, landing).wait_recv()
            total_ref[rows, :] += landing[me, rows, :].astype(jnp.float32)

        @pl.when(has_right)
        def _():
            sum_copy(1, me, part, landing).wait_recv()
            total_ref[rows, :] += landing[count, rows, :].astype(jnp.float32)

    for block in range(count):
        for part in range(parts):

            @pl.when((me >= block) & has_right)
            def _():
                join_copy(0, block, part).wait_send()

            @pl.when((me <= block) & has_left)
            def _():
                join_copy(1, block, part).wait_send()

            @pl.when(me < block)
            def _():
                sum_copy(0, block, part, partial).wait_send()

            @pl.when(me > block)
            def _():
                sum_copy(1, block, part, partial).wait_send()

        part_store(block).wait()

    if down_rest:
        down_store(down_count, down_rest).wait()


def feed_forward(own, dy, gate_up_mat, down_mat, count, ident, parts=4):
    size, width = own.shape
    units = down_mat.shape[0]
    dma = pltpu.SemaphoreType.DMA
    down_part, grad_open, grad_down, total = pl.pallas_call(
        functools.partial(feed_kernel, count, parts),
        out_shape=[
            bf16(count, size, width),
            bf16(width, 2 * units),
            bf16(units, width),
            f32(size, width),
        ],
        in_specs=[pl.BlockSpec(memory_space=pltpu.VMEM)] + [pl.BlockSpec(memory_space=pl.ANY)] * 3,
        out_specs=[pl.BlockSpec(memory_space=pl.ANY)] * 3 + [pl.BlockSpec(memory_space=pltpu.VMEM)],
        scratch_shapes=[
            pltpu.VMEM((width, 2 * units), jnp.bfloat16),
            pltpu.VMEM((units, width), jnp.bfloat16),
            pltpu.VMEM((count, size, width), jnp.bfloat16),
            pltpu.VMEM((count, size, width), jnp.bfloat16),
            pltpu.VMEM((count, size, units), jnp.bfloat16),
            pltpu.VMEM((count, size, 2 * units), jnp.bfloat16),
            pltpu.VMEM((count, size, width), jnp.bfloat16),
            pltpu.VMEM((count + 1, size, width), jnp.bfloat16),
            pltpu.VMEM((count, size, width), jnp.bfloat16),
            pltpu.VMEM((2, 2 * HEAD, 2 * units), jnp.bfloat16),
            pltpu.VMEM((2, 2 * HEAD, width), jnp.bfloat16),
            dma((3,)),
            dma((count,)),
            dma((2,)),
            dma((2,)),
            dma((2, count, parts)),
            dma((count, parts)),
            dma((2, count, parts)),
            dma((2, count, parts)),
        ],
        compiler_params=pltpu.CompilerParams(
            collective_id=ident, has_side_effects=True, vmem_limit_bytes=63 * 1024 * 1024
        ),
        cost_estimate=busy(120),
        name="feed_forward",
    )(own, dy.reshape(count, size, width), gate_up_mat, down_mat)
    return down_part.reshape(count * size, width), grad_open, grad_down, total


def per_device(
    hidden_in,
    out_grad,
    deal,
    lengths,
    qkv_weight,
    qkv_first,
    qkv_second,
    beta_weight,
    beta_first,
    beta_second,
    out_weight,
    out_first,
    out_second,
    gate_up_weight,
    gate_up_first,
    gate_up_second,
    down_weight,
    down_first,
    down_second,
    conv_weight,
    conv_first,
    conv_second,
    gains,
    gains_first,
    gains_second,
):
    row_count, model_width = hidden_in.shape
    heads = beta_weight.shape[1]
    inner = qkv_weight.shape[2]
    units = down_weight.shape[0]
    devices = lax.axis_size("seq")
    layers = lax.axis_size("shard")
    place = lax.axis_index("shard")
    longest = {4: 4096, 16: 8192}[lengths.shape[0]]
    hops = min(devices - 1, -(-longest // row_count))
    share = row_count // devices // layers
    quarter = devices * share
    _, order, sent_place = lax.sort(
        (deal // row_count, jnp.arange(row_count, dtype=jnp.int32), deal % row_count), num_keys=1
    )
    ordered = order.reshape(devices, layers, share)
    own_order = lax.dynamic_index_in_dim(ordered, place, 1, keepdims=False).reshape(quarter)
    by_layer = jnp.swapaxes(ordered, 0, 1).reshape(row_count)
    chosen = one_hot(own_order, row_count)
    sorting = one_hot(by_layer, row_count)

    def exchanged(rows):
        width = rows.shape[-1]
        return lax.all_to_all(
            rows.reshape(devices, share, width), "seq", split_axis=0, concat_axis=0, tiled=True
        ).reshape(quarter, width)

    plane = (share, model_width) if share % 16 == 0 else (share * model_width // HEAD, HEAD)
    chosen_x = moved_back(chosen, hidden_in).reshape((devices,) + plane)
    sent_place = sent_place.reshape(devices, 1, layers * share)
    sent_place = jnp.pad(sent_place, ((0, 0), (0, 0), (0, -(layers * share) % HEAD)))
    own_x, got_place, out_rows = start_exchange(
        chosen_x, sent_place, low(out_weight), layers, 9
    )
    own_x = own_x.reshape(quarter, model_width).astype(jnp.float32)
    out_rows = out_rows.reshape(layers * inner, out_weight.shape[1])
    got_place = got_place[:, 0, : layers * share]
    all_dy = lax.all_to_all(
        moved_back(one_hot(order, row_count), out_grad).reshape(
            devices, layers, share, model_width
        ),
        "seq",
        split_axis=0,
        concat_axis=0,
        tiled=True,
    )

    first_place = lax.axis_index("seq") * row_count
    places = first_place + jnp.arange(0, row_count, GROUP, dtype=jnp.int32)
    starts = jnp.cumsum(lengths) - lengths
    keep = jnp.all(starts[None, :] != places[:, None], axis=1).astype(jnp.float32)

    beta_pad = jnp.zeros((beta_weight.shape[0], HEAD - heads), jnp.bfloat16)
    mixer_mat = lax.all_gather(
        jnp.concatenate(
            [low(qkv_weight[:, item]) for item in range(3)] + [low(beta_weight), beta_pad], axis=1
        ),
        "seq",
        axis=0,
        tiled=True,
    )
    out_mat = lax.all_gather(out_rows, "seq", axis=1, tiled=True)
    gate_up_mat = lax.all_gather(
        low(gate_up_weight).reshape(-1, 2 * units), "seq", axis=0, tiled=True
    )
    down_mat = lax.all_gather(low(down_weight), "seq", axis=1, tiled=True)
    gain_in = gains[:model_width]
    gain_ff = gains[model_width : 2 * model_width]
    gain_out = gains[2 * model_width :].reshape(1, HEAD)
    conv_mat = conv_weight.reshape(TAPS, 3 * inner)

    normed_in = join_rows(low(rms_unit(own_x) * gain_in), layers, 0)
    normed_in, all_dy = lax.optimization_barrier((normed_in, all_dy))
    got_place = jnp.swapaxes(got_place.reshape(devices, layers, share), 0, 1).reshape(row_count)
    to_chain = one_hot(got_place, row_count)
    all_dy = jnp.swapaxes(all_dy, 0, 1).reshape(row_count, model_width)
    own_dy = lax.dynamic_slice_in_dim(all_dy, place * quarter, quarter, 0)
    mixed_in = product(normed_in, mixer_mat)
    logits = mixed_in[:, 3 * inner :]
    logits_high = low(logits)
    logits_low = low(logits - logits_high.astype(jnp.float32))
    chain_in = product(
        to_chain,
        jnp.concatenate([low(mixed_in[:, : 3 * inner]), logits_high, logits_low], axis=1),
    )
    projected = low(chain_in[:, : 3 * inner])
    logits = (
        chain_in[:, 3 * inner : 3 * inner + heads]
        + chain_in[:, 3 * inner + HEAD : 3 * inner + HEAD + heads]
    )
    edge_rows = passed_along(projected[row_count - 8 :], "seq", 1).astype(jnp.float32)
    edge_rows = edge_rows * (jnp.arange(8) >= 8 - (TAPS - 1)).astype(jnp.float32)[:, None]
    rule = Rule(keep, heads, row_count)
    conv, solved, square, step, fresh, reach, zero_out, total = rule.maps(
        projected, edge_rows, logits, conv_mat
    )
    incoming = relayed(total, total[:, :, HEAD:], hops, False, 7)
    state, mixed, normed = rule.outputs(incoming, step, fresh, reach, zero_out, gain_out)

    normed = moved_back(to_chain, normed)
    own_normed = swap_blocks(normed.reshape(layers, quarter, inner), layers, 1, True)
    residual = own_x + product(own_normed, out_mat)
    result, grad_gate_up, grad_down, d_normed_ff = feed_forward(
        low(rms_unit(residual) * gain_ff), all_dy, gate_up_mat, down_mat, layers, 2
    )
    red_down = seq_summed(grad_down, 1)
    d_residual, grad_gain_ff = rms_back(residual, gain_ff, d_normed_ff)
    d_residual = own_dy.astype(jnp.float32) + d_residual
    own_mix = low(d_residual)
    all_mix = join_rows(own_mix, layers, 4)
    out_own = lax.dynamic_slice_in_dim(out_mat, place * inner, inner, 0)
    d_normed = low(product(all_mix, out_own, ((1,), (1,))))
    d_normed, grad_gate_up, result = lax.optimization_barrier((d_normed, grad_gate_up, result))
    result = lax.psum_scatter(result, "shard", scatter_dimension=0, tiled=True)
    red_gate_up = seq_summed(grad_gate_up, 0)
    d_normed = product(to_chain, d_normed)
    d_mixed, d_first_state, grad_gain_out = rule.tail(d_normed, mixed, gain_out, step, reach)
    d_mixed, red_down = lax.optimization_barrier((d_mixed, red_down))
    outgoing = relayed(total, d_first_state, hops, True, 8)
    d_pre, d_tail, d_edge, grad_taps = rule.back(
        outgoing, projected, edge_rows, logits, conv_mat, conv, solved, square, step, reach, state,
        d_mixed,
    )
    d_tail = low(d_tail + passed_along(d_edge, "seq", -1))
    d_pre = lax.dynamic_update_slice(d_pre, d_tail, (row_count - 8, 0))
    d_pre, all_mix = lax.optimization_barrier((d_pre, all_mix))
    d_mixed_in = moved_back(to_chain, d_pre)
    grad_out = low(product(normed, all_mix, ((0,), (0,))))
    red_out = seq_summed(grad_out, 1)
    d_mixed_in, result = lax.optimization_barrier((d_mixed_in, result))
    result = exchanged(low(residual + result.astype(jnp.float32)))
    red_down = red_down.astype(jnp.float32)
    down_new = adamw(down_weight, down_first, down_second, red_down, RATE_DOWN, SHRINK)
    result, *down_new = lax.optimization_barrier((result, *down_new))
    d_normed_in, result, grad_mixer = total_and_join(
        d_mixed_in, mixer_mat, normed_in, result, layers, 5
    )
    d_normed_in, red_gate_up, red_out = lax.optimization_barrier(
        (d_normed_in, red_gate_up, red_out)
    )
    d_input, grad_gain_in = rms_back(own_x, gain_in, d_normed_in)
    d_input = exchanged(low(d_residual + d_input))
    red_gate_up = red_gate_up.astype(jnp.float32).reshape(gate_up_weight.shape)
    gate_up_new = adamw(
        gate_up_weight, gate_up_first, gate_up_second, red_gate_up, RATE_WIDE, SHRINK
    )
    d_input, grad_mixer, *gate_up_new = lax.optimization_barrier(
        (d_input, grad_mixer, *gate_up_new)
    )
    red_mixer = seq_summed(grad_mixer, 0)
    shared = -(-gains.shape[0] // (8 * HEAD)) * 8
    small = jnp.concatenate(
        [
            grad_gain_in,
            grad_gain_ff,
            grad_gain_out.reshape(HEAD),
            jnp.zeros((shared * HEAD - gains.shape[0],), jnp.float32),
            grad_taps.reshape(-1),
        ]
    ).reshape(-1, HEAD)
    d_input, small_sum = join_rows_and_sum(d_input, small, shared, layers, 6)
    d_input, red_mixer = lax.optimization_barrier((d_input, red_mixer))


    red_mixer = red_mixer.astype(jnp.float32)
    red_qkv = jnp.stack(
        [red_mixer[:, item * inner : (item + 1) * inner] for item in range(3)], axis=1
    )
    red_beta = red_mixer[:, 3 * inner : 3 * inner + heads]
    red_out = red_out.astype(jnp.float32)
    red_conv = small_sum[shared:].reshape(conv_weight.shape)
    red_gains = small_sum[:shared].reshape(-1)[: gains.shape[0]]
    qkv_new = adamw(qkv_weight, qkv_first, qkv_second, red_qkv, RATE_WIDE, SHRINK)
    beta_new = adamw(beta_weight, beta_first, beta_second, red_beta, RATE_WIDE, SHRINK)
    out_new = adamw(out_weight, out_first, out_second, red_out, RATE_WIDE, SHRINK)
    conv_new = adamw(conv_weight, conv_first, conv_second, red_conv, RATE_CONV, 0.0)
    gains_new = adamw(gains, gains_first, gains_second, red_gains, RATE_GAIN, 0.0)
    return (
        moved(sorting, result),
        moved(sorting, d_input),
        *qkv_new,
        *beta_new,
        *out_new,
        *gate_up_new,
        *down_new,
        *conv_new,
        *gains_new,
    )


def solution(mesh):
    return jax.shard_map(
        per_device,
        mesh=mesh,
        in_specs=(
            P("seq", None),
            P("seq", None),
            P("seq"),
            P(),
            P("seq", None, "shard"),
            P("seq", None, "shard"),
            P("seq", None, "shard"),
            P("seq", "shard"),
            P("seq", "shard"),
            P("seq", "shard"),
            P("shard", "seq"),
            P("shard", "seq"),
            P("shard", "seq"),
            P("seq", None, "shard"),
            P("seq", None, "shard"),
            P("seq", None, "shard"),
            P("shard", "seq"),
            P("shard", "seq"),
            P("shard", "seq"),
            P(None, None, "shard"),
            P(None, None, "shard"),
            P(None, None, "shard"),
            P(),
            P(),
            P(),
        ),
        out_specs=(
            P("seq", None),
            P("seq", None),
            P("seq", None, "shard"),
            P("seq", None, "shard"),
            P("seq", None, "shard"),
            P("seq", "shard"),
            P("seq", "shard"),
            P("seq", "shard"),
            P("shard", "seq"),
            P("shard", "seq"),
            P("shard", "seq"),
            P("seq", None, "shard"),
            P("seq", None, "shard"),
            P("seq", None, "shard"),
            P("shard", "seq"),
            P("shard", "seq"),
            P("shard", "seq"),
            P(None, None, "shard"),
            P(None, None, "shard"),
            P(None, None, "shard"),
            P(),
            P(),
            P(),
        ),
        check_vma=False,
    )
```

```python
import functools

import jax
import jax.numpy as jnp
from jax import lax
from jax.experimental import pallas as pl
from jax.experimental.pallas import tpu as pltpu
from jax.sharding import PartitionSpec as P

HEAD = 128
TAPS = 4
GROUP = 64
BUSY_FLOPS = 10_000_000
MAPS_BATCH = 4
CHAIN_BATCH = 4
BACK_BATCH = 2
STEP = 10


EPSILON = 1e-06
PRECISE = lax.Precision.HIGHEST
MESH = pl.DeviceIdType.MESH
FIRST_DECAY = 0.9
SECOND_DECAY = 0.95
ADAM_EPSILON = 1e-08
RATE_WIDE = 0.044
RATE_DOWN = 0.027
RATE_CONV = 0.8
RATE_GAIN = 0.3
SHRINK = 0.1


def halves(value):
    high = value.astype(jnp.bfloat16)
    return high, (value - high.astype(jnp.float32)).astype(jnp.bfloat16)


def mul(left, right, dims=((1,), (0,))):
    def one(a, b):
        return lax.dot_general(a, b, (dims, ((), ())), preferred_element_type=jnp.float32)

    left_high, left_low = halves(left)
    right_high, right_low = halves(right)
    return one(left_high, right_high) + (one(left_high, right_low) + one(left_low, right_high))


def mul_nt(left, right):
    return mul(left, right, ((1,), (1,)))


def quick(left, right, dims=((1,), (0,))):
    return lax.dot_general(
        left.astype(jnp.bfloat16),
        right.astype(jnp.bfloat16),
        (dims, ((), ())),
        preferred_element_type=jnp.float32,
    )


def quick_nt(left, right):
    return quick(left, right, ((1,), (1,)))


def grid_indices(size):
    return (
        lax.broadcasted_iota(jnp.int32, (size, size), 0),
        lax.broadcasted_iota(jnp.int32, (size, size), 1),
    )


def unit_lower_inverses(strict_parts):
    size = strict_parts[0].shape[0]
    rows, cols = grid_indices(size)
    inverses = [jnp.where(rows == cols, 1.0, 0.0) for _ in strict_parts]
    level = 0
    while (1 << level) < size:
        corner = (
            ((rows >> (level + 1)) == (cols >> (level + 1)))
            & (((rows >> level) & 1) == 1)
            & (((cols >> level) & 1) == 0)
        )
        parts = [jnp.where(corner, strict, 0.0) for strict in strict_parts]
        if level == 0:
            inverses = [inverse - part for inverse, part in zip(inverses, parts)]
        else:
            inner = [mul(part, inverse) for inverse, part in zip(inverses, parts)]
            outer = [mul(inverse, part) for inverse, part in zip(inverses, inner)]
            inverses = [inverse - part for inverse, part in zip(inverses, outer)]
        level += 1
    return inverses


def sigmoid(value):
    return 1.0 / (1.0 + jnp.exp(-value))


def unit_scale(act):
    return lax.rsqrt(jnp.sum(act * act, axis=-1, keepdims=True) + EPSILON)


def head_lanes(column):
    return slice(column * HEAD, (column + 1) * HEAD)


def maps_kernel(
    heads,
    batch,
    keep_ref,
    pre_ref,
    edge_ref,
    logit_ref,
    taps_ref,
    conv_ref,
    solved_ref,
    square_ref,
    step_ref,
    fresh_ref,
    reach_ref,
    zero_out_ref,
    total_ref,
    history,
    running,
):
    turn = pl.program_id(0)
    scale = HEAD**-0.5
    pairs = [(item, head) for item in range(batch) for head in range(heads)]
    keeps = [keep_ref[turn * batch + item] for item in range(batch)]

    @pl.when(turn == 0)
    def _():
        history[0, 0:8, :] = edge_ref[...] * keeps[0]
        rows, cols = grid_indices(HEAD)
        start = jnp.where(rows == cols, 1.0, 0.0)
        for head in range(heads):
            running[head, :, 0:HEAD] = start
            running[head, :, HEAD : 2 * HEAD] = jnp.zeros((HEAD, HEAD), jnp.float32)

    @pl.when(turn > 0)
    def _():
        history[0, 0:8, :] = history[batch - 1, GROUP : GROUP + 8, :] * keeps[0]

    for item in range(batch):
        history[item, 8 : GROUP + 8, :] = pre_ref[
            item * GROUP : (item + 1) * GROUP, :
        ].astype(jnp.float32)
        if item:
            history[item, 0:8, :] = history[item - 1, GROUP : GROUP + 8, :] * keeps[item]

    def conv_of(item, column):
        cols = head_lanes(column)
        total = taps_ref[0:1, cols] * history[item, 5 : 5 + GROUP, cols]
        for tap in range(1, TAPS):
            shifted = history[item, 5 + tap : 5 + tap + GROUP, cols]
            total = total + taps_ref[tap : tap + 1, cols] * shifted
        conv_ref[item * GROUP : (item + 1) * GROUP, cols] = total
        return total * sigmoid(total)

    rows, cols = grid_indices(GROUP)
    big_rows, big_cols = grid_indices(HEAD)
    keys = [conv_of(item, heads + head) for item, head in pairs]
    keys = [key * unit_scale(key) for key in keys]
    strengths = [
        sigmoid(logit_ref[item * GROUP : (item + 1) * GROUP, head : head + 1])
        for item, head in pairs
    ]
    overlaps = [mul_nt(key, key) for key in keys]
    inverses = unit_lower_inverses(
        [
            jnp.where(rows > cols, strength * overlap, 0.0)
            for strength, overlap in zip(strengths, overlaps)
        ]
    )
    queries = [conv_of(item, head) for item, head in pairs]
    queries = [query * unit_scale(query) for query in queries]
    scores = [
        jnp.where(rows >= cols, mul_nt(query, key), 0.0) for query, key in zip(queries, keys)
    ]
    values = [conv_of(item, 2 * heads + head) for item, head in pairs]
    solved = [
        mul(inverse, jnp.concatenate([strength * key, strength * value], axis=1))
        for inverse, strength, key, value in zip(inverses, strengths, keys, values)
    ]
    pushed = [mul(key.T, part) for key, part in zip(keys, solved)]
    mixed = [mul(score, part) for score, part in zip(scores, solved)]
    steps = [jnp.where(big_rows == big_cols, 1.0, 0.0) - part[:, 0:HEAD] for part in pushed]
    for index, (item, head) in enumerate(pairs):
        here = slice(item * GROUP, (item + 1) * GROUP)
        solved_ref[item, head] = solved[index]
        square_ref[item, head, :, 0:GROUP] = inverses[index]
        square_ref[item, head, :, GROUP : 2 * GROUP] = scores[index]
        reach_ref[here, head_lanes(head)] = scale * (queries[index] - mixed[index][:, 0:HEAD])
        zero_out_ref[here, head_lanes(head)] = scale * mixed[index][:, HEAD:]
        step_ref[item, head] = steps[index]
        fresh_ref[item, head] = pushed[index][:, HEAD:]
    now = [running[head] for head in range(heads)]
    for item in range(batch):
        first = item * heads
        moved = [mul(steps[first + head], now[head] * keeps[item]) for head in range(heads)]
        now = [
            jnp.concatenate(
                [moved[head][:, 0:HEAD], moved[head][:, HEAD:] + pushed[first + head][:, HEAD:]],
                axis=1,
            )
            for head in range(heads)
        ]
    for head in range(heads):
        running[head] = now[head]
    total_ref[...] = running[...]


def outputs_kernel(
    heads,
    batch,
    keep_ref,
    incoming_ref,
    step_ref,
    fresh_ref,
    reach_ref,
    zero_out_ref,
    gain_ref,
    state_ref,
    mixed_ref,
    normed_ref,
    running,
):
    turn = pl.program_id(0)

    @pl.when(turn == 0)
    def _():
        running[...] = incoming_ref[...]

    now = [running[head] for head in range(heads)]
    states = []
    for item in range(batch):
        keep = keep_ref[turn * batch + item]
        now = [state * keep for state in now]
        states.append(now)
        now = [
            mul(step_ref[item, head], now[head]) + fresh_ref[item, head] for head in range(heads)
        ]
    for head in range(heads):
        running[head] = now[head]
    for item in range(batch):
        here = slice(item * GROUP, (item + 1) * GROUP)
        outs = [
            mul(reach_ref[here, head_lanes(head)], states[item][head])
            + zero_out_ref[here, head_lanes(head)]
            for head in range(heads)
        ]
        for head, mixed in enumerate(outs):
            state_ref[item, head] = states[item][head]
            mixed_ref[here, head_lanes(head)] = mixed
            inverse_rms = lax.rsqrt(jnp.mean(mixed * mixed, axis=-1, keepdims=True) + EPSILON)
            normed_ref[here, head_lanes(head)] = (mixed * inverse_rms * gain_ref[...]).astype(
                jnp.bfloat16
            )


def tail_kernel(
    heads,
    batch,
    keep_ref,
    d_normed_ref,
    mixed_ref,
    gain_ref,
    step_ref,
    reach_ref,
    d_mixed_ref,
    d_state_ref,
    d_gain_ref,
    running,
):
    turn = pl.num_programs(0) - 1 - pl.program_id(0)

    @pl.when(pl.program_id(0) == 0)
    def _():
        running[...] = jnp.zeros_like(running)
        d_gain_ref[...] = jnp.zeros_like(d_gain_ref)

    gain_sum = jnp.zeros((1, HEAD), jnp.float32)
    pulled = []
    for item in range(batch):
        here = slice(item * GROUP, (item + 1) * GROUP)
        grads = []
        for head in range(heads):
            mixed = mixed_ref[here, head_lanes(head)]
            d_normed = d_normed_ref[here, head_lanes(head)]
            inverse_rms = lax.rsqrt(jnp.mean(mixed * mixed, axis=-1, keepdims=True) + EPSILON)
            unit = mixed * inverse_rms
            gain_sum = gain_sum + jnp.sum(d_normed * unit, axis=0, keepdims=True)
            d_unit = d_normed * gain_ref[...]
            d_mixed = inverse_rms * (
                d_unit - unit * jnp.mean(d_unit * unit, axis=-1, keepdims=True)
            )
            d_mixed_ref[here, head_lanes(head)] = d_mixed
            grads.append(d_mixed)
        pulled.append(
            [mul(reach_ref[here, head_lanes(head)].T, grads[head]) for head in range(heads)]
        )
    now = [running[head] for head in range(heads)]
    for item in reversed(range(batch)):
        keep = keep_ref[turn * batch + item]
        now = [
            keep * (mul(step_ref[item, head].T, now[head]) + pulled[item][head])
            for head in range(heads)
        ]
    for head in range(heads):
        running[head] = now[head]
    d_gain_ref[...] += gain_sum
    d_state_ref[...] = running[...]


def back_kernel(
    heads,
    batch,
    keep_ref,
    outgoing_ref,
    pre_ref,
    edge_ref,
    logit_ref,
    taps_ref,
    conv_ref,
    solved_ref,
    square_ref,
    step_ref,
    reach_ref,
    state_ref,
    d_mixed_ref,
    d_pre_ref,
    d_tail_ref,
    d_edge_ref,
    d_taps_ref,
    d_history,
    edge_history,
    running,
):
    count = pl.num_programs(0)
    turn = count - 1 - pl.program_id(0)
    scale = HEAD**-0.5
    rows, cols = grid_indices(GROUP)
    pairs = [(item, head) for item in range(batch) for head in range(heads)]
    indices = range(len(pairs))
    keeps = [keep_ref[turn * batch + item] for item in range(batch)]

    @pl.when(pl.program_id(0) == 0)
    def _():
        running[...] = outgoing_ref[...]
        d_history[batch - 1, GROUP : GROUP + 8, :] = jnp.zeros(
            (8, d_history.shape[2]), jnp.float32
        )
        d_taps_ref[...] = jnp.zeros_like(d_taps_ref)

    @pl.when(pl.program_id(0) > 0)
    def _():
        d_history[batch - 1, GROUP : GROUP + 8, :] = (
            d_history[0, 0:8, :] * keep_ref[(turn + 1) * batch]
        )

    def spot(item):
        return slice(item * GROUP, (item + 1) * GROUP)

    def act_of(item, column):
        conv = conv_ref[spot(item), head_lanes(column)]
        return conv * sigmoid(conv)

    def slope_of(item, column):
        conv = conv_ref[spot(item), head_lanes(column)]
        gate = sigmoid(conv)
        return gate * (1.0 + conv * (1.0 - gate))

    def d_unit(unit, inverse_norm, grad):
        return inverse_norm * (grad - unit * jnp.sum(unit * grad, axis=-1, keepdims=True))

    d_mixed = [d_mixed_ref[spot(item), head_lanes(head)] for item, head in pairs]
    pulled = [
        mul(reach_ref[spot(item), head_lanes(head)].T, d_mixed[index])
        for index, (item, head) in enumerate(pairs)
    ]
    d_states = [None] * len(pairs)
    now = [running[head] for head in range(heads)]
    for item in reversed(range(batch)):
        first = item * heads
        d_states[first : first + heads] = now
        now = [
            keeps[item] * (mul(step_ref[item, head].T, now[head]) + pulled[first + head])
            for head in range(heads)
        ]
    for head in range(heads):
        running[head] = now[head]

    d_out = [scale * grad for grad in d_mixed]
    states = [state_ref[item, head] for item, head in pairs]
    solved = [solved_ref[item, head] for item, head in pairs]
    scores = [square_ref[item, head, :, GROUP : 2 * GROUP] for item, head in pairs]
    acts = [act_of(item, heads + head) for item, head in pairs]
    key_scales = [unit_scale(act) for act in acts]
    keys = [act * size for act, size in zip(acts, key_scales)]
    fresh = [
        solved[index][:, HEAD:] - quick(solved[index][:, 0:HEAD], states[index])
        for index in indices
    ]
    d_fresh = [
        quick(scores[index].T, d_out[index]) + quick(keys[index], d_states[index])
        for index in indices
    ]
    d_scores = [
        jnp.where(rows >= cols, quick_nt(d_out[index], fresh[index]), 0.0) for index in indices
    ]
    d_solved = [
        jnp.concatenate([-quick_nt(d_fresh[index], states[index]), d_fresh[index]], axis=1)
        for index in indices
    ]
    d_right = [
        quick(square_ref[item, head, :, 0:GROUP].T, d_solved[index])
        for index, (item, head) in enumerate(pairs)
    ]
    d_queries = [
        quick_nt(d_out[index], states[index]) + quick(d_scores[index], keys[index])
        for index in indices
    ]
    acts = [act_of(item, head) for item, head in pairs]
    query_scales = [unit_scale(act) for act in acts]
    queries = [act * size for act, size in zip(acts, query_scales)]
    d_keys = [
        quick(d_scores[index].T, queries[index]) + quick_nt(fresh[index], d_states[index])
        for index in indices
    ]
    d_strict = [
        jnp.where(rows > cols, -quick_nt(d_right[index], solved[index]), 0.0) for index in indices
    ]
    strengths = [
        sigmoid(logit_ref[spot(item), head : head + 1]) for item, head in pairs
    ]
    overlaps = [quick_nt(key, key) for key in keys]
    both = [
        strengths[index] * d_strict[index] + (strengths[index] * d_strict[index]).T
        for index in indices
    ]
    d_keys = [
        d_keys[index]
        + strengths[index] * d_right[index][:, 0:HEAD]
        + quick(both[index], keys[index])
        for index in indices
    ]
    d_logits = []
    for index, (item, head) in enumerate(pairs):
        strength = strengths[index]
        value = act_of(item, 2 * heads + head)
        d_strength = (
            jnp.sum(d_right[index][:, 0:HEAD] * keys[index], axis=-1, keepdims=True)
            + jnp.sum(d_right[index][:, HEAD:] * value, axis=-1, keepdims=True)
            + jnp.sum(d_strict[index] * overlaps[index], axis=-1, keepdims=True)
        )
        d_logits.append(d_strength * strength * (1.0 - strength))
        for column, grad in (
            (head, d_unit(queries[index], query_scales[index], d_queries[index])),
            (heads + head, d_unit(keys[index], key_scales[index], d_keys[index])),
            (2 * heads + head, strength * d_right[index][:, HEAD:]),
        ):
            d_history[item, 0:GROUP, head_lanes(column)] = grad * slope_of(item, column)

    spread = lax.broadcasted_iota(jnp.int32, (GROUP, HEAD), 1)
    for item in range(batch):
        placed = jnp.zeros((GROUP, HEAD), jnp.float32)
        for head in range(heads):
            placed = jnp.where(spread == head, d_logits[item * heads + head], placed)
        d_pre_ref[spot(item), 3 * heads * HEAD :] = placed.astype(jnp.bfloat16)

    for item in reversed(range(batch - 1)):
        d_history[item, GROUP : GROUP + 8, :] = d_history[item + 1, 0:8, :] * keeps[item + 1]
    for column in range(3 * heads):
        lanes = head_lanes(column)
        for item in range(batch):
            pre = pre_ref[spot(item), lanes].astype(jnp.float32)
            total = jnp.zeros((GROUP, HEAD), jnp.float32)
            for tap in range(TAPS):
                part = d_history[item, TAPS - 1 - tap : TAPS - 1 - tap + GROUP, lanes]
                total = total + taps_ref[tap : tap + 1, lanes] * part
                d_taps_ref[tap : tap + 1, lanes] += jnp.sum(pre * part, axis=0, keepdims=True)
            d_pre_ref[spot(item), lanes] = total.astype(jnp.bfloat16)
        d_tail_ref[:, lanes] = jnp.where(
            turn == count - 1, total[GROUP - 8 :, :], d_tail_ref[:, lanes]
        )

    @pl.when(turn == 0)
    def _():
        edge_history[0:8, :] = jnp.zeros((8, edge_history.shape[1]), jnp.float32)
        edge_history[8:16, :] = d_history[0, 0:8, :] * keeps[0]
        total = jnp.zeros(d_edge_ref.shape, jnp.float32)
        for tap in range(TAPS):
            part = edge_history[TAPS - 1 - tap : TAPS - 1 - tap + 8, :]
            total = total + taps_ref[tap : tap + 1, :] * part
            d_taps_ref[tap : tap + 1, :] += jnp.sum(edge_ref[...] * part, axis=0, keepdims=True)
        d_edge_ref[...] = total


def passed_along(value, axis, by):
    count = lax.axis_size(axis)
    pairs = [(i, i + by) for i in range(count) if 0 <= i + by < count]
    return lax.ppermute(value, axis, pairs)


def adamw(weight, first, second, grad, rate, decay):
    first = FIRST_DECAY * first + (1.0 - FIRST_DECAY) * grad
    second = SECOND_DECAY * second + (1.0 - SECOND_DECAY) * grad * grad
    stepped = (
        first
        / (1.0 - FIRST_DECAY**STEP)
        / (jnp.sqrt(second / (1.0 - SECOND_DECAY**STEP)) + ADAM_EPSILON)
    )
    return (weight - rate * (stepped + decay * weight), first, second)


def f32(*shape):
    return jax.ShapeDtypeStruct(shape, jnp.float32)


def bf16(*shape):
    return jax.ShapeDtypeStruct(shape, jnp.bfloat16)


class Rule:
    def __init__(self, keep, heads, row_count):
        self.keep, self.heads, self.rows = keep, heads, row_count
        self.count = row_count // GROUP
        self.params = pltpu.CompilerParams(
            dimension_semantics=("arbitrary",), vmem_limit_bytes=48 * 1024 * 1024
        )

    def rows_spec(self, width, batch, back=False):
        last = self.count // batch - 1
        if back:
            return pl.BlockSpec((batch * GROUP, width), lambda n: (last - n, 0))
        return pl.BlockSpec((batch * GROUP, width), lambda n: (n, 0))

    def block_spec(self, shape, batch, back=False):
        last = self.count // batch - 1
        if back:
            return pl.BlockSpec((batch,) + shape, lambda n: (last - n, 0, 0, 0))
        return pl.BlockSpec((batch,) + shape, lambda n: (n, 0, 0, 0))

    def whole(self, *shape):
        return pl.BlockSpec(shape, lambda n: (0,) * len(shape))

    def smem(self):
        return pl.BlockSpec(memory_space=pltpu.SMEM)

    def maps(self, pre, edge, logits, taps):
        heads, rows, count, inner = self.heads, self.rows, self.count, self.heads * HEAD
        return pl.pallas_call(
            functools.partial(maps_kernel, heads, MAPS_BATCH),
            grid=(count // MAPS_BATCH,),
            in_specs=[
                self.smem(),
                self.rows_spec(3 * inner, MAPS_BATCH),
                self.whole(8, 3 * inner),
                self.rows_spec(heads, MAPS_BATCH),
                self.whole(TAPS, 3 * inner),
            ],
            out_specs=[
                self.rows_spec(3 * inner, MAPS_BATCH),
                self.block_spec((heads, GROUP, 2 * HEAD), MAPS_BATCH),
                self.block_spec((heads, GROUP, 2 * GROUP), MAPS_BATCH),
                self.block_spec((heads, HEAD, HEAD), MAPS_BATCH),
                self.block_spec((heads, HEAD, HEAD), MAPS_BATCH),
                self.rows_spec(inner, MAPS_BATCH),
                self.rows_spec(inner, MAPS_BATCH),
                self.whole(heads, HEAD, 2 * HEAD),
            ],
            out_shape=[
                f32(rows, 3 * inner),
                f32(count, heads, GROUP, 2 * HEAD),
                f32(count, heads, GROUP, 2 * GROUP),
                f32(count, heads, HEAD, HEAD),
                f32(count, heads, HEAD, HEAD),
                f32(rows, inner),
                f32(rows, inner),
                f32(heads, HEAD, 2 * HEAD),
            ],
            scratch_shapes=[
                pltpu.VMEM((MAPS_BATCH, GROUP + 8, 3 * inner), jnp.float32),
                pltpu.VMEM((heads, HEAD, 2 * HEAD), jnp.float32),
            ],
            compiler_params=self.params,
            cost_estimate=busy(35),
            name="delta_maps",
        )(self.keep, pre, edge, logits, taps)

    def outputs(self, incoming, step, fresh, reach, zero_out, gain):
        heads, rows, count, inner = self.heads, self.rows, self.count, self.heads * HEAD
        return pl.pallas_call(
            functools.partial(outputs_kernel, heads, CHAIN_BATCH),
            grid=(count // CHAIN_BATCH,),
            in_specs=[
                self.smem(),
                self.whole(heads, HEAD, HEAD),
                self.block_spec((heads, HEAD, HEAD), CHAIN_BATCH),
                self.block_spec((heads, HEAD, HEAD), CHAIN_BATCH),
                self.rows_spec(inner, CHAIN_BATCH),
                self.rows_spec(inner, CHAIN_BATCH),
                self.whole(1, HEAD),
            ],
            out_specs=[
                self.block_spec((heads, HEAD, HEAD), CHAIN_BATCH),
                self.rows_spec(inner, CHAIN_BATCH),
                self.rows_spec(inner, CHAIN_BATCH),
            ],
            out_shape=[f32(count, heads, HEAD, HEAD), f32(rows, inner), bf16(rows, inner)],
            scratch_shapes=[pltpu.VMEM((heads, HEAD, HEAD), jnp.float32)],
            compiler_params=self.params,
            cost_estimate=busy(9),
            name="delta_outputs",
        )(self.keep, incoming, step, fresh, reach, zero_out, gain)

    def tail(self, d_normed, mixed, gain, step, reach):
        heads, rows, count, inner = self.heads, self.rows, self.count, self.heads * HEAD
        return pl.pallas_call(
            functools.partial(tail_kernel, heads, CHAIN_BATCH),
            grid=(count // CHAIN_BATCH,),
            in_specs=[
                self.smem(),
                self.rows_spec(inner, CHAIN_BATCH, True),
                self.rows_spec(inner, CHAIN_BATCH, True),
                self.whole(1, HEAD),
                self.block_spec((heads, HEAD, HEAD), CHAIN_BATCH, True),
                self.rows_spec(inner, CHAIN_BATCH, True),
            ],
            out_specs=[
                self.rows_spec(inner, CHAIN_BATCH, True),
                self.whole(heads, HEAD, HEAD),
                self.whole(1, HEAD),
            ],
            out_shape=[f32(rows, inner), f32(heads, HEAD, HEAD), f32(1, HEAD)],
            scratch_shapes=[pltpu.VMEM((heads, HEAD, HEAD), jnp.float32)],
            compiler_params=self.params,
            cost_estimate=busy(11),
            name="delta_tail",
        )(self.keep, d_normed, mixed, gain, step, reach)

    def back(self, outgoing, pre, edge, logits, taps, conv, solved, square, step, reach, state, d_mixed):
        heads, rows, count, inner = self.heads, self.rows, self.count, self.heads * HEAD
        return pl.pallas_call(
            functools.partial(back_kernel, heads, BACK_BATCH),
            grid=(count // BACK_BATCH,),
            in_specs=[
                self.smem(),
                self.whole(heads, HEAD, HEAD),
                self.rows_spec(3 * inner, BACK_BATCH, True),
                self.whole(8, 3 * inner),
                self.rows_spec(heads, BACK_BATCH, True),
                self.whole(TAPS, 3 * inner),
                self.rows_spec(3 * inner, BACK_BATCH, True),
                self.block_spec((heads, GROUP, 2 * HEAD), BACK_BATCH, True),
                self.block_spec((heads, GROUP, 2 * GROUP), BACK_BATCH, True),
                self.block_spec((heads, HEAD, HEAD), BACK_BATCH, True),
                self.rows_spec(inner, BACK_BATCH, True),
                self.block_spec((heads, HEAD, HEAD), BACK_BATCH, True),
                self.rows_spec(inner, BACK_BATCH, True),
            ],
            out_specs=[
                self.rows_spec(3 * inner + HEAD, BACK_BATCH, True),
                self.whole(8, 3 * inner),
                self.whole(8, 3 * inner),
                self.whole(TAPS, 3 * inner),
            ],
            out_shape=[
                bf16(rows, 3 * inner + HEAD),
                f32(8, 3 * inner),
                f32(8, 3 * inner),
                f32(TAPS, 3 * inner),
            ],
            scratch_shapes=[
                pltpu.VMEM((BACK_BATCH, GROUP + 8, 3 * inner), jnp.float32),
                pltpu.VMEM((16, 3 * inner), jnp.float32),
                pltpu.VMEM((heads, HEAD, HEAD), jnp.float32),
            ],
            compiler_params=self.params,
            cost_estimate=busy(45),
            name="delta_back",
        )(
            self.keep, outgoing, pre, edge, logits, taps, conv, solved, square, step, reach, state,
            d_mixed,
        )


def rms_unit(values):
    return values * lax.rsqrt(jnp.mean(values * values, axis=-1, keepdims=True) + EPSILON)


def rms_back(values, gain_vec, grad):
    inverse_rms = lax.rsqrt(jnp.mean(values * values, axis=-1, keepdims=True) + EPSILON)
    unit = values * inverse_rms
    d_unit = grad * gain_vec
    d_values = inverse_rms * (d_unit - unit * jnp.mean(d_unit * unit, axis=-1, keepdims=True))
    return d_values, jnp.sum(grad * unit, axis=0)


def low(values):
    return values.astype(jnp.bfloat16)


def product(left, right, dims=((1,), (0,))):
    return lax.dot_general(left, right, (dims, ((), ())), preferred_element_type=jnp.float32)


def rows_summed(partial):
    return lax.psum_scatter(low(partial), "shard", scatter_dimension=0, tiled=True)


def rows_joined(rows):
    return lax.all_gather(rows, "shard", axis=0, tiled=True)


def seq_summed(grad, dim):
    return lax.psum_scatter(grad, "seq", scatter_dimension=dim, tiled=True)


def one_hot(indices, size):
    return (jnp.arange(size, dtype=jnp.int32)[:, None] == indices[None, :]).astype(jnp.bfloat16)


def moved(matrix, values):
    return low(product(matrix, values))


def moved_back(matrix, values):
    return low(product(matrix, values, ((0,), (0,))))


def busy(micros):
    return pl.CostEstimate(flops=micros * BUSY_FLOPS, bytes_accessed=0, transcendentals=0)


def ends(count):
    me = lax.axis_index("shard")
    return me, me > 0, me < count - 1


def meet_neighbours(count):
    me, has_left, has_right = ends(count)
    barrier = pltpu.get_barrier_semaphore()

    @pl.when(has_left)
    def _():
        pl.semaphore_signal(barrier, inc=1, device_id={"shard": me - 1}, device_id_type=MESH)

    @pl.when(has_right)
    def _():
        pl.semaphore_signal(barrier, inc=1, device_id={"shard": me + 1}, device_id_type=MESH)

    pl.semaphore_wait(barrier, has_left.astype(jnp.int32) + has_right.astype(jnp.int32))


def join_kernel(count, parts, own_ref, out_ref, own_sem, send_sem, recv_sem):
    me, has_left, has_right = ends(count)
    size = own_ref.shape[0] // parts
    meet_neighbours(count)
    own_copy = pltpu.make_async_copy(own_ref, out_ref.at[me], own_sem)
    own_copy.start()

    def piece_copy(way, block, part, source, target):
        rows = pl.ds(part * size, size)
        return pltpu.make_async_remote_copy(
            src_ref=source.at[rows] if source is own_ref else source.at[block, rows],
            dst_ref=out_ref.at[block, rows],
            send_sem=send_sem.at[way, block, part],
            recv_sem=recv_sem.at[block, part],
            device_id={"shard": target},
            device_id_type=MESH,
        )

    def each(action):
        for far in range(count):
            for part in range(parts):
                for way, present, onward, block, target in (
                    (0, me >= far, has_right, me - far, me + 1),
                    (1, me + far < count, has_left, me + far, me - 1),
                ):
                    action(far, part, way, present, onward, block, target)

    def start(far, part, way, present, onward, block, target):
        source = own_ref if far == 0 else out_ref

        if far:

            @pl.when(present)
            def _():
                piece_copy(way, block, part, out_ref, target).wait_recv()

        @pl.when(present & onward)
        def _():
            piece_copy(way, block, part, source, target).start()

    def finish(far, part, way, present, onward, block, target):
        source = own_ref if far == 0 else out_ref

        @pl.when(present & onward)
        def _():
            piece_copy(way, block, part, source, target).wait_send()

    each(start)
    each(finish)
    own_copy.wait()


def join_rows(rows, count, ident, parts=4):
    size, width = rows.shape
    return pl.pallas_call(
        functools.partial(join_kernel, count, parts),
        out_shape=jax.ShapeDtypeStruct((count, size, width), rows.dtype),
        in_specs=[pl.BlockSpec(memory_space=pl.ANY)],
        out_specs=pl.BlockSpec(memory_space=pl.ANY),
        scratch_shapes=[
            pltpu.SemaphoreType.DMA(()),
            pltpu.SemaphoreType.DMA((2, count, parts)),
            pltpu.SemaphoreType.DMA((count, parts)),
        ],
        compiler_params=pltpu.CompilerParams(collective_id=ident, has_side_effects=True),
        cost_estimate=busy(70),
        name="join_rows",
    )(rows).reshape(count * size, width)


def swap_kernel(count, to_columns, in_ref, out_ref, own_sem, send_sem, recv_sem):
    me = lax.axis_index("shard")
    barrier = pltpu.get_barrier_semaphore()
    for hop in range(1, count):
        other = lax.rem(me + hop, count)
        pl.semaphore_signal(barrier, inc=1, device_id={"shard": other}, device_id_type=MESH)
    pl.semaphore_wait(barrier, count - 1)
    if to_columns:
        width = in_ref.shape[2]
    else:
        width = out_ref.shape[2]

    def columns(ref, index):
        return ref.at[:, pl.ds(pl.multiple_of(index * width, width), width)]

    def source(block):
        return in_ref.at[block] if to_columns else columns(in_ref, block)

    def landing(block):
        return columns(out_ref, block) if to_columns else out_ref.at[block]

    own_copy = pltpu.make_async_copy(source(me), landing(me), own_sem)
    own_copy.start()

    def block_copy(hop):
        other = lax.rem(me + hop, count)
        return pltpu.make_async_remote_copy(
            src_ref=source(other),
            dst_ref=landing(me),
            send_sem=send_sem.at[hop],
            recv_sem=recv_sem.at[hop],
            device_id={"shard": other},
            device_id_type=MESH,
        )

    for hop in range(1, count):
        block_copy(hop).start()
    for hop in range(1, count):
        block_copy(hop).wait()
    own_copy.wait()


def swap_blocks(value, count, ident, to_columns):
    if to_columns:
        _, size, width = value.shape
        shape = (size, count * width)
    else:
        size, width = value.shape[0], value.shape[1] // count
        shape = (count, size, width)
    return pl.pallas_call(
        functools.partial(swap_kernel, count, to_columns),
        out_shape=jax.ShapeDtypeStruct(shape, value.dtype),
        in_specs=[pl.BlockSpec(memory_space=pl.ANY)],
        out_specs=pl.BlockSpec(memory_space=pl.ANY),
        scratch_shapes=[
            pltpu.SemaphoreType.DMA(()),
            pltpu.SemaphoreType.DMA((count,)),
            pltpu.SemaphoreType.DMA((count,)),
        ],
        compiler_params=pltpu.CompilerParams(collective_id=ident, has_side_effects=True),
        cost_estimate=busy(23),
        name="swap_blocks",
    )(value)


def relay_kernel(heads, hops, back, total_ref, fresh_ref, out_ref, sending, landing, send_sem, recv_sem):
    count = lax.axis_size("seq")
    me = lax.axis_index("seq")
    if back:
        follows, precedes, target, origin = me < count - 1, me > 0, me - 1, me + 1
    else:
        follows, precedes, target, origin = me > 0, me < count - 1, me + 1, me - 1
    barrier = pltpu.get_barrier_semaphore()

    @pl.when(follows)
    def _():
        pl.semaphore_signal(barrier, inc=1, device_id={"seq": origin}, device_id_type=MESH)

    @pl.when(precedes)
    def _():
        pl.semaphore_signal(barrier, inc=1, device_id={"seq": target}, device_id_type=MESH)

    pl.semaphore_wait(barrier, follows.astype(jnp.int32) + precedes.astype(jnp.int32))

    def state_copy(hop, head):
        return pltpu.make_async_remote_copy(
            src_ref=sending.at[hop, head],
            dst_ref=landing.at[hop, head],
            send_sem=send_sem.at[hop, head],
            recv_sem=recv_sem.at[hop, head],
            device_id={"seq": target},
            device_id_type=MESH,
        )

    for hop in range(hops):
        for head in range(heads):
            fresh = fresh_ref[head]
            if hop == 0:
                sending[hop, head] = low(fresh)
            else:

                @pl.when(follows)
                def _():
                    state_copy(hop - 1, head).wait_recv()
                    step = total_ref[head, :, 0:HEAD]
                    step = step.T if back else step
                    sending[hop, head] = low(
                        fresh + mul(step, landing[hop - 1, head].astype(jnp.float32))
                    )

                @pl.when(jnp.logical_not(follows))
                def _():
                    sending[hop, head] = low(fresh)

            @pl.when(precedes)
            def _():
                state_copy(hop, head).start()

    for head in range(heads):

        @pl.when(follows)
        def _():
            state_copy(hops - 1, head).wait_recv()
            out_ref[head] = landing[hops - 1, head].astype(jnp.float32)

        @pl.when(jnp.logical_not(follows))
        def _():
            out_ref[head] = jnp.zeros((HEAD, HEAD), jnp.float32)

    @pl.when(precedes)
    def _():
        for hop in range(hops):
            for head in range(heads):
                state_copy(hop, head).wait_send()


def relayed(total, fresh, hops, back, ident):
    heads = fresh.shape[0]
    return pl.pallas_call(
        functools.partial(relay_kernel, heads, hops, back),
        out_shape=jax.ShapeDtypeStruct((heads, HEAD, HEAD), jnp.float32),
        in_specs=[pl.BlockSpec(memory_space=pltpu.VMEM)] * 2,
        out_specs=pl.BlockSpec(memory_space=pltpu.VMEM),
        scratch_shapes=[
            pltpu.VMEM((hops, heads, HEAD, HEAD), jnp.bfloat16),
            pltpu.VMEM((hops, heads, HEAD, HEAD), jnp.bfloat16),
            pltpu.SemaphoreType.DMA((hops, heads)),
            pltpu.SemaphoreType.DMA((hops, heads)),
        ],
        compiler_params=pltpu.CompilerParams(collective_id=ident, has_side_effects=True),
        cost_estimate=busy(15),
        name="relay_back" if back else "relay",
    )(total, fresh)


def last_join_kernel(
    count,
    parts,
    shared,
    own_ref,
    small_ref,
    out_ref,
    small_out,
    seq_slots,
    layer_slots,
    own_sem,
    send_sem,
    recv_sem,
    seq_send,
    seq_recv,
    layer_send,
    layer_recv,
):
    me, has_left, has_right = ends(count)
    size = own_ref.shape[0] // parts
    devices = lax.axis_size("seq")
    here = lax.axis_index("seq")
    barrier = pltpu.get_barrier_semaphore()
    for hop in range(1, devices):
        other = lax.rem(here + hop, devices)
        pl.semaphore_signal(barrier, inc=1, device_id={"seq": other}, device_id_type=MESH)
    for hop in range(1, count):
        other = lax.rem(me + hop, count)
        pl.semaphore_signal(barrier, inc=1, device_id={"shard": other}, device_id_type=MESH)
    pl.semaphore_wait(barrier, devices + count - 2)
    own_copy = pltpu.make_async_copy(own_ref, out_ref.at[me], own_sem)
    own_copy.start()

    def seq_copy(hop):
        return pltpu.make_async_remote_copy(
            src_ref=small_ref,
            dst_ref=seq_slots.at[here],
            send_sem=seq_send.at[hop],
            recv_sem=seq_recv.at[hop],
            device_id={"seq": lax.rem(here + hop, devices)},
            device_id_type=MESH,
        )

    def layer_copy(hop):
        return pltpu.make_async_remote_copy(
            src_ref=small_out.at[pl.ds(0, shared)],
            dst_ref=layer_slots.at[me],
            send_sem=layer_send.at[hop],
            recv_sem=layer_recv.at[hop],
            device_id={"shard": lax.rem(me + hop, count)},
            device_id_type=MESH,
        )

    def piece_copy(way, block, part, source, target):
        rows = pl.ds(part * size, size)
        return pltpu.make_async_remote_copy(
            src_ref=source.at[rows] if source is own_ref else source.at[block, rows],
            dst_ref=out_ref.at[block, rows],
            send_sem=send_sem.at[way, block, part],
            recv_sem=recv_sem.at[block, part],
            device_id={"shard": target},
            device_id_type=MESH,
        )

    def each(far, action):
        for part in range(parts):
            for way, present, onward, block, target in (
                (0, me >= far, has_right, me - far, me + 1),
                (1, me + far < count, has_left, me + far, me - 1),
            ):
                action(far, part, way, present, onward, block, target)

    def start(far, part, way, present, onward, block, target):
        if far:

            @pl.when(present)
            def _():
                piece_copy(way, block, part, out_ref, target).wait_recv()

        @pl.when(present & onward)
        def _():
            piece_copy(way, block, part, out_ref if far else own_ref, target).start()

    def finish(far, part, way, present, onward, block, target):
        @pl.when(present & onward)
        def _():
            piece_copy(way, block, part, out_ref if far else own_ref, target).wait_send()

    def seq_start(hop, carry):
        seq_copy(hop).start()
        return carry

    def seq_finish(hop, carry):
        seq_copy(hop).wait()
        return carry

    lax.fori_loop(1, devices, seq_start, 0)
    seq_slots[here] = small_ref[...]
    each(0, start)
    lax.fori_loop(1, devices, seq_finish, 0)
    total = seq_slots[0]
    for index in range(1, devices):
        total = total + seq_slots[index]
    small_out[...] = total
    for hop in range(1, count):
        layer_copy(hop).start()
    layer_slots[me] = total[0:shared]
    for far in range(1, count):
        each(far, start)
    for hop in range(1, count):
        layer_copy(hop).wait()
    total = layer_slots[0]
    for index in range(1, count):
        total = total + layer_slots[index]
    small_out[0:shared, :] = total
    for far in range(count):
        each(far, finish)
    own_copy.wait()


def join_rows_and_sum(rows, small, shared, count, ident, parts=4):
    size, width = rows.shape
    devices = lax.axis_size("seq")
    joined, summed = pl.pallas_call(
        functools.partial(last_join_kernel, count, parts, shared),
        out_shape=[jax.ShapeDtypeStruct((count, size, width), rows.dtype), f32(*small.shape)],
        in_specs=[pl.BlockSpec(memory_space=pl.ANY), pl.BlockSpec(memory_space=pltpu.VMEM)],
        out_specs=[pl.BlockSpec(memory_space=pl.ANY), pl.BlockSpec(memory_space=pltpu.VMEM)],
        scratch_shapes=[
            pltpu.VMEM((devices,) + small.shape, jnp.float32),
            pltpu.VMEM((count, shared, small.shape[1]), jnp.float32),
            pltpu.SemaphoreType.DMA(()),
            pltpu.SemaphoreType.DMA((2, count, parts)),
            pltpu.SemaphoreType.DMA((count, parts)),
            pltpu.SemaphoreType.DMA((devices,)),
            pltpu.SemaphoreType.DMA((devices,)),
            pltpu.SemaphoreType.DMA((count,)),
            pltpu.SemaphoreType.DMA((count,)),
        ],
        compiler_params=pltpu.CompilerParams(collective_id=ident, has_side_effects=True),
        cost_estimate=busy(70),
        name="join_rows_and_sum",
    )(rows, small)
    return joined.reshape(count * size, width), summed


def start_kernel(
    x_ref,
    place_ref,
    out_ref,
    x_got,
    place_got,
    out_got,
    own_sem,
    x_send,
    x_recv,
    place_send,
    place_recv,
    out_send,
    out_recv,
):
    count, me = lax.axis_size("shard"), lax.axis_index("shard")
    devices, here = lax.axis_size("seq"), lax.axis_index("seq")
    barrier = pltpu.get_barrier_semaphore()

    def greet(hop, carry):
        other = lax.rem(here + hop, devices)
        pl.semaphore_signal(barrier, inc=1, device_id={"seq": other}, device_id_type=MESH)
        return carry

    lax.fori_loop(1, devices, greet, 0)
    for hop in range(1, count):
        other = lax.rem(me + hop, count)
        pl.semaphore_signal(barrier, inc=1, device_id={"shard": other}, device_id_type=MESH)
    own_copies = [
        pltpu.make_async_copy(x_ref.at[here], x_got.at[here], own_sem.at[0]),
        pltpu.make_async_copy(place_ref.at[here], place_got.at[here], own_sem.at[1]),
        pltpu.make_async_copy(out_ref, out_got.at[me], own_sem.at[2]),
    ]
    for copy in own_copies:
        copy.start()
    pl.semaphore_wait(barrier, devices + count - 2)

    def seq_copies(hop):
        other = lax.rem(here + hop, devices)
        return [
            pltpu.make_async_remote_copy(
                src_ref=source.at[other],
                dst_ref=target.at[here],
                send_sem=send.at[hop],
                recv_sem=recv.at[hop],
                device_id={"seq": other},
                device_id_type=MESH,
            )
            for source, target, send, recv in (
                (x_ref, x_got, x_send, x_recv),
                (place_ref, place_got, place_send, place_recv),
            )
        ]

    def out_copy(hop):
        return pltpu.make_async_remote_copy(
            src_ref=out_ref,
            dst_ref=out_got.at[me],
            send_sem=out_send.at[hop],
            recv_sem=out_recv.at[hop],
            device_id={"shard": lax.rem(me + hop, count)},
            device_id_type=MESH,
        )

    def start(hop, carry):
        for copy in seq_copies(hop):
            copy.start()
        return carry

    def finish(hop, carry):
        for copy in seq_copies(hop):
            copy.wait()
        return carry

    lax.fori_loop(1, devices, start, 0)
    for hop in range(1, count):
        out_copy(hop).start()
    lax.fori_loop(1, devices, finish, 0)
    for hop in range(1, count):
        out_copy(hop).wait()
    for copy in own_copies:
        copy.wait()


def start_exchange(rows, places, out_low, layers, ident):
    devices = rows.shape[0]
    dma = pltpu.SemaphoreType.DMA
    return pl.pallas_call(
        start_kernel,
        out_shape=[
            jax.ShapeDtypeStruct(rows.shape, rows.dtype),
            jax.ShapeDtypeStruct(places.shape, places.dtype),
            jax.ShapeDtypeStruct((layers,) + out_low.shape, out_low.dtype),
        ],
        in_specs=[pl.BlockSpec(memory_space=pl.ANY)] * 3,
        out_specs=[pl.BlockSpec(memory_space=pl.ANY)] * 3,
        scratch_shapes=[
            dma((3,)),
            dma((devices,)),
            dma((devices,)),
            dma((devices,)),
            dma((devices,)),
            dma((layers,)),
            dma((layers,)),
        ],
        compiler_params=pltpu.CompilerParams(collective_id=ident, has_side_effects=True),
        cost_estimate=busy(20),
        name="start_exchange",
    )(rows, places, out_low)


def total_join_kernel(
    count,
    parts,
    grads_ref,
    weights_ref,
    rows_ref,
    own_ref,
    out_ref,
    joined_ref,
    weigh_ref,
    grads,
    weights,
    rows_in,
    part_ref,
    weighed,
    from_left,
    from_right,
    load_sem,
    weigh_sem,
    own_sem,
    send_sem,
    recv_sem,
    join_send,
    join_recv,
):
    me, has_left, has_right = ends(count)
    size = out_ref.shape[0] // parts
    tile = 2 * HEAD
    width = out_ref.shape[1]
    loads = [
        pltpu.make_async_copy(source, target, load_sem.at[index])
        for index, (source, target) in enumerate(
            ((grads_ref, grads), (weights_ref, weights), (rows_ref, rows_in))
        )
    ]
    for load in loads:
        load.start()
    meet_neighbours(count)
    own_copy = pltpu.make_async_copy(own_ref, joined_ref.at[me], own_sem)
    own_copy.start()

    def sum_copy(way, block, part, source, target):
        rows = pl.ds(part * size, size)
        landing = (from_left, from_right)[way]
        return pltpu.make_async_remote_copy(
            src_ref=source.at[block, rows],
            dst_ref=landing.at[block, rows],
            send_sem=send_sem.at[way, block, part],
            recv_sem=recv_sem.at[way, block, part],
            device_id={"shard": target},
            device_id_type=MESH,
        )

    def join_copy(way, block, part, source, target):
        rows = pl.ds(part * size, size)
        return pltpu.make_async_remote_copy(
            src_ref=source.at[rows] if source is own_ref else source.at[block, rows],
            dst_ref=joined_ref.at[block, rows],
            send_sem=join_send.at[way, block, part],
            recv_sem=join_recv.at[block, part],
            device_id={"shard": target},
            device_id_type=MESH,
        )

    def sum_way(way, block):
        if way == 0:
            return me < block, has_left, me + 1
        return me > block, has_right, me - 1

    def join_way(far, way):
        if way == 0:
            return me >= far, has_right, me - far, me + 1
        return me + far < count, has_left, me + far, me - 1

    def join_start(far, way, part):
        present, onward, block, target = join_way(far, way)
        if far:

            @pl.when(present)
            def _():
                join_copy(way, block, part, joined_ref, target).wait_recv()

        @pl.when(present & onward)
        def _():
            join_copy(way, block, part, joined_ref if far else own_ref, target).start()

    def sum_start(way, block, part):
        sends, receives, target = sum_way(way, block)
        landing = (from_left, from_right)[way]
        rows = pl.ds(part * size, size)

        @pl.when(sends & receives)
        def _():
            sum_copy(way, block, part, landing, target).wait_recv()
            landing[block, rows, :] = (
                landing[block, rows, :].astype(jnp.float32)
                + part_ref[block, rows, :].astype(jnp.float32)
            ).astype(jnp.bfloat16)
            sum_copy(way, block, part, landing, target).start()

    for part in range(parts):
        for way in range(2):
            join_start(0, way, part)
    loads[0].wait()
    loads[1].wait()

    def block_turn(turn, carry):
        block = jnp.int32(0)
        for place in range(count):
            by_distance = sorted(range(count), key=lambda other: -abs(other - place))
            for index, other in enumerate(by_distance):
                block = jnp.where((me == place) & (turn == index), other, block)

        def tile_turn(index, inner_carry):
            across = pl.ds(pl.multiple_of(index * tile, tile), tile)
            part_ref[block, :, across] = low(
                product(grads[block], weights[across, :], ((1,), (1,)))
            )
            return inner_carry

        lax.fori_loop(0, width // tile, tile_turn, 0)

        @pl.when((block > me) & jnp.logical_not(has_left))
        def _():
            for part in range(parts):
                sum_copy(0, block, part, part_ref, me + 1).start()

        @pl.when((block < me) & jnp.logical_not(has_right))
        def _():
            for part in range(parts):
                sum_copy(1, block, part, part_ref, me - 1).start()

        return carry

    lax.fori_loop(0, count, block_turn, 0)
    loads[2].wait()
    wide = weights.shape[1]
    rows_total = count * out_ref.shape[0]

    def weigh_store(turn):
        rows = pl.ds(pl.multiple_of(turn * tile, tile), tile)
        return pltpu.make_async_copy(weighed.at[rows], weigh_ref.at[rows], weigh_sem.at[turn])

    def weigh_turn(turn, carry):
        rows = pl.ds(pl.multiple_of(turn * tile, tile), tile)
        turned = rows_in[:, rows].T

        def weigh_tile(first, span):
            against = grads[:, :, pl.ds(first, span)].reshape(rows_total, span)
            weighed[rows, pl.ds(first, span)] = low(product(turned, against))

        def tile_turn(index, inner_carry):
            weigh_tile(pl.multiple_of(index * tile, tile), tile)
            return inner_carry

        lax.fori_loop(0, wide // tile, tile_turn, 0)
        if wide % tile:
            weigh_tile(wide // tile * tile, wide % tile)
        weigh_store(turn).start()
        return carry

    for step in range(count):
        if step == min(2, count - 1):
            lax.fori_loop(0, width // tile, weigh_turn, 0)
        for part in range(parts):
            if step:
                for way in range(2):
                    join_start(step, way, part)
            if step < count - 1:
                sum_start(0, count - 1 - step, part)
                sum_start(1, step, part)

    for block in range(count):

        @pl.when(me == block)
        def _():
            for part in range(parts):
                rows = pl.ds(part * size, size)
                total = part_ref[block, rows, :].astype(jnp.float32)
                if block > 0:
                    sum_copy(0, block, part, from_left, me).wait_recv()
                    total = total + from_left[block, rows, :].astype(jnp.float32)
                if block < count - 1:
                    sum_copy(1, block, part, from_right, me).wait_recv()
                    total = total + from_right[block, rows, :].astype(jnp.float32)
                out_ref[rows, :] = total

    for step in range(count):
        for part in range(parts):
            for way in range(2):
                present, onward, block, target = join_way(step, way)

                @pl.when(present & onward)
                def _():
                    source = joined_ref if step else own_ref
                    join_copy(way, block, part, source, target).wait_send()

            if step < count - 1:
                for way, block in ((0, count - 1 - step), (1, step)):
                    sends, _, target = sum_way(way, block)

                    @pl.when(sends)
                    def _():
                        sum_copy(way, block, part, part_ref, target).wait_send()

    own_copy.wait()

    def weigh_finish(turn, carry):
        weigh_store(turn).wait()
        return carry

    lax.fori_loop(0, width // tile, weigh_finish, 0)


def total_and_join(grads, weights, rows, own, count, ident, parts=4):
    size, width = own.shape
    wide = grads.shape[1]
    total, joined, weighed = pl.pallas_call(
        functools.partial(total_join_kernel, count, parts),
        out_shape=[
            jax.ShapeDtypeStruct((size, width), jnp.float32),
            jax.ShapeDtypeStruct((count, size, width), own.dtype),
            bf16(width, wide),
        ],
        in_specs=[pl.BlockSpec(memory_space=pl.ANY)] * 4,
        out_specs=[pl.BlockSpec(memory_space=pltpu.VMEM)] + [pl.BlockSpec(memory_space=pl.ANY)] * 2,
        scratch_shapes=[
            pltpu.VMEM((count, size, wide), jnp.bfloat16),
            pltpu.VMEM((width, wide), jnp.bfloat16),
            pltpu.VMEM((count * size, width), jnp.bfloat16),
            pltpu.VMEM((count, size, width), jnp.bfloat16),
            pltpu.VMEM((width, wide), jnp.bfloat16),
            pltpu.VMEM((count, size, width), jnp.bfloat16),
            pltpu.VMEM((count, size, width), jnp.bfloat16),
            pltpu.SemaphoreType.DMA((3,)),
            pltpu.SemaphoreType.DMA((width // (2 * HEAD),)),
            pltpu.SemaphoreType.DMA(()),
            pltpu.SemaphoreType.DMA((2, count, parts)),
            pltpu.SemaphoreType.DMA((2, count, parts)),
            pltpu.SemaphoreType.DMA((2, count, parts)),
            pltpu.SemaphoreType.DMA((count, parts)),
        ],
        compiler_params=pltpu.CompilerParams(
            collective_id=ident, has_side_effects=True, vmem_limit_bytes=60 * 1024 * 1024
        ),
        cost_estimate=busy(95),
        name="total_and_join",
    )(grads.reshape(count, size, wide), weights, rows, own)
    return total, joined.reshape(count * size, width), weighed


def feed_kernel(
    count,
    parts,
    own_ref,
    dy_ref,
    gate_up_ref,
    down_ref,
    down_part_out,
    grad_open_out,
    grad_down_out,
    total_ref,
    gate_up,
    down,
    dy,
    rows_all,
    hidden,
    d_both,
    partial,
    landing,
    down_part,
    open_stage,
    down_stage,
    load_sem,
    part_sem,
    open_sem,
    down_sem,
    join_send,
    join_recv,
    sum_send,
    sum_recv,
):
    me, has_left, has_right = ends(count)
    units, width = down.shape
    piece = own_ref.shape[0] // parts
    tile = 2 * HEAD
    loads = [
        pltpu.make_async_copy(gate_up_ref, gate_up, load_sem.at[0]),
        pltpu.make_async_copy(dy_ref, dy, load_sem.at[1]),
        pltpu.make_async_copy(down_ref, down, load_sem.at[2]),
    ]
    for load in loads:
        load.start()
    rows_all[me] = own_ref[...]
    meet_neighbours(count)

    def part_store(block):
        return pltpu.make_async_copy(
            down_part.at[block], down_part_out.at[block], part_sem.at[block]
        )

    def open_store(turn):
        slot = lax.rem(turn, 2)
        rows = pl.ds(pl.multiple_of(turn * tile, tile), tile)
        return pltpu.make_async_copy(
            open_stage.at[slot], grad_open_out.at[rows], open_sem.at[slot]
        )

    def down_store(turn, size):
        slot = lax.rem(turn, 2)
        rows = pl.ds(pl.multiple_of(turn * tile, tile), size)
        return pltpu.make_async_copy(
            down_stage.at[slot, pl.ds(0, size)], grad_down_out.at[rows], down_sem.at[slot]
        )

    def join_copy(way, block, part):
        rows = pl.ds(part * piece, piece)
        return pltpu.make_async_remote_copy(
            src_ref=rows_all.at[block, rows],
            dst_ref=rows_all.at[block, rows],
            send_sem=join_send.at[way, block, part],
            recv_sem=join_recv.at[block, part],
            device_id={"shard": me - 1 if way else me + 1},
            device_id_type=MESH,
        )

    def sum_copy(way, block, part, source):
        rows = pl.ds(part * piece, piece)
        target = me - 1 if way else me + 1
        slot = jnp.where(block == target, count, block) if way else block
        return pltpu.make_async_remote_copy(
            src_ref=source.at[block, rows],
            dst_ref=landing.at[slot, rows],
            send_sem=sum_send.at[way, block, part],
            recv_sem=sum_recv.at[way, block, part],
            device_id={"shard": target},
            device_id_type=MESH,
        )

    def open_tile(block, first, size):
        across = pl.ds(first, size)
        beyond = pl.ds(pl.multiple_of(units + first, HEAD), size)
        rows = rows_all[block]
        gate = jnp.dot(rows, gate_up[:, across], preferred_element_type=jnp.float32)
        up = jnp.dot(rows, gate_up[:, beyond], preferred_element_type=jnp.float32)
        d_hidden = product(dy[block], down[across, :], ((1,), (1,)))
        opened = sigmoid(gate)
        wave = gate * opened
        hidden[block, :, across] = low(wave * up)
        d_both[block, :, across] = low(d_hidden * up * (opened * (1.0 + gate * (1.0 - opened))))
        d_both[block, :, beyond] = low(d_hidden * wave)

    def compute(block):
        def open_turn(turn, carry):
            open_tile(block, pl.multiple_of(turn * tile, tile), tile)
            return carry

        lax.fori_loop(0, units // tile, open_turn, 0)
        if units % tile:
            open_tile(block, units // tile * tile, units % tile)

        def close_turn(turn, carry):
            across = pl.ds(pl.multiple_of(turn * tile, tile), tile)
            partial[block, :, across] = low(
                product(d_both[block], gate_up[across, :], ((1,), (1,)))
            )
            return carry

        def down_turn(turn, carry):
            across = pl.ds(pl.multiple_of(turn * tile, tile), tile)
            down_part[block, :, across] = low(product(hidden[block], down[:, across]))
            return carry

        lax.fori_loop(0, width // tile, close_turn, 0)
        lax.fori_loop(0, width // tile, down_turn, 0)

    def slot_turn(slot, carry):
        far = (slot + 1) // 2
        rightward = lax.rem(slot, 2) == 1

        @pl.when(slot == 0)
        def _():
            for part in range(parts):

                @pl.when(has_right)
                def _():
                    join_copy(0, me, part).start()

                @pl.when(has_left)
                def _():
                    join_copy(1, me, part).start()

            for load in loads:
                load.wait()

        @pl.when(rightward)
        def _():
            for part in range(parts):
                for way, present, onward, block in (
                    (0, me >= far, has_right, me - far),
                    (1, me + far < count, has_left, me + far),
                ):

                    @pl.when(present)
                    def _():
                        join_copy(way, block, part).wait_recv()

                    @pl.when(present & onward)
                    def _():
                        join_copy(way, block, part).start()

        block = jnp.where(rightward, me - far, me + far)

        @pl.when((block >= 0) & (block < count))
        def _():
            compute(block)
            part_store(block).start()

            @pl.when((block > me) & jnp.logical_not(has_left))
            def _():
                for part in range(parts):
                    sum_copy(0, block, part, partial).start()

            @pl.when((block < me) & jnp.logical_not(has_right))
            def _():
                for part in range(parts):
                    sum_copy(1, block, part, partial).start()

        return carry

    lax.fori_loop(0, 2 * count - 1, slot_turn, 0)

    def add_on(way, block, part):
        rows = pl.ds(part * piece, piece)
        sum_copy(way, block, part, landing).wait_recv()
        landing[block, rows, :] = low(
            landing[block, rows, :].astype(jnp.float32)
            + partial[block, rows, :].astype(jnp.float32)
        )
        sum_copy(way, block, part, landing).start()

    rows_total = count * own_ref.shape[0]

    def weigh(left, right, stage, across_count):
        turned = left.reshape(rows_total, left.shape[2]).T

        span = across_count * tile // 2

        def turn_of(turn, carry):
            across = pl.ds(pl.multiple_of(turn * span, HEAD), span)
            against = right[:, :, across].reshape(rows_total, span)
            stage[:, across] = low(product(turned, against))
            return carry

        lax.fori_loop(0, 2, turn_of, 0)

    open_count = width // tile
    down_count, down_rest = units // tile, units % tile

    def late_turn(turn, carry):
        step, part = 2 + turn // parts, lax.rem(turn, parts)

        @pl.when((step < count) & (me < step) & has_left)
        def _():
            add_on(0, step, part)

        @pl.when((step < count) & (me > count - 1 - step) & has_right)
        def _():
            add_on(1, count - 1 - step, part)

        slot = lax.rem(turn, 2)
        cols = pl.ds(pl.multiple_of(turn * tile, tile), tile)

        @pl.when(turn < open_count)
        def _():
            @pl.when(turn >= 2)
            def _():
                open_store(turn - 2).wait()

            weigh(rows_all[:, :, cols], d_both, open_stage.at[slot], 2 * units // tile)
            open_store(turn).start()

        @pl.when(turn < down_count)
        def _():
            @pl.when(turn >= 2)
            def _():
                down_store(turn - 2, tile).wait()

            weigh(hidden[:, :, cols], dy, down_stage.at[slot], width // tile)
            down_store(turn, tile).start()

        return carry

    late_count = max((count - 2) * parts, open_count)
    lax.fori_loop(0, late_count, late_turn, 0)
    for turn in range(max(0, open_count - 2), open_count):
        open_store(turn).wait()
    for turn in range(max(0, down_count - 2), down_count):
        down_store(turn, tile).wait()
    if down_rest:
        weigh(
            hidden[:, :, down_count * tile :],
            dy,
            down_stage.at[down_count % 2, pl.ds(0, down_rest)],
            width // tile,
        )
        down_store(down_count, down_rest).start()

    for part in range(parts):
        rows = pl.ds(part * piece, piece)
        total_ref[rows, :] = partial[me, rows, :].astype(jnp.float32)

        @pl.when(has_left)
        def _():
            sum_copy(0, me, part, landing).wait_recv()
            total_ref[rows, :] += landing[me, rows, :].astype(jnp.float32)

        @pl.when(has_right)
        def _():
            sum_copy(1, me, part, landing).wait_recv()
            total_ref[rows, :] += landing[count, rows, :].astype(jnp.float32)

    for block in range(count):
        for part in range(parts):

            @pl.when((me >= block) & has_right)
            def _():
                join_copy(0, block, part).wait_send()

            @pl.when((me <= block) & has_left)
            def _():
                join_copy(1, block, part).wait_send()

            @pl.when(me < block)
            def _():
                sum_copy(0, block, part, partial).wait_send()

            @pl.when(me > block)
            def _():
                sum_copy(1, block, part, partial).wait_send()

        part_store(block).wait()

    if down_rest:
        down_store(down_count, down_rest).wait()


def feed_forward(own, dy, gate_up_mat, down_mat, count, ident, parts=4):
    size, width = own.shape
    units = down_mat.shape[0]
    dma = pltpu.SemaphoreType.DMA
    down_part, grad_open, grad_down, total = pl.pallas_call(
        functools.partial(feed_kernel, count, parts),
        out_shape=[
            bf16(count, size, width),
            bf16(width, 2 * units),
            bf16(units, width),
            f32(size, width),
        ],
        in_specs=[pl.BlockSpec(memory_space=pltpu.VMEM)] + [pl.BlockSpec(memory_space=pl.ANY)] * 3,
        out_specs=[pl.BlockSpec(memory_space=pl.ANY)] * 3 + [pl.BlockSpec(memory_space=pltpu.VMEM)],
        scratch_shapes=[
            pltpu.VMEM((width, 2 * units), jnp.bfloat16),
            pltpu.VMEM((units, width), jnp.bfloat16),
            pltpu.VMEM((count, size, width), jnp.bfloat16),
            pltpu.VMEM((count, size, width), jnp.bfloat16),
            pltpu.VMEM((count, size, units), jnp.bfloat16),
            pltpu.VMEM((count, size, 2 * units), jnp.bfloat16),
            pltpu.VMEM((count, size, width), jnp.bfloat16),
            pltpu.VMEM((count + 1, size, width), jnp.bfloat16),
            pltpu.VMEM((count, size, width), jnp.bfloat16),
            pltpu.VMEM((2, 2 * HEAD, 2 * units), jnp.bfloat16),
            pltpu.VMEM((2, 2 * HEAD, width), jnp.bfloat16),
            dma((3,)),
            dma((count,)),
            dma((2,)),
            dma((2,)),
            dma((2, count, parts)),
            dma((count, parts)),
            dma((2, count, parts)),
            dma((2, count, parts)),
        ],
        compiler_params=pltpu.CompilerParams(
            collective_id=ident, has_side_effects=True, vmem_limit_bytes=63 * 1024 * 1024
        ),
        cost_estimate=busy(120),
        name="feed_forward",
    )(own, dy.reshape(count, size, width), gate_up_mat, down_mat)
    return down_part.reshape(count * size, width), grad_open, grad_down, total


def per_device(
    hidden_in,
    out_grad,
    deal,
    lengths,
    qkv_weight,
    qkv_first,
    qkv_second,
    beta_weight,
    beta_first,
    beta_second,
    out_weight,
    out_first,
    out_second,
    gate_up_weight,
    gate_up_first,
    gate_up_second,
    down_weight,
    down_first,
    down_second,
    conv_weight,
    conv_first,
    conv_second,
    gains,
    gains_first,
    gains_second,
):
    row_count, model_width = hidden_in.shape
    heads = beta_weight.shape[1]
    inner = qkv_weight.shape[2]
    units = down_weight.shape[0]
    devices = lax.axis_size("seq")
    layers = lax.axis_size("shard")
    place = lax.axis_index("shard")
    longest = {4: 4096, 16: 8192}[lengths.shape[0]]
    hops = min(devices - 1, -(-longest // row_count))
    share = row_count // devices // layers
    quarter = devices * share
    _, order, sent_place = lax.sort(
        (deal // row_count, jnp.arange(row_count, dtype=jnp.int32), deal % row_count), num_keys=1
    )
    ordered = order.reshape(devices, layers, share)
    own_order = lax.dynamic_index_in_dim(ordered, place, 1, keepdims=False).reshape(quarter)
    by_layer = jnp.swapaxes(ordered, 0, 1).reshape(row_count)
    chosen = one_hot(own_order, row_count)
    sorting = one_hot(by_layer, row_count)

    def exchanged(rows):
        width = rows.shape[-1]
        return lax.all_to_all(
            rows.reshape(devices, share, width), "seq", split_axis=0, concat_axis=0, tiled=True
        ).reshape(quarter, width)

    plane = (share, model_width) if share % 16 == 0 else (share * model_width // HEAD, HEAD)
    chosen_x = moved_back(chosen, hidden_in).reshape((devices,) + plane)
    sent_place = sent_place.reshape(devices, 1, layers * share)
    sent_place = jnp.pad(sent_place, ((0, 0), (0, 0), (0, -(layers * share) % HEAD)))
    own_x, got_place, out_rows = start_exchange(
        chosen_x, sent_place, low(out_weight), layers, 9
    )
    own_x = own_x.reshape(quarter, model_width).astype(jnp.float32)
    out_rows = out_rows.reshape(layers * inner, out_weight.shape[1])
    got_place = got_place[:, 0, : layers * share]
    all_dy = lax.all_to_all(
        moved_back(one_hot(order, row_count), out_grad).reshape(
            devices, layers, share, model_width
        ),
        "seq",
        split_axis=0,
        concat_axis=0,
        tiled=True,
    )

    first_place = lax.axis_index("seq") * row_count
    places = first_place + jnp.arange(0, row_count, GROUP, dtype=jnp.int32)
    starts = jnp.cumsum(lengths) - lengths
    keep = jnp.all(starts[None, :] != places[:, None], axis=1).astype(jnp.float32)

    beta_pad = jnp.zeros((beta_weight.shape[0], HEAD - heads), jnp.bfloat16)
    mixer_mat = lax.all_gather(
        jnp.concatenate(
            [low(qkv_weight[:, item]) for item in range(3)] + [low(beta_weight), beta_pad], axis=1
        ),
        "seq",
        axis=0,
        tiled=True,
    )
    out_mat = lax.all_gather(out_rows, "seq", axis=1, tiled=True)
    gate_up_mat = lax.all_gather(
        low(gate_up_weight).reshape(-1, 2 * units), "seq", axis=0, tiled=True
    )
    down_mat = lax.all_gather(low(down_weight), "seq", axis=1, tiled=True)
    gain_in = gains[:model_width]
    gain_ff = gains[model_width : 2 * model_width]
    gain_out = gains[2 * model_width :].reshape(1, HEAD)
    conv_mat = conv_weight.reshape(TAPS, 3 * inner)

    normed_in = join_rows(low(rms_unit(own_x) * gain_in), layers, 0)
    normed_in, all_dy = lax.optimization_barrier((normed_in, all_dy))
    got_place = jnp.swapaxes(got_place.reshape(devices, layers, share), 0, 1).reshape(row_count)
    to_chain = one_hot(got_place, row_count)
    all_dy = jnp.swapaxes(all_dy, 0, 1).reshape(row_count, model_width)
    own_dy = lax.dynamic_slice_in_dim(all_dy, place * quarter, quarter, 0)
    mixed_in = product(normed_in, mixer_mat)
    logits = mixed_in[:, 3 * inner :]
    logits_high = low(logits)
    logits_low = low(logits - logits_high.astype(jnp.float32))
    chain_in = product(
        to_chain,
        jnp.concatenate([low(mixed_in[:, : 3 * inner]), logits_high, logits_low], axis=1),
    )
    projected = low(chain_in[:, : 3 * inner])
    logits = (
        chain_in[:, 3 * inner : 3 * inner + heads]
        + chain_in[:, 3 * inner + HEAD : 3 * inner + HEAD + heads]
    )
    edge_rows = passed_along(projected[row_count - 8 :], "seq", 1).astype(jnp.float32)
    edge_rows = edge_rows * (jnp.arange(8) >= 8 - (TAPS - 1)).astype(jnp.float32)[:, None]
    rule = Rule(keep, heads, row_count)
    conv, solved, square, step, fresh, reach, zero_out, total = rule.maps(
        projected, edge_rows, logits, conv_mat
    )
    incoming = relayed(total, total[:, :, HEAD:], hops, False, 7)
    state, mixed, normed = rule.outputs(incoming, step, fresh, reach, zero_out, gain_out)

    normed = moved_back(to_chain, normed)
    own_normed = swap_blocks(normed.reshape(layers, quarter, inner), layers, 1, True)
    residual = own_x + product(own_normed, out_mat)
    result, grad_gate_up, grad_down, d_normed_ff = feed_forward(
        low(rms_unit(residual) * gain_ff), all_dy, gate_up_mat, down_mat, layers, 2
    )
    red_down = seq_summed(grad_down, 1)
    d_residual, grad_gain_ff = rms_back(residual, gain_ff, d_normed_ff)
    d_residual = own_dy.astype(jnp.float32) + d_residual
    own_mix = low(d_residual)
    all_mix = join_rows(own_mix, layers, 4)
    all_mix, grad_gate_up, result = lax.optimization_barrier((all_mix, grad_gate_up, result))
    out_own = lax.dynamic_slice_in_dim(out_mat, place * inner, inner, 0)
    d_normed = low(product(all_mix, out_own, ((1,), (1,))))
    result = lax.psum_scatter(result, "shard", scatter_dimension=0, tiled=True)
    red_gate_up = seq_summed(grad_gate_up, 0)
    d_normed = product(to_chain, d_normed)
    d_mixed, d_first_state, grad_gain_out = rule.tail(d_normed, mixed, gain_out, step, reach)
    d_mixed, red_down = lax.optimization_barrier((d_mixed, red_down))
    outgoing = relayed(total, d_first_state, hops, True, 8)
    d_pre, d_tail, d_edge, grad_taps = rule.back(
        outgoing, projected, edge_rows, logits, conv_mat, conv, solved, square, step, reach, state,
        d_mixed,
    )
    d_tail = low(d_tail + passed_along(d_edge, "seq", -1))
    d_pre = lax.dynamic_update_slice(d_pre, d_tail, (row_count - 8, 0))
    d_pre, all_mix = lax.optimization_barrier((d_pre, all_mix))
    grad_out = low(product(normed, all_mix, ((0,), (0,))))
    red_out = seq_summed(grad_out, 1)
    d_pre, result = lax.optimization_barrier((d_pre, result))
    d_mixed_in = moved_back(to_chain, d_pre)
    result = exchanged(low(residual + result.astype(jnp.float32)))
    red_down = red_down.astype(jnp.float32)
    down_new = adamw(down_weight, down_first, down_second, red_down, RATE_DOWN, SHRINK)
    result, *down_new = lax.optimization_barrier((result, *down_new))
    d_normed_in, result, grad_mixer = total_and_join(
        d_mixed_in, mixer_mat, normed_in, result, layers, 5
    )
    d_normed_in, red_gate_up, red_out = lax.optimization_barrier(
        (d_normed_in, red_gate_up, red_out)
    )
    d_input, grad_gain_in = rms_back(own_x, gain_in, d_normed_in)
    d_input, red_gate_up = lax.optimization_barrier((low(d_residual + d_input), red_gate_up))
    d_input = exchanged(d_input)
    red_gate_up = red_gate_up.astype(jnp.float32).reshape(gate_up_weight.shape)
    gate_up_new = adamw(
        gate_up_weight, gate_up_first, gate_up_second, red_gate_up, RATE_WIDE, SHRINK
    )
    d_input, grad_mixer, *gate_up_new = lax.optimization_barrier(
        (d_input, grad_mixer, *gate_up_new)
    )
    red_mixer = seq_summed(grad_mixer, 0)
    shared = -(-gains.shape[0] // (8 * HEAD)) * 8
    small = jnp.concatenate(
        [
            grad_gain_in,
            grad_gain_ff,
            grad_gain_out.reshape(HEAD),
            jnp.zeros((shared * HEAD - gains.shape[0],), jnp.float32),
            grad_taps.reshape(-1),
        ]
    ).reshape(-1, HEAD)
    d_input, small_sum = join_rows_and_sum(d_input, small, shared, layers, 6)
    d_input, red_mixer = lax.optimization_barrier((d_input, red_mixer))


    red_mixer = red_mixer.astype(jnp.float32)
    red_qkv = jnp.stack(
        [red_mixer[:, item * inner : (item + 1) * inner] for item in range(3)], axis=1
    )
    red_beta = red_mixer[:, 3 * inner : 3 * inner + heads]
    red_out = red_out.astype(jnp.float32)
    red_conv = small_sum[shared:].reshape(conv_weight.shape)
    red_gains = small_sum[:shared].reshape(-1)[: gains.shape[0]]
    qkv_new = adamw(qkv_weight, qkv_first, qkv_second, red_qkv, RATE_WIDE, SHRINK)
    beta_new = adamw(beta_weight, beta_first, beta_second, red_beta, RATE_WIDE, SHRINK)
    out_new = adamw(out_weight, out_first, out_second, red_out, RATE_WIDE, SHRINK)
    conv_new = adamw(conv_weight, conv_first, conv_second, red_conv, RATE_CONV, 0.0)
    gains_new = adamw(gains, gains_first, gains_second, red_gains, RATE_GAIN, 0.0)
    return (
        moved(sorting, result),
        moved(sorting, d_input),
        *qkv_new,
        *beta_new,
        *out_new,
        *gate_up_new,
        *down_new,
        *conv_new,
        *gains_new,
    )


def solution(mesh):
    return jax.shard_map(
        per_device,
        mesh=mesh,
        in_specs=(
            P("seq", None),
            P("seq", None),
            P("seq"),
            P(),
            P("seq", None, "shard"),
            P("seq", None, "shard"),
            P("seq", None, "shard"),
            P("seq", "shard"),
            P("seq", "shard"),
            P("seq", "shard"),
            P("shard", "seq"),
            P("shard", "seq"),
            P("shard", "seq"),
            P("seq", None, "shard"),
            P("seq", None, "shard"),
            P("seq", None, "shard"),
            P("shard", "seq"),
            P("shard", "seq"),
            P("shard", "seq"),
            P(None, None, "shard"),
            P(None, None, "shard"),
            P(None, None, "shard"),
            P(),
            P(),
            P(),
        ),
        out_specs=(
            P("seq", None),
            P("seq", None),
            P("seq", None, "shard"),
            P("seq", None, "shard"),
            P("seq", None, "shard"),
            P("seq", "shard"),
            P("seq", "shard"),
            P("seq", "shard"),
            P("shard", "seq"),
            P("shard", "seq"),
            P("shard", "seq"),
            P("seq", None, "shard"),
            P("seq", None, "shard"),
            P("seq", None, "shard"),
            P("shard", "seq"),
            P("shard", "seq"),
            P("shard", "seq"),
            P(None, None, "shard"),
            P(None, None, "shard"),
            P(None, None, "shard"),
            P(),
            P(),
            P(),
        ),
        check_vma=False,
    )
```
